128 devices in a mesh: gx: 8 (over x, core), gy: 16 (over y, z).
Axes of the slice: x: 4, y: 4, z: 4, core: 2. Of those that a mesh axis runs over, the one named last changes fastest.
Arguments:
- fields: float32 [4, 4, 4096, 4096], P(None, None, 'gx', 'gy'), may hold values from -8 to 8
- ginv_x: float32 [4, 4096, 512], P(None, 'gx'), may hold values from 0 to 1.45
- ginv_y: float32 [4, 4096, 256], P(None, 'gy'), may hold values from 0 to 1.45
- coupling_x: float32 [4], replicated, may hold values from 0.49 to 0.505
- coupling_y: float32 [4], replicated, may hold values from 0.49 to 0.505
Outputs:
- advanced: float32 [4, 4, 4096, 4096], P(None, None, 'gx', 'gy')
The draws below stay inside these ranges and needn't reach their ends.
All inputs are finite; a program needn't handle non-finite values.
Results may differ from the reference program's by a relative error of at most 0.0003.
Values sent between devices are 32-bit elements; how exact they have to be, the bound alone decides.
No kernel may reach another device: no remote copies, remote signals or barrier semaphores. Data moves between devices by JAX's collectives and lax.ppermute only.
A program may use at most 192 MiB of HBM per device.

```python
import jax
import jax.numpy as jnp
from jax import lax

FIELDS = 4
PLANES = 4
CX = 512
CY = 256
NX = 4096
NY = 4096


def block_inverses(key, total, cells):
    first, second, third = jax.random.split(key, 3)
    far_corner = jax.random.uniform(first, (FIELDS, 1, 1, 1), jnp.float32, 0.9, 0.94)
    rates = -jnp.log(far_corner) / (cells - 1)
    places = jnp.arange(cells)
    edge = (places == 0) | (places == cells - 1)
    scales = jax.random.uniform(second, (FIELDS, total // cells, cells), jnp.float32, 0.85, 1.18)
    scales = jnp.where(edge[None, None, :], 1.0, scales)
    distance = jnp.abs(places[:, None] - places[None, :]).astype(jnp.float32)
    blocks = scales[:, :, :, None] * scales[:, :, None, :] * jnp.exp(-rates * distance)
    dense = jax.random.uniform(third, (FIELDS, total // cells, cells, cells), jnp.float32, -0.03, 0.03)
    corner = edge[:, None] & edge[None, :]
    dense = jnp.where(corner[None, None, :, :], 0.0, dense)
    blocks = blocks + dense
    return blocks.reshape(FIELDS, total, cells)


def draw_fields(key, part):
    key = jax.random.fold_in(key, 11)
    shape = (FIELDS, PLANES, NX, NY)
    values = jax.random.normal(key, shape, jnp.float32)
    return jnp.clip(values, -8.0, 8.0)


def draw_ginv_x(key, part):
    key = jax.random.fold_in(key, 12)
    return block_inverses(key, NX, CX)


def draw_ginv_y(key, part):
    key = jax.random.fold_in(key, 13)
    return block_inverses(key, NY, CY)


def setup_inputs(seed: int = 0) -> dict:
    seeds = jax.random.split(jax.random.key(seed), 6)
    fields = draw_fields(jax.random.fold_in(seeds[5], 71), 0)
    ginv_x = draw_ginv_x(jax.random.fold_in(seeds[5], 71), 0)
    ginv_y = draw_ginv_y(jax.random.fold_in(seeds[5], 71), 0)
    coupling_x = jnp.clip(jax.random.uniform(seeds[3], (FIELDS,), jnp.float32, 0.49, 0.505), 0.49, 0.505)
    coupling_y = jnp.clip(jax.random.uniform(seeds[4], (FIELDS,), jnp.float32, 0.49, 0.505), 0.49, 0.505)
    return dict(fields=fields, ginv_x=ginv_x, ginv_y=ginv_y, coupling_x=coupling_x, coupling_y=coupling_y)


COEFS = (0.75, -0.15, 1.0 / 60.0)
ADVECT = 0.3
BUOY = 0.5


def derive(padded, axis, count):
    total = jnp.zeros_like(lax.slice_in_dim(padded, 3, 3 + count, axis=axis))
    for offset, weight in zip((1, 2, 3), COEFS):
        upper = lax.slice_in_dim(padded, 3 + offset, 3 + offset + count, axis=axis)
        lower_part = lax.slice_in_dim(padded, 3 - offset, 3 - offset + count, axis=axis)
        total = total + weight * (upper - lower_part)
    return total


def settle_chain(r_first, r_last, coef_p, coef_s, coef_q, coef_t):
    def forward(carry, items):
        e_prev, c_prev = carry
        first_k, last_k, p_k, s_k, q_k, t_k = items
        denom = 1.0 - p_k * e_prev
        c_first = (first_k + p_k * c_prev) / denom
        c_last = q_k * e_prev * c_first + last_k + q_k * c_prev
        e_first = s_k / denom
        e_last = q_k * e_prev * e_first + t_k
        return (e_last, c_last), (e_first, e_last, c_first, c_last)

    start = (jnp.zeros_like(coef_p[0]), jnp.zeros_like(r_first[0]))
    ignored, stacks = lax.scan(forward, start, (r_first, r_last, coef_p, coef_s, coef_q, coef_t))

    def backward(a_next, items):
        e_first, e_last, c_first, c_last = items
        a_here = e_first * a_next + c_first
        b_here = e_last * a_next + c_last
        return a_here, (a_here, b_here)

    ignored, (first_vals, last_vals) = lax.scan(backward, jnp.zeros_like(r_first[0]), stacks, reverse=True)
    return first_vals, last_vals


def solve_lines(source, blocks, beta, cells):
    planes, length, width = source.shape
    count = length // cells
    source_blocks = source.reshape(planes, count, cells, width)
    inverse = blocks.reshape(count, cells, cells)
    solved = jnp.einsum('kij,zkjm->zkim', inverse, source_blocks, precision=lax.Precision.HIGHEST)
    r_first = jnp.transpose(solved[:, :, 0, :], (1, 0, 2))
    r_last = jnp.transpose(solved[:, :, -1, :], (1, 0, 2))
    shape = (count, 1, 1)
    first_vals, last_vals = settle_chain(r_first, r_last,
                                         (beta * inverse[:, 0, 0]).reshape(shape),
                                         (beta * inverse[:, 0, -1]).reshape(shape),
                                         (beta * inverse[:, -1, 0]).reshape(shape),
                                         (beta * inverse[:, -1, -1]).reshape(shape))
    zero = jnp.zeros_like(first_vals[:1])
    before = jnp.concatenate([zero, last_vals[:-1]])
    after = jnp.concatenate([first_vals[1:], zero])
    before = jnp.transpose(before, (1, 0, 2))[:, :, None, :]
    after = jnp.transpose(after, (1, 0, 2))[:, :, None, :]
    column_first = inverse[:, :, 0][None, :, :, None]
    column_last = inverse[:, :, -1][None, :, :, None]
    result = solved + beta * (before * column_first + after * column_last)
    return result.reshape(planes, length, width)


def reference(fields, ginv_x, ginv_y, coupling_x, coupling_y):
    results = []
    for index in range(4):
        field = fields[index]
        wide = jnp.pad(field, ((0, 0), (3, 3), (0, 0)))
        tall = jnp.pad(field, ((0, 0), (0, 0), (3, 3)))
        across = derive(wide, 1, field.shape[1])
        along = derive(tall, 2, field.shape[2])
        upward = 0.5 * (jnp.roll(field, -1, axis=0) - jnp.roll(field, 1, axis=0))
        forcing = field - ADVECT * (fields[1] * across + fields[2] * along + fields[3] * upward)
        if index == 3:
            forcing = forcing + BUOY * fields[0]
        section = solve_lines(forcing, ginv_x[index], coupling_x[index], CX)
        final = solve_lines(jnp.swapaxes(section, 1, 2), ginv_y[index], coupling_y[index], CY)
        results.append(jnp.swapaxes(final, 1, 2))
    return jnp.stack(results)
```

```python
import functools

import jax
import jax.numpy as jnp
from jax import lax
from jax.experimental import pallas as pl
from jax.experimental.pallas import tpu as pltpu
from jax.sharding import PartitionSpec as P

F32 = jnp.float32
BF16 = jnp.bfloat16
COEFS = (0.75, -0.15, 1.0 / 60.0)
BAND = (45.0, -9.0, 1.0)
ADVECT = 0.3
BUOY = 0.5
CX = 512
CY = 256
NF = 4
NZ = 4
ROWS = NF * NZ
MIB = 1024 * 1024

VM = pl.BlockSpec(memory_space=pltpu.VMEM)
SM = pl.BlockSpec(memory_space=pltpu.SMEM)
HB = pl.BlockSpec(memory_space=pl.ANY)


def shaped(*dims):
    return jax.ShapeDtypeStruct(dims, F32)


def halves(value):
    high = value.astype(BF16)
    return high, (value - high.astype(F32)).astype(BF16)


def dot(left, right):
    return lax.dot_general(left, right, (((1,), (0,)), ((), ())), preferred_element_type=F32)


def dot_nt(left, right):
    return lax.dot_general(left, right, (((1,), (1,)), ((), ())), preferred_element_type=F32)


def dot_tn(left, right):
    return lax.dot_general(left, right, (((0,), (0,)), ((), ())), preferred_element_type=F32)


def pack_kernel(fields, top, bottom, left, right, planes, lanes, turned, sems):
    for z in range(NZ):
        pltpu.make_async_copy(fields.at[:, z], planes.at[z], sems.at[z]).start()
    lanes[...] = jnp.zeros_like(lanes)
    step = 64
    for z in range(NZ):
        pltpu.make_async_copy(fields.at[:, z], planes.at[z], sems.at[z]).wait()

        def chunk(r, carry, z=z):
            at = pl.ds(pl.multiple_of(r * step, step), step)
            spot = lax.broadcasted_iota(jnp.int32, (step, 128), 1)
            total = lanes[at, :]
            for f in range(NF):
                k = 4 * (f * NZ + z)
                first = pltpu.roll(planes[z, f, at, 0:128], k, 1)
                last = pltpu.roll(planes[z, f, at, 128:256], (64 + k - 125) % 128, 1)
                total = jnp.where((spot >= k) & (spot < k + 3), first, total)
                total = jnp.where((spot >= 64 + k) & (spot < 64 + k + 3), last, total)
            lanes[at, :] = total
            return carry

        lax.fori_loop(0, CX // step, chunk, 0)
        for f in range(NF):
            k = f * NZ + z
            for c in range(3):
                top[c, k : k + 1, :] = planes[z, f, c : c + 1, :]
                bottom[c, k : k + 1, :] = planes[z, f, CX - 3 + c : CX - 2 + c, :]
    for t in range(CX // 128):
        part = slice(t * 128, (t + 1) * 128)
        turned[t] = jnp.transpose(lanes[part, :])
        for c in range(3):
            left[c, :, part] = turned[t, pl.ds(c, ROWS, stride=4), :]
            right[c, :, part] = turned[t, pl.ds(64 + c, ROWS, stride=4), :]


def pack(fields):
    return pl.pallas_call(
        pack_kernel,
        out_shape=(shaped(3, ROWS, CY), shaped(3, ROWS, CY), shaped(3, ROWS, CX), shaped(3, ROWS, CX)),
        in_specs=[HB],
        out_specs=(VM,) * 4,
        scratch_shapes=[
            pltpu.VMEM((NZ, NF, CX, CY), F32),
            pltpu.VMEM((CX, 128), F32),
            pltpu.VMEM((CX // 128, 128, 128), F32),
            pltpu.SemaphoreType.DMA((NZ,)),
        ],
        compiler_params=pltpu.CompilerParams(vmem_limit_bytes=20 * MIB),
        cost_estimate=pl.CostEstimate(flops=4_000_000, bytes_accessed=9 * MIB, transcendentals=0),
        name="pack_edges",
    )(fields)


WINDOW = 256
CHUNK = 64


def band(shape, offset, along):
    gap = lax.broadcasted_iota(jnp.int32, shape, along) - lax.broadcasted_iota(jnp.int32, shape, 1 - along)
    gap = gap - offset
    total = jnp.zeros(shape, F32)
    for reach, weight in zip((1, 2, 3), BAND):
        total = jnp.where(gap == reach, weight, total)
        total = jnp.where(gap == -reach, -weight, total)
    return total.astype(BF16)


STRIPS = ((0, 176, 0), (176, 160, 128), (336, 176, 256))


def big_kernel(
    fields, ginv_x, ginv_y, out, r_first, r_last, r_cols, edge_x, edge_y,
    planes, gx, gy, gx_cat, gy_cat, band_y, band_x, q_cat, dx, f_cat, res, cols, sems, out_sems,
):
    copy_gx = pltpu.make_async_copy(ginv_x, gx, sems.at[4])
    copy_gy = pltpu.make_async_copy(ginv_y, gy, sems.at[5])
    loads = [pltpu.make_async_copy(fields.at[:, z], planes.at[z], sems.at[z]) for z in range(NZ)]
    copy_gy.start()
    copy_gx.start()
    for z in (3, 0, 1, 2):
        loads[z].start()
    both = band((CY, CY), 0, 0)
    band_y[0:CY, :] = both
    band_y[CY:, :] = both
    for start, count, base in STRIPS:
        band_x[start : start + count, :] = band((count, WINDOW), start - base, 1)
    copy_gy.wait()
    for f in range(NF):
        turned = jnp.transpose(gy[f])
        high, low = halves(turned)
        gy_cat[f, 0:CY, :] = high
        gy_cat[f, CY : 2 * CY, :] = low
        gy_cat[f, 2 * CY :, :] = high
        edge_y[f, 0:3, :] = turned[0:3]
        edge_y[f, 3:6, :] = turned[CY - 3 : CY]
        edge_y[f, 6:7, :] = gy[f, 0:1, :]
        edge_y[f, 7:8, :] = gy[f, CY - 1 : CY, :]
    copy_gx.wait()
    for f in range(NF):

        def split(r, carry, f=f):
            at = pl.ds(pl.multiple_of(r * CHUNK, CHUNK), CHUNK)
            high, low = halves(gx[f, at, :])
            gx_cat[f, at, 0:CX] = high
            gx_cat[f, at, CX : 2 * CX] = high
            gx_cat[f, at, 2 * CX :] = low
            return carry

        lax.fori_loop(0, CX // CHUNK, split, 0)
        edge_x[f, 0:3, :] = jnp.transpose(gx[f, :, 0:128])[0:3]
        edge_x[f, 3:6, :] = jnp.transpose(gx[f, :, CX - 128 : CX])[125:128]
        edge_x[f, 6:7, :] = gx[f, 0:1, :]
        edge_x[f, 7:8, :] = gx[f, CX - 1 : CX, :]
    cols[...] = jnp.zeros_like(cols)

    def plane(z, carry):
        above = lax.rem(z + 1, NZ)
        below = lax.rem(z + NZ - 1, NZ)
        for f in range(NF):

            def cut(r, c, f=f):
                at = pl.ds(pl.multiple_of(r * CHUNK, CHUNK), CHUNK)
                high, low = halves(planes[z, f, at, :])
                q_cat[at, 0:CY] = high
                q_cat[at, CY:] = low
                return c

            lax.fori_loop(0, CX // CHUNK, cut, 0, unroll=True)
            for start, count, base in STRIPS:
                mine = band_x[start : start + count, :]
                dx[start : start + count, :] = dot(mine, q_cat[base : base + WINDOW, 0:CY]) + dot(
                    mine, q_cat[base : base + WINDOW, CY:]
                )

            def force(r, c, f=f):
                at = pl.ds(pl.multiple_of(r * CHUNK, CHUNK), CHUNK)
                dy = dot(q_cat[at, :], band_y[...])
                q = planes[z, f, at, :]
                rise = planes[above, f, at, :] - planes[below, f, at, :]
                value = q - (
                    (ADVECT / 60.0) * (planes[z, 1, at, :] * dx[at, :] + planes[z, 2, at, :] * dy)
                    + (0.5 * ADVECT) * (planes[z, 3, at, :] * rise)
                )
                if f == 3:
                    value = value + BUOY * planes[z, 0, at, :]
                high, low = halves(value)
                f_cat[pl.ds(pl.multiple_of(r * CHUNK, CHUNK), CHUNK), :] = high
                f_cat[pl.ds(pl.multiple_of(CX + r * CHUNK, CHUNK), CHUNK), :] = low
                f_cat[pl.ds(pl.multiple_of(2 * CX + r * CHUNK, CHUNK), CHUNK), :] = high
                return c

            lax.fori_loop(0, CX // CHUNK, force, 0, unroll=True)
            k = f * NZ + z
            wide = 256
            for r in range(CX // wide):
                section = dot(gx_cat[f, r * wide : (r + 1) * wide, :], f_cat[...])
                if r == 0:
                    r_first[pl.ds(k, 1), :] = section[0:1]
                if r == CX // wide - 1:
                    r_last[pl.ds(k, 1), :] = section[wide - 1 : wide]
                high, low = halves(section)
                value = dot(jnp.concatenate([high, high, low], axis=1), gy_cat[f])
                res[k, r * wide : (r + 1) * wide, :] = value
                spot = lax.broadcasted_iota(jnp.int32, (wide, 128), 1)
                total = cols[r * wide : (r + 1) * wide, :]
                total = jnp.where(spot == k, pltpu.roll(value[:, 0:128], k, 1), total)
                total = jnp.where(spot == ROWS + k, pltpu.roll(value[:, 128:256], k + ROWS + 1, 1), total)
                cols[r * wide : (r + 1) * wide, :] = total
            pltpu.make_async_copy(res.at[k], out.at[f, z], out_sems.at[k]).start()
        return carry

    for z in (3, 0, 1, 2):
        loads[z].wait()
    lax.fori_loop(0, NZ, plane, 0)
    r_cols[...] = jnp.transpose(cols[...])[0 : 2 * ROWS, :]
    for k in range(ROWS):
        pltpu.make_async_copy(res.at[k], out.at[k // NZ, k % NZ], out_sems.at[k]).wait()


def big(fields, ginv_x, ginv_y):
    return pl.pallas_call(
        big_kernel,
        out_shape=(
            shaped(NF, NZ, CX, CY),
            shaped(ROWS, CY),
            shaped(ROWS, CY),
            shaped(2 * ROWS, CX),
            shaped(NF, 8, CX),
            shaped(NF, 8, CY),
        ),
        in_specs=[HB, HB, HB],
        out_specs=(HB, VM, VM, VM, VM, VM),
        scratch_shapes=[
            pltpu.VMEM((NZ, NF, CX, CY), F32),
            pltpu.VMEM((NF, CX, CX), F32),
            pltpu.VMEM((NF, CY, CY), F32),
            pltpu.VMEM((NF, CX, 3 * CX), BF16),
            pltpu.VMEM((NF, 3 * CY, CY), BF16),
            pltpu.VMEM((2 * CY, CY), BF16),
            pltpu.VMEM((CX, WINDOW), BF16),
            pltpu.VMEM((CX, 2 * CY), BF16),
            pltpu.VMEM((CX, CY), F32),
            pltpu.VMEM((3 * CX, CY), BF16),
            pltpu.VMEM((ROWS, CX, CY), F32),
            pltpu.VMEM((CX, 128), F32),
            pltpu.SemaphoreType.DMA((6,)),
            pltpu.SemaphoreType.DMA((ROWS,)),
        ],
        compiler_params=pltpu.CompilerParams(vmem_limit_bytes=52 * MIB),
        cost_estimate=pl.CostEstimate(flops=6_000_000_000, bytes_accessed=21 * MIB, transcendentals=0),
        name="forcing_and_products",
    )(fields, ginv_x, ginv_y)


def fill_coefs(beta, first_first, first_last, last_first, last_last):
    spot = lax.broadcasted_iota(jnp.int32, (NZ, 128), 1)
    values = jnp.where(
        spot == 0,
        first_first,
        jnp.where(spot == 1, first_last, jnp.where(spot == 2, last_first, jnp.where(spot == 3, last_last, 0.0))),
    )
    return beta * values


def halo_kernel(
    top, bottom, left, right, top_in, bottom_in, left_in, right_in, r_first, r_last, edge_x, beta_x,
    d_rows, d_cols, message,
):
    spot = lax.broadcasted_iota(jnp.int32, (NZ, CY), 1)
    for f in range(NF):
        s = slice(f * NZ, (f + 1) * NZ)
        for j in range(3):
            for own, halo, speed, ref, rising in (
                (top, top_in, 1, d_rows, False),
                (bottom, bottom_in, 1, d_rows, True),
                (left, left_in, 2, d_cols, False),
                (right, right_in, 2, d_cols, True),
            ):
                total = None
                for o in (1, 2, 3):
                    c = j + o - 3 if rising else 3 + j - o
                    if 0 <= c < 3:
                        term = COEFS[o - 1] * halo[c, s, :]
                        total = term if total is None else total + term
                sign = -ADVECT if rising else ADVECT
                ref[j + (3 if rising else 0), s, :] = sign * (own[j, speed * NZ : (speed + 1) * NZ, :] * total)
        sums = []
        for e, source in ((0, r_first), (1, r_last)):
            total = source[s, :]
            at = 0 if e == 0 else CX - 1
            for i in range(6):
                total = total + edge_x[f, i : i + 1, at : at + 1] * d_rows[i, s, :]
            for i in range(6):
                add = jnp.sum(d_cols[i, s, :] * edge_x[f, 6 + e : 7 + e, :], axis=1, keepdims=True)
                total = total + jnp.where(spot == (i if i < 3 else CY - 6 + i), add, 0.0)
            message[s, e * CY : (e + 1) * CY] = total
        message[s, 2 * CY :] = fill_coefs(
            beta_x[f],
            edge_x[f, 0:1, 0:1],
            edge_x[f, 5:6, 0:1],
            edge_x[f, 0:1, CX - 1 : CX],
            edge_x[f, 5:6, CX - 1 : CX],
        )


def halo(own, received, r_first, r_last, edge_x, beta_x):
    return pl.pallas_call(
        halo_kernel,
        out_shape=(shaped(6, ROWS, CY), shaped(6, ROWS, CX), shaped(ROWS, 2 * CY + 128)),
        in_specs=[VM] * 11 + [SM],
        out_specs=(VM,) * 3,
        cost_estimate=pl.CostEstimate(flops=2_000_000, bytes_accessed=1 * MIB, transcendentals=0),
        name="halo_terms",
    )(*own, *received, r_first, r_last, edge_x, beta_x)


def merge(side, mine, other, state, width):
    is_right = jnp.broadcast_to(side, (ROWS, 1)) == 1

    def parts(ref):
        c = 2 * width
        return [
            ref[:, 0:width], ref[:, width:c],
            ref[:, c : c + 1], ref[:, c + 1 : c + 2], ref[:, c + 2 : c + 3], ref[:, c + 3 : c + 4],
        ]

    own, far = parts(mine), parts(other)
    l_first, l_last, l_p, l_s, l_q, l_t = [jnp.where(is_right, b, a) for a, b in zip(own, far)]
    r_first, r_last, r_p, r_s, r_q, r_t = [jnp.where(is_right, a, b) for a, b in zip(own, far)]
    inner = 1.0 / (1.0 - l_t * r_p)
    m_b = (l_last + l_t * r_first) * inner
    m_a = (r_first + r_p * l_last) * inner
    b_from_b, b_from_a = l_q * inner, l_t * r_s * inner
    a_from_b, a_from_a = r_p * l_q * inner, r_s * inner
    group = (
        l_first + l_s * m_a,
        r_last + r_q * m_b,
        l_p + l_s * a_from_b,
        l_s * a_from_a,
        r_q * b_from_b,
        r_t + r_q * b_from_a,
    )
    prior, later, prior_b, prior_a, later_b, later_a = parts(state)
    fresh = []
    for base, by_b, by_a in ((prior, prior_b, prior_a), (later, later_b, later_a)):
        fresh.append(
            (
                base + jnp.where(is_right, by_b * m_b, by_a * m_a),
                jnp.where(is_right, by_b * b_from_b, by_b + by_a * a_from_b),
                jnp.where(is_right, by_a + by_b * b_from_a, by_a * a_from_a),
            )
        )
    return group, fresh


def lanes_of(values):
    spot = lax.broadcasted_iota(jnp.int32, (ROWS, 128), 1)
    total = jnp.zeros((ROWS, 128), F32)
    for place, value in enumerate(values):
        total = jnp.where(spot == place, value, total)
    return total


def merge_kernel(width, side, mine, other, state, group_out, state_out):
    group, fresh = merge(side[0], mine, other, state, width)
    group_out[:, 0:width] = group[0]
    group_out[:, width : 2 * width] = group[1]
    group_out[:, 2 * width :] = lanes_of(group[2:])
    state_out[:, 0:width] = fresh[0][0]
    state_out[:, width : 2 * width] = fresh[1][0]
    state_out[:, 2 * width :] = lanes_of((fresh[0][1], fresh[0][2], fresh[1][1], fresh[1][2]))


def merge_step(side, mine, other, state, width):
    return pl.pallas_call(
        functools.partial(merge_kernel, width),
        out_shape=(shaped(ROWS, 2 * width + 128),) * 2,
        in_specs=[SM, VM, VM, VM],
        out_specs=(VM, VM),
        cost_estimate=pl.CostEstimate(flops=200_000, bytes_accessed=200_000, transcendentals=0),
        name="merge_groups",
    )(side, mine, other, state)


def fresh_state(width):
    spot = lax.broadcasted_iota(jnp.int32, (ROWS, 2 * width + 128), 1)
    return jnp.where((spot == 2 * width) | (spot == 2 * width + 3), 1.0, 0.0).astype(F32)


def exchange(message, axis, width):
    count = lax.axis_size(axis)
    place = lax.axis_index(axis)
    state = fresh_state(width)
    reach = 1
    while True:
        other = lax.ppermute(message, axis, [(i, i ^ reach) for i in range(count)])
        side = lax.rem(place // reach, 2).astype(jnp.int32).reshape(1)
        if 2 * reach >= count:
            return side, message, other, state
        message, state = merge_step(side, message, other, state, width)
        reach *= 2


def columns_kernel(d_rows, d_cols, ginv_x, r_cols, edge_x, edge_y, m_cols, y_rhs):
    high, low = halves(d_cols[...].reshape(6 * ROWS, CX))
    owner = lax.rem(lax.broadcasted_iota(jnp.int32, (6 * ROWS, 1), 0), ROWS) // NZ
    total = jnp.zeros((6 * ROWS, CX), F32)
    for f in range(NF):
        g_high, g_low = halves(ginv_x[f])
        value = dot_nt(high, g_high) + dot_nt(low, g_high) + dot_nt(high, g_low)
        total = jnp.where(owner == f, value, total)
    m_cols[...] = total.reshape(6, ROWS, CX)
    for f in range(NF):
        s = slice(f * NZ, (f + 1) * NZ)
        for e in range(2):
            value = r_cols[e * ROWS + f * NZ : e * ROWS + (f + 1) * NZ, :]
            for i in range(6):
                scale = jnp.sum(d_rows[i, s, :] * edge_y[f, 6 + e : 7 + e, :], axis=1, keepdims=True)
                value = value + scale * edge_x[f, i : i + 1, :]
                at = i if i < 3 else CY - 6 + i
                value = value + m_cols[i, s, :] * edge_y[f, 6 + e : 7 + e, at : at + 1]
            y_rhs[e, s, :] = value


def columns(d_rows, d_cols, ginv_x, r_cols, edge_x, edge_y):
    return pl.pallas_call(
        columns_kernel,
        out_shape=(shaped(6, ROWS, CX), shaped(2, ROWS, CX)),
        in_specs=[VM] * 6,
        out_specs=(VM, VM),
        compiler_params=pltpu.CompilerParams(vmem_limit_bytes=24 * MIB),
        cost_estimate=pl.CostEstimate(flops=1_200_000_000, bytes_accessed=5 * MIB, transcendentals=0),
        name="halo_columns",
    )(d_rows, d_cols, ginv_x, r_cols, edge_x, edge_y)


def middle_kernel(side, mine, other, state, d_rows, y_rhs, edge_x, edge_y, beta_x, beta_y, rows_out, message):
    group, fresh = merge(side[0], mine, other, state, CY)
    rows_out[...] = d_rows[...]
    for f in range(NF):
        s = slice(f * NZ, (f + 1) * NZ)
        enter = [beta_x[f] * fresh[e][0][s, :] for e in range(2)]
        rows_out[0, s, :] = d_rows[0, s, :] + enter[0]
        rows_out[5, s, :] = d_rows[5, s, :] + enter[1]
        for e in range(2):
            value = y_rhs[e, s, :]
            for g in range(2):
                scale = jnp.sum(enter[g] * edge_y[f, 6 + e : 7 + e, :], axis=1, keepdims=True)
                value = value + scale * edge_x[f, 5 * g : 5 * g + 1, :]
            message[s, e * CX : (e + 1) * CX] = value
        message[s, 2 * CX :] = fill_coefs(
            beta_y[f],
            edge_y[f, 0:1, 0:1],
            edge_y[f, 5:6, 0:1],
            edge_y[f, 0:1, CY - 1 : CY],
            edge_y[f, 5:6, CY - 1 : CY],
        )


def middle(last, d_rows, y_rhs, edge_x, edge_y, beta_x, beta_y):
    return pl.pallas_call(
        middle_kernel,
        out_shape=(shaped(6, ROWS, CY), shaped(ROWS, 2 * CX + 128)),
        in_specs=[SM] + [VM] * 7 + [SM, SM],
        out_specs=(VM, VM),
        cost_estimate=pl.CostEstimate(flops=500_000, bytes_accessed=500_000, transcendentals=0),
        name="between_interfaces",
    )(*last, d_rows, y_rhs, edge_x, edge_y, beta_x, beta_y)


def rows_kernel(rows, ginv_y, out):
    high, low = halves(rows[...].reshape(6 * ROWS, CY))
    owner = lax.rem(lax.broadcasted_iota(jnp.int32, (6 * ROWS, 1), 0), ROWS) // NZ
    total = jnp.zeros((6 * ROWS, CY), F32)
    for f in range(NF):
        g_high, g_low = halves(ginv_y[f])
        value = dot_nt(high, g_high) + dot_nt(low, g_high) + dot_nt(high, g_low)
        total = jnp.where(owner == f, value, total)
    out[...] = total.reshape(6, ROWS, CY)


def row_products(rows, ginv_y):
    return pl.pallas_call(
        rows_kernel,
        out_shape=shaped(6, ROWS, CY),
        in_specs=[VM, VM],
        out_specs=VM,
        cost_estimate=pl.CostEstimate(flops=300_000_000, bytes_accessed=2 * MIB, transcendentals=0),
        name="row_products",
    )(rows, ginv_y)


def last_kernel(side, mine, other, state, m_cols, beta_y, out):
    group, fresh = merge(side[0], mine, other, state, CX)
    out[...] = m_cols[...]
    for f in range(NF):
        s = slice(f * NZ, (f + 1) * NZ)
        out[0, s, :] = m_cols[0, s, :] + beta_y[f] * fresh[0][0][s, :]
        out[5, s, :] = m_cols[5, s, :] + beta_y[f] * fresh[1][0][s, :]


def last_merge(last, m_cols, beta_y):
    return pl.pallas_call(
        last_kernel,
        out_shape=shaped(6, ROWS, CX),
        in_specs=[SM] + [VM] * 4 + [SM],
        out_specs=VM,
        cost_estimate=pl.CostEstimate(flops=500_000, bytes_accessed=800_000, transcendentals=0),
        name="last_merge",
    )(*last, m_cols, beta_y)


def update_kernel(base, cols, rows, edge_x, edge_y, out, tall, wide):
    k = pl.program_id(0)
    f = k // NZ
    tall[...] = jnp.zeros_like(tall)
    wide[...] = jnp.zeros_like(wide)
    tall[0:6, :] = edge_x[f, 0:6, :]
    wide[8:14, :] = edge_y[f, 0:6, :]
    for i in range(6):
        tall[8 + i : 9 + i, :] = cols[i, pl.ds(k, 1), :]
        wide[i : i + 1, :] = rows[i, pl.ds(k, 1), :]
    a_high, a_low = halves(tall[...])
    b_high, b_low = halves(wide[...])
    change = dot_tn(
        jnp.concatenate([a_high, a_low, a_high], axis=0), jnp.concatenate([b_high, b_high, b_low], axis=0)
    )
    out[0, 0] = base[0, 0] + change


def update(base, cols, rows, edge_x, edge_y):
    block = pl.BlockSpec((1, 1, CX, CY), lambda k: (k // NZ, k % NZ, 0, 0))
    return pl.pallas_call(
        update_kernel,
        out_shape=shaped(NF, NZ, CX, CY),
        grid=(ROWS,),
        in_specs=[block, VM, VM, VM, VM],
        out_specs=block,
        scratch_shapes=[pltpu.VMEM((16, CX), F32), pltpu.VMEM((16, CY), F32)],
        cost_estimate=pl.CostEstimate(flops=200_000_000, bytes_accessed=17 * MIB, transcendentals=0),
        name="update_result",
    )(base, cols, rows, edge_x, edge_y)


def neighbours(axis):
    count = lax.axis_size(axis)
    return [(i, i + 1) for i in range(count - 1)], [(i + 1, i) for i in range(count - 1)]


def local(fields, ginv_x, ginv_y, coupling_x, coupling_y):
    own = pack(fields)
    top, bottom, left, right = own
    up_x, down_x = neighbours("gx")
    up_y, down_y = neighbours("gy")
    received = (
        lax.ppermute(bottom, "gx", up_x),
        lax.ppermute(top, "gx", down_x),
        lax.ppermute(right, "gy", up_y),
        lax.ppermute(left, "gy", down_y),
    )
    base, r_first, r_last, r_cols, edge_x, edge_y = big(fields, ginv_x, ginv_y)
    d_rows, d_cols, message = halo(own, received, r_first, r_last, edge_x, coupling_x)
    m_cols, y_rhs = columns(d_rows, d_cols, ginv_x, r_cols, edge_x, edge_y)
    last_x = exchange(message, "gx", CY)
    rows, message_y = middle(last_x, d_rows, y_rhs, edge_x, edge_y, coupling_x, coupling_y)
    rows = row_products(rows, ginv_y)
    last_y = exchange(message_y, "gy", CX)
    cols = last_merge(last_y, m_cols, coupling_y)
    return update(base, cols, rows, edge_x, edge_y)


def solution(mesh):
    in_specs = (P(None, None, "gx", "gy"), P(None, "gx", None), P(None, "gy", None), P(), P())
    out_specs = P(None, None, "gx", "gy")
    return jax.shard_map(local, mesh=mesh, in_specs=in_specs, out_specs=out_specs, check_vma=False)
```

```python
import functools

import jax
import jax.numpy as jnp
from jax import lax
from jax.experimental import pallas as pl
from jax.experimental.pallas import tpu as pltpu
from jax.sharding import PartitionSpec as P

F32 = jnp.float32
BF16 = jnp.bfloat16
BAND = (45.0, -9.0, 1.0)
ADVECT = 0.3
BUOY = 0.5
CX = 512
CY = 256
NF = 4
NZ = 4
ROWS = NF * NZ
MIB = 1024 * 1024

VM = pl.BlockSpec(memory_space=pltpu.VMEM)
SM = pl.BlockSpec(memory_space=pltpu.SMEM)
HB = pl.BlockSpec(memory_space=pltpu.HBM)
SMALL = pltpu.CompilerParams(vmem_limit_bytes=4 * MIB)


def shaped(*dims):
    return jax.ShapeDtypeStruct(dims, F32)


def halves(value):
    high = value.astype(BF16)
    return high, (value - high.astype(F32)).astype(BF16)


def dot(left, right):
    return lax.dot_general(left, right, (((1,), (0,)), ((), ())), preferred_element_type=F32)


def dot_nt(left, right):
    return lax.dot_general(left, right, (((1,), (1,)), ((), ())), preferred_element_type=F32)


def dot_tn(left, right):
    return lax.dot_general(left, right, (((0,), (0,)), ((), ())), preferred_element_type=F32)


def pack_kernel(odd, fields, planes, x_inner, x_outer, y_inner, y_outer, lanes, turned, sems):
    for f in range(NF):
        pltpu.make_async_copy(fields.at[f], planes.at[f], sems.at[f]).start()
    step = 64
    for f in range(NF):
        pltpu.make_async_copy(fields.at[f], planes.at[f], sems.at[f]).wait()

        def chunk(r, carry, f=f):
            at = pl.ds(pl.multiple_of(r * step, step), step)
            spot = lax.broadcasted_iota(jnp.int32, (step, 128), 1)
            total = jnp.zeros((step, 128), F32) if f == 0 else lanes[at, :]
            for z in range(NZ):
                ends = jnp.where(spot >= 125, planes[f, z, at, 128:256], 0.0)
                ends = jnp.where(spot < 3, planes[f, z, at, 0:128], ends)
                total = total + pltpu.roll(ends, 8 * (f * NZ + z) + 3, 1)
            lanes[at, :] = total
            return carry

        lax.fori_loop(0, CX // step, chunk, 0)
        for z in range(NZ):
            k = f * NZ + z
            for c in range(3):
                top = planes[f, z, c : c + 1, :]
                bottom = planes[f, z, CX - 3 + c : CX - 2 + c, :]
                x_inner[c, k : k + 1, :] = jnp.where(odd[0] == 1, top, bottom)
                x_outer[c, k : k + 1, :] = jnp.where(odd[0] == 1, bottom, top)
    for t in range(CX // 128):
        part = slice(t * 128, (t + 1) * 128)
        turned[t] = jnp.transpose(lanes[part, :])
        for c in range(3):
            right = turned[t, pl.ds(c, ROWS, stride=8), :]
            left = turned[t, pl.ds(3 + c, ROWS, stride=8), :]
            y_inner[c, :, part] = jnp.where(odd[1] == 1, left, right)
            y_outer[c, :, part] = jnp.where(odd[1] == 1, right, left)


def pack(odd, fields):
    return pl.pallas_call(
        pack_kernel,
        out_shape=(
            shaped(NF, NZ, CX, CY),
            shaped(3, ROWS, CY),
            shaped(3, ROWS, CY),
            shaped(3, ROWS, CX),
            shaped(3, ROWS, CX),
        ),
        in_specs=[SM, HB],
        out_specs=(VM,) * 5,
        scratch_shapes=[
            pltpu.VMEM((CX, 128), F32),
            pltpu.VMEM((CX // 128, 128, 128), F32),
            pltpu.SemaphoreType.DMA((NF,)),
        ],
        compiler_params=pltpu.CompilerParams(vmem_limit_bytes=44 * MIB),
        cost_estimate=pl.CostEstimate(flops=4_000_000, bytes_accessed=9 * MIB, transcendentals=0),
        name="pack_edges",
    )(odd, fields)


WINDOW = 256
CHUNK = 128
STRIPS = CX // CHUNK
BASES = (0, 64, 192, 256)


def band(shape, offset, along):
    gap = lax.broadcasted_iota(jnp.int32, shape, along) - lax.broadcasted_iota(jnp.int32, shape, 1 - along)
    gap = gap - offset
    total = jnp.zeros(shape, F32)
    for reach, weight in zip((1, 2, 3), BAND):
        total = jnp.where(gap == reach, weight, total)
        total = jnp.where(gap == -reach, -weight, total)
    return total.astype(BF16)


def halo_sums(before, after):
    sums = []
    for j in range(3):
        sums.append(sum(-BAND[o - 1] * before[3 + j - o] for o in range(j + 1, 4)))
    for j in range(3):
        sums.append(sum(BAND[o - 1] * after[j + o - 3] for o in range(3 - j, 4)))
    return sums


def fill_coefs(beta, first_first, first_last, last_first, last_last):
    spot = lax.broadcasted_iota(jnp.int32, (NZ, 128), 1)
    values = jnp.where(
        spot == 0,
        first_first,
        jnp.where(spot == 1, first_last, jnp.where(spot == 2, last_first, jnp.where(spot == 3, last_last, 0.0))),
    )
    return beta * values


def big_kernel(
    odd, fields, gx, gy, x_inner, x_outer, y_inner, y_outer, beta_x,
    out, message, y_rhs, edge_x, edge_y,
    gx_cat, gy_cat, band_y, band_x, q_0, q_1, f_0, f_1, s_0, s_1, cols, halo_rows, halo_cols, turned,
):
    both = band((CY, CY), 0, 0)
    band_y[0:CY, :] = both
    band_y[CY:, :] = both
    for r in range(STRIPS):
        band_x[r] = band((CHUNK, WINDOW), r * CHUNK - BASES[r], 1)
    halo_rows[...] = jnp.zeros_like(halo_rows)
    turned[...] = jnp.zeros_like(turned)
    x_odd, y_odd = odd[0] == 1, odd[1] == 1
    above = [jnp.where(x_odd, x_inner[c], x_outer[c]) for c in range(3)]
    below = [jnp.where(x_odd, x_outer[c], x_inner[c]) for c in range(3)]
    for j, value in enumerate(halo_sums(above, below)):
        for k in range(ROWS):
            if j < 3:
                halo_rows[k, j : j + 1, :] = value[k : k + 1, :]
            else:
                halo_rows[k, j + 10 : j + 11, :] = value[k : k + 1, :]
    before = [jnp.where(y_odd, y_inner[c], y_outer[c]) for c in range(3)]
    behind = [jnp.where(y_odd, y_outer[c], y_inner[c]) for c in range(3)]
    for j, value in enumerate(halo_sums(before, behind)):
        for t in range(STRIPS):
            turned[t, pl.ds(j if j < 3 else j + 2, ROWS, stride=8), :] = value[:, t * 128 : (t + 1) * 128]
    for t in range(STRIPS):
        halo_cols[t * 128 : (t + 1) * 128, :] = jnp.transpose(turned[t])
    cols[...] = jnp.zeros_like(cols)
    for f in range(NF):
        turned_g = jnp.transpose(gy[f])
        high, low = halves(turned_g)
        gy_cat[f, 0:CY, :] = high
        gy_cat[f, CY : 2 * CY, :] = high
        gy_cat[f, 2 * CY :, :] = low
        edge_y[f, 0:1, :] = turned_g[0:1]
        edge_y[f, 1:2, :] = turned_g[CY - 1 : CY]
        edge_y[f, 2:3, :] = gy[f, 0:1, :]
        edge_y[f, 3:4, :] = gy[f, CY - 1 : CY, :]
    for f in range(NF):

        def split(r, carry, f=f):
            at = pl.ds(pl.multiple_of(r * CHUNK, CHUNK), CHUNK)
            high, low = halves(gx[f, at, :])
            gx_cat[f, at, 0:CX] = high
            gx_cat[f, at, CX:] = low
            return carry

        lax.fori_loop(0, CX // CHUNK, split, 0)
        edge_x[f, 0:1, :] = jnp.transpose(gx[f, :, 0:128])[0:1]
        edge_x[f, 1:2, :] = jnp.transpose(gx[f, :, CX - 128 : CX])[127:128]
        s = slice(f * NZ, (f + 1) * NZ)
        message[s, 2 * CY :] = fill_coefs(
            beta_x[f],
            gx[f, 0:1, 0:1],
            gx[f, 0:1, CX - 1 : CX],
            gx[f, CX - 1 : CX, 0:1],
            gx[f, CX - 1 : CX, CX - 1 : CX],
        )

    def cut(z, f, q_cat):
        for r in range(STRIPS):
            at = slice(r * CHUNK, (r + 1) * CHUNK)
            high, low = halves(fields[f, z, at, :])
            q_cat[at, 0:CY] = high
            q_cat[at, CY:] = low

    def force(z, f, r, q_cat, f_cat):
        at = slice(r * CHUNK, (r + 1) * CHUNK)
        k = f * NZ + z
        window = slice(BASES[r], BASES[r] + WINDOW)
        dx = dot(band_x[r], q_cat[window, 0:CY]) + dot(band_x[r], q_cat[window, CY:])
        dy = dot(q_cat[at, :], band_y[...])
        if r == 0:
            dx = jnp.concatenate([dx[0:8] + halo_rows[k, 0:8], dx[8:]], axis=0)
        if r == STRIPS - 1:
            dx = jnp.concatenate([dx[: CHUNK - 8], dx[CHUNK - 8 :] + halo_rows[k, 8:16]], axis=0)
        spot = lax.broadcasted_iota(jnp.int32, (CHUNK, 128), 1)
        side = halo_cols[at, :]
        left = jnp.where(spot < 3, pltpu.roll(side, lax.rem(128 - 8 * k, 128), 1), 0.0)
        right = jnp.where(spot >= 125, pltpu.roll(side, lax.rem(248 - 8 * k, 128), 1), 0.0)
        dy = dy + jnp.concatenate([left, right], axis=1)
        q = fields[f, z, at, :]
        rise = fields[f, lax.rem(z + 1, NZ), at, :] - fields[f, lax.rem(z + NZ - 1, NZ), at, :]
        value = q - (
            (ADVECT / 60.0) * (fields[1, z, at, :] * dx + fields[2, z, at, :] * dy)
            + (0.5 * ADVECT) * (fields[3, z, at, :] * rise)
        )
        if f == 3:
            value = value + BUOY * fields[0, z, at, :]
        high, low = halves(value)
        f_cat[at, :] = high
        f_cat[CX + r * CHUNK : CX + (r + 1) * CHUNK, :] = low

    def solve_x(z, f, r, f_cat, s_cat):
        at = slice(r * CHUNK, (r + 1) * CHUNK)
        k = f * NZ + z
        section = dot(gx_cat[f, at, 0:CX], f_cat[0:CX, :]) + dot(gx_cat[f, at, 0:CX], f_cat[CX:, :])
        section = section + dot(gx_cat[f, at, CX:], f_cat[0:CX, :])
        if r == 0:
            message[pl.ds(k, 1), 0:CY] = section[0:1]
        if r == STRIPS - 1:
            message[pl.ds(k, 1), CY : 2 * CY] = section[CHUNK - 1 : CHUNK]
        high, low = halves(section)
        s_cat[at, 0:CY] = high
        s_cat[at, CY:] = low

    def solve_y(z, f, r, s_cat):
        at = slice(r * CHUNK, (r + 1) * CHUNK)
        k = f * NZ + z
        value = dot(s_cat[at, :], gy_cat[f, 0 : 2 * CY, :]) + dot(s_cat[at, 0:CY], gy_cat[f, 2 * CY :, :])
        out[f, z, at, :] = value
        spot = lax.broadcasted_iota(jnp.int32, (CHUNK, 128), 1)
        total = cols[at, :]
        total = jnp.where(spot == k, pltpu.roll(value[:, 0:128], k, 1), total)
        total = jnp.where(spot == ROWS + k, pltpu.roll(value[:, 128:256], k + ROWS + 1, 1), total)
        cols[at, :] = total

    q_bufs, f_bufs, s_bufs = (q_0, q_1), (f_0, f_1), (s_0, s_1)

    def plane(z, last):
        for f in range(NF):
            ahead = [(z, f + d) if f + d < NF else (z + 1, f + d - NF) for d in (1, 2)]
            (z_x, f_x), (z_f, f_f) = ahead
            do_x = not (last and f + 1 >= NF)
            do_f = not (last and f + 2 >= NF)
            if do_f:
                cut(z_f, f_f, q_bufs[f_f % 2])
            for r in range(STRIPS):
                if do_f:
                    force(z_f, f_f, r, q_bufs[f_f % 2], f_bufs[f_f % 2])
                if do_x:
                    solve_x(z_x, f_x, r, f_bufs[f_x % 2], s_bufs[f_x % 2])
                solve_y(z, f, r, s_bufs[f % 2])

    def step(z, carry):
        plane(z, False)
        return carry

    for f in range(2):
        cut(0, f, q_bufs[f])
        for r in range(STRIPS):
            force(0, f, r, q_bufs[f], f_bufs[f])
    for r in range(STRIPS):
        solve_x(0, 0, r, f_0, s_0)
    lax.fori_loop(0, NZ - 1, step, 0)
    plane(NZ - 1, True)
    for t in range(STRIPS):
        part = slice(t * 128, (t + 1) * 128)
        value = jnp.transpose(cols[part, :])
        y_rhs[0, :, part] = value[0:ROWS]
        y_rhs[1, :, part] = value[ROWS : 2 * ROWS]


def big(odd, fields, ginv_x, ginv_y, received, beta_x):
    return pl.pallas_call(
        big_kernel,
        out_shape=(
            shaped(NF, NZ, CX, CY),
            shaped(ROWS, 2 * CY + 128),
            shaped(2, ROWS, CX),
            shaped(NF, 8, CX),
            shaped(NF, 8, CY),
        ),
        in_specs=[SM] + [VM] * 7 + [SM],
        out_specs=(VM,) * 5,
        scratch_shapes=[
            pltpu.VMEM((NF, CX, 2 * CX), BF16),
            pltpu.VMEM((NF, 3 * CY, CY), BF16),
            pltpu.VMEM((2 * CY, CY), BF16),
            pltpu.VMEM((STRIPS, CHUNK, WINDOW), BF16),
            pltpu.VMEM((CX, 2 * CY), BF16),
            pltpu.VMEM((CX, 2 * CY), BF16),
            pltpu.VMEM((2 * CX, CY), BF16),
            pltpu.VMEM((2 * CX, CY), BF16),
            pltpu.VMEM((CX, 2 * CY), BF16),
            pltpu.VMEM((CX, 2 * CY), BF16),
            pltpu.VMEM((CX, 128), F32),
            pltpu.VMEM((ROWS, 16, CY), F32),
            pltpu.VMEM((CX, 128), F32),
            pltpu.VMEM((CX // 128, 128, 128), F32),
        ],
        compiler_params=pltpu.CompilerParams(vmem_limit_bytes=24 * MIB),
        cost_estimate=pl.CostEstimate(flops=6_000_000_000, bytes_accessed=21 * MIB, transcendentals=0),
        name="forcing_and_products",
    )(odd, fields, ginv_x, ginv_y, *received, beta_x)


def merge(side, mine, other, state, width):
    is_right = jnp.broadcast_to(side, (ROWS, 1)) == 1

    def parts(ref):
        c = 2 * width
        return [
            ref[:, 0:width], ref[:, width:c],
            ref[:, c : c + 1], ref[:, c + 1 : c + 2], ref[:, c + 2 : c + 3], ref[:, c + 3 : c + 4],
        ]

    own, far = parts(mine), parts(other)
    l_first, l_last, l_p, l_s, l_q, l_t = [jnp.where(is_right, b, a) for a, b in zip(own, far)]
    r_first, r_last, r_p, r_s, r_q, r_t = [jnp.where(is_right, a, b) for a, b in zip(own, far)]
    inner = 1.0 / (1.0 - l_t * r_p)
    m_b = (l_last + l_t * r_first) * inner
    m_a = (r_first + r_p * l_last) * inner
    b_from_b, b_from_a = l_q * inner, l_t * r_s * inner
    a_from_b, a_from_a = r_p * l_q * inner, r_s * inner
    group = (
        l_first + l_s * m_a,
        r_last + r_q * m_b,
        l_p + l_s * a_from_b,
        l_s * a_from_a,
        r_q * b_from_b,
        r_t + r_q * b_from_a,
    )
    if state is None:
        prior, later, prior_b, prior_a, later_b, later_a = 0.0, 0.0, 1.0, 0.0, 0.0, 1.0
    else:
        prior, later, prior_b, prior_a, later_b, later_a = parts(state)
    fresh = []
    for base, by_b, by_a in ((prior, prior_b, prior_a), (later, later_b, later_a)):
        fresh.append(
            (
                base + jnp.where(is_right, by_b * m_b, by_a * m_a),
                jnp.where(is_right, by_b * b_from_b, by_b + by_a * a_from_b),
                jnp.where(is_right, by_a + by_b * b_from_a, by_a * a_from_a),
            )
        )
    return group, fresh


def lanes_of(values):
    spot = lax.broadcasted_iota(jnp.int32, (ROWS, 128), 1)
    total = jnp.zeros((ROWS, 128), F32)
    for place, value in enumerate(values):
        total = jnp.where(spot == place, value, total)
    return total


def merge_kernel(width, side, mine, other, *refs):
    state, (group_out, state_out) = (refs[0], refs[1:]) if len(refs) == 3 else (None, refs)
    group, fresh = merge(side[0], mine, other, state, width)
    group_out[:, 0:width] = group[0]
    group_out[:, width : 2 * width] = group[1]
    group_out[:, 2 * width :] = lanes_of(group[2:])
    state_out[:, 0:width] = fresh[0][0]
    state_out[:, width : 2 * width] = fresh[1][0]
    state_out[:, 2 * width :] = lanes_of((fresh[0][1], fresh[0][2], fresh[1][1], fresh[1][2]))


def merge_step(side, mine, other, state, width):
    carried = [] if state is None else [state]
    return pl.pallas_call(
        functools.partial(merge_kernel, width),
        out_shape=(shaped(ROWS, 2 * width + 128),) * 2,
        in_specs=[SM, VM, VM] + [VM] * len(carried),
        out_specs=(VM, VM),
        compiler_params=SMALL,
        cost_estimate=pl.CostEstimate(flops=200_000, bytes_accessed=200_000, transcendentals=0),
        name="merge_groups",
    )(side, mine, other, *carried)


def exchange(message, axis, width):
    count = lax.axis_size(axis)
    place = lax.axis_index(axis)
    state = None
    reach = 1
    while True:
        other = lax.ppermute(message, axis, [(i, i ^ reach) for i in range(count)])
        side = lax.rem(place // reach, 2).astype(jnp.int32).reshape(1)
        if 2 * reach >= count:
            return side, message, other, state
        message, state = merge_step(side, message, other, state, width)
        reach *= 2


def middle_kernel(side, mine, other, state, y_rhs, edge_x, edge_y, beta_x, beta_y, enter, message):
    group, fresh = merge(side[0], mine, other, state, CY)
    for f in range(NF):
        s = slice(f * NZ, (f + 1) * NZ)
        for e in range(2):
            enter[e, s, :] = beta_x[f] * fresh[e][0][s, :]
        for e in range(2):
            value = y_rhs[e, s, :]
            for g in range(2):
                scale = jnp.sum(enter[g, s, :] * edge_y[f, 2 + e : 3 + e, :], axis=1, keepdims=True)
                value = value + scale * edge_x[f, g : g + 1, :]
            message[s, e * CX : (e + 1) * CX] = value
        message[s, 2 * CX :] = fill_coefs(
            beta_y[f],
            edge_y[f, 0:1, 0:1],
            edge_y[f, 1:2, 0:1],
            edge_y[f, 0:1, CY - 1 : CY],
            edge_y[f, 1:2, CY - 1 : CY],
        )


def middle(last, y_rhs, edge_x, edge_y, beta_x, beta_y):
    return pl.pallas_call(
        middle_kernel,
        out_shape=(shaped(2, ROWS, CY), shaped(ROWS, 2 * CX + 128)),
        in_specs=[SM] + [VM] * 6 + [SM, SM],
        out_specs=(VM, VM),
        compiler_params=SMALL,
        cost_estimate=pl.CostEstimate(flops=500_000, bytes_accessed=500_000, transcendentals=0),
        name="between_interfaces",
    )(*last, y_rhs, edge_x, edge_y, beta_x, beta_y)


def rows_kernel(rows, ginv_y, out):
    high, low = halves(rows[...].reshape(2 * ROWS, CY))
    owner = lax.rem(lax.broadcasted_iota(jnp.int32, (2 * ROWS, 1), 0), ROWS) // NZ
    total = jnp.zeros((2 * ROWS, CY), F32)
    for f in range(NF):
        g_high, g_low = halves(ginv_y[f])
        value = dot_nt(high, g_high) + dot_nt(low, g_high) + dot_nt(high, g_low)
        total = jnp.where(owner == f, value, total)
    out[...] = total.reshape(2, ROWS, CY)


def row_products(rows, ginv_y):
    return pl.pallas_call(
        rows_kernel,
        out_shape=shaped(2, ROWS, CY),
        in_specs=[VM, VM],
        out_specs=VM,
        compiler_params=SMALL,
        cost_estimate=pl.CostEstimate(flops=300_000_000, bytes_accessed=2 * MIB, transcendentals=0),
        name="row_products",
    )(rows, ginv_y)


def update_kernel(side, mine, other, state, base, rows, edge_x, edge_y, beta_y, out, tall, wide, leave, done, sems):
    group, fresh = merge(side[0], mine, other, state, CX)
    for f in range(NF):
        s = slice(f * NZ, (f + 1) * NZ)
        for e in range(2):
            leave[e, s, :] = beta_y[f] * fresh[e][0][s, :]
    tall[...] = jnp.zeros_like(tall)
    wide[...] = jnp.zeros_like(wide)
    for k in range(ROWS):
        f = k // NZ
        tall[k, 0:2, :] = edge_x[f, 0:2, :]
        wide[k, 2:4, :] = edge_y[f, 0:2, :]
        for e in range(2):
            tall[k, 2 + e : 3 + e, :] = leave[e, k : k + 1, :]
            wide[k, e : e + 1, :] = rows[e, k : k + 1, :]

    def step(k, carry):
        f = k // NZ
        z = lax.rem(k, NZ)
        a_high, a_low = halves(tall[k])
        b_high, b_low = halves(wide[k])
        change = dot_tn(
            jnp.concatenate([a_high, a_low, a_high], axis=0), jnp.concatenate([b_high, b_high, b_low], axis=0)
        )
        done[f, z] = base[f, z] + change
        pltpu.make_async_copy(done.at[f, z], out.at[f, z], sems.at[k]).start()
        return carry

    lax.fori_loop(0, ROWS, step, 0)
    for k in range(ROWS):
        pltpu.make_async_copy(done.at[k // NZ, k % NZ], out.at[k // NZ, k % NZ], sems.at[k]).wait()


def update(last, base, rows, edge_x, edge_y, beta_y):
    return pl.pallas_call(
        update_kernel,
        out_shape=shaped(NF, NZ, CX, CY),
        in_specs=[SM] + [VM] * 7 + [SM],
        out_specs=HB,
        scratch_shapes=[
            pltpu.VMEM((ROWS, 16, CX), F32),
            pltpu.VMEM((ROWS, 16, CY), F32),
            pltpu.VMEM((2, ROWS, CX), F32),
            pltpu.VMEM((NF, NZ, CX, CY), F32),
            pltpu.SemaphoreType.DMA((ROWS,)),
        ],
        compiler_params=pltpu.CompilerParams(vmem_limit_bytes=12 * MIB),
        cost_estimate=pl.CostEstimate(flops=200_000_000, bytes_accessed=17 * MIB, transcendentals=0),
        name="update_result",
    )(*last, base, rows, edge_x, edge_y, beta_y)


def swap_pairs(value, axis, inner):
    count = lax.axis_size(axis)
    pairs = []
    for i in range(0 if inner else 1, count - 1, 2):
        pairs += [(i, i + 1), (i + 1, i)]
    return lax.ppermute(value, axis, pairs)


def local(fields, ginv_x, ginv_y, coupling_x, coupling_y):
    odd = jnp.stack([lax.rem(lax.axis_index(axis), 2) for axis in ("gx", "gy")]).astype(jnp.int32)
    fields, x_inner, x_outer, y_inner, y_outer = pack(odd, fields)
    received = (
        swap_pairs(x_inner, "gx", True),
        swap_pairs(x_outer, "gx", False),
        swap_pairs(y_inner, "gy", True),
        swap_pairs(y_outer, "gy", False),
    )
    base, message, y_rhs, edge_x, edge_y = big(odd, fields, ginv_x, ginv_y, received, coupling_x)
    last_x = exchange(message, "gx", CY)
    enter, message_y = middle(last_x, y_rhs, edge_x, edge_y, coupling_x, coupling_y)
    rows = row_products(enter, ginv_y)
    last_y = exchange(message_y, "gy", CX)
    return update(last_y, base, rows, edge_x, edge_y, coupling_y)


def solution(mesh):
    in_specs = (P(None, None, "gx", "gy"), P(None, "gx", None), P(None, "gy", None), P(), P())
    out_specs = P(None, None, "gx", "gy")
    return jax.shard_map(local, mesh=mesh, in_specs=in_specs, out_specs=out_specs, check_vma=False)
```

```python
import functools

import jax
import jax.numpy as jnp
from jax import lax
from jax.experimental import pallas as pl
from jax.experimental.pallas import tpu as pltpu
from jax.sharding import PartitionSpec as P

F32 = jnp.float32
BF16 = jnp.bfloat16
BAND = (45.0, -9.0, 1.0)
ADVECT = 0.3
BUOY = 0.5
CX = 512
CY = 256
NF = 4
NZ = 4
ROWS = NF * NZ
MIB = 1024 * 1024

VM = pl.BlockSpec(memory_space=pltpu.VMEM)
SM = pl.BlockSpec(memory_space=pltpu.SMEM)
HB = pl.BlockSpec(memory_space=pltpu.HBM)
SMALL = pltpu.CompilerParams(vmem_limit_bytes=4 * MIB)


def shaped(*dims):
    return jax.ShapeDtypeStruct(dims, F32)


def halves(value):
    high = value.astype(BF16)
    return high, (value - high.astype(F32)).astype(BF16)


def dot(left, right):
    return lax.dot_general(left, right, (((1,), (0,)), ((), ())), preferred_element_type=F32)


def dot_nt(left, right):
    return lax.dot_general(left, right, (((1,), (1,)), ((), ())), preferred_element_type=F32)


def dot_tn(left, right):
    return lax.dot_general(left, right, (((0,), (0,)), ((), ())), preferred_element_type=F32)


def odd_blocks():
    return [lax.rem(lax.axis_index(axis), 2) == 1 for axis in ("gx", "gy")]


def pack_kernel(fields, planes, x_inner, x_outer, y_inner, y_outer, lanes, turned, sems):
    for f in range(NF):
        pltpu.make_async_copy(fields.at[f], planes.at[f], sems.at[f]).start()
    x_odd, y_odd = odd_blocks()
    step = 64
    for f in range(NF):
        pltpu.make_async_copy(fields.at[f], planes.at[f], sems.at[f]).wait()

        def chunk(r, carry, f=f):
            at = pl.ds(pl.multiple_of(r * step, step), step)
            spot = lax.broadcasted_iota(jnp.int32, (step, 128), 1)
            total = jnp.zeros((step, 128), F32) if f == 0 else lanes[at, :]
            for z in range(NZ):
                ends = jnp.where(spot >= 125, planes[f, z, at, 128:256], 0.0)
                ends = jnp.where(spot < 3, planes[f, z, at, 0:128], ends)
                total = total + pltpu.roll(ends, 8 * (f * NZ + z) + 3, 1)
            lanes[at, :] = total
            return carry

        lax.fori_loop(0, CX // step, chunk, 0, unroll=True)
        for z in range(NZ):
            k = f * NZ + z
            for c in range(3):
                top = planes[f, z, c : c + 1, :]
                bottom = planes[f, z, CX - 3 + c : CX - 2 + c, :]
                x_inner[c, k : k + 1, :] = jnp.where(x_odd, top, bottom)
                x_outer[c, k : k + 1, :] = jnp.where(x_odd, bottom, top)
    for t in range(CX // 128):
        part = slice(t * 128, (t + 1) * 128)
        turned[t] = jnp.transpose(lanes[part, :])
        for c in range(3):
            right = turned[t, pl.ds(c, ROWS, stride=8), :]
            left = turned[t, pl.ds(3 + c, ROWS, stride=8), :]
            y_inner[c, :, part] = jnp.where(y_odd, left, right)
            y_outer[c, :, part] = jnp.where(y_odd, right, left)


def pack(fields):
    return pl.pallas_call(
        pack_kernel,
        out_shape=(
            shaped(NF, NZ, CX, CY),
            shaped(3, ROWS, CY),
            shaped(3, ROWS, CY),
            shaped(3, ROWS, CX),
            shaped(3, ROWS, CX),
        ),
        in_specs=[HB],
        out_specs=(VM,) * 5,
        scratch_shapes=[
            pltpu.VMEM((CX, 128), F32),
            pltpu.VMEM((CX // 128, 128, 128), F32),
            pltpu.SemaphoreType.DMA((NF,)),
        ],
        compiler_params=pltpu.CompilerParams(vmem_limit_bytes=44 * MIB),
        cost_estimate=pl.CostEstimate(flops=4_000_000, bytes_accessed=9 * MIB, transcendentals=0),
        name="pack_edges",
    )(fields)


WINDOW = 256
CHUNK = 128
STRIPS = CX // CHUNK
BASES = (0, 64, 192, 256)


def band(shape, offset, along):
    gap = lax.broadcasted_iota(jnp.int32, shape, along) - lax.broadcasted_iota(jnp.int32, shape, 1 - along)
    gap = gap - offset
    total = jnp.zeros(shape, F32)
    for reach, weight in zip((1, 2, 3), BAND):
        total = jnp.where(gap == reach, weight, total)
        total = jnp.where(gap == -reach, -weight, total)
    return total.astype(BF16)


def halo_sums(before, after):
    sums = []
    for j in range(3):
        sums.append(sum(-BAND[o - 1] * before[3 + j - o] for o in range(j + 1, 4)))
    for j in range(3):
        sums.append(sum(BAND[o - 1] * after[j + o - 3] for o in range(3 - j, 4)))
    return sums


def fill_coefs(beta, first_first, first_last, last_first, last_last):
    spot = lax.broadcasted_iota(jnp.int32, (NZ, 128), 1)
    values = jnp.where(
        spot == 0,
        first_first,
        jnp.where(spot == 1, first_last, jnp.where(spot == 2, last_first, jnp.where(spot == 3, last_last, 0.0))),
    )
    return beta * values


def prep_kernel(gx, gy, beta_x, gx_cat, gy_cat, gx_rows, gy_rows, edge_x, edge_y, coefs):
    gx_rows[...] = jnp.zeros_like(gx_rows)
    gy_rows[...] = jnp.zeros_like(gy_rows)
    tile = 16
    spot = lax.broadcasted_iota(jnp.int32, (tile, 1), 0)

    def ends(first, last):
        f_high, f_low = halves(first)
        l_high, l_low = halves(last)
        parts = [value.astype(F32) for value in (f_high, l_high, f_low, l_low)]
        total = jnp.zeros((tile, first.shape[1]), F32)
        for place, value in enumerate(parts):
            total = jnp.where(spot == place, value, total)
        return total.astype(BF16)

    for f in range(NF):
        turned_g = jnp.transpose(gy[f])
        high, low = halves(turned_g)
        gy_cat[f, 0:CY, :] = high
        gy_cat[f, CY : 2 * CY, :] = high
        gy_cat[f, 2 * CY :, :] = low
        edge_y[f, 0:1, :] = turned_g[0:1]
        edge_y[f, 1:2, :] = turned_g[CY - 1 : CY]
        edge_y[f, 2:3, :] = gy[f, 0:1, :]
        edge_y[f, 3:4, :] = gy[f, CY - 1 : CY, :]
        gy_rows[f] = ends(gy[f, 0:1, :], gy[f, CY - 1 : CY, :])
        gx_rows[f] = ends(gx[f, 0:1, :], gx[f, CX - 1 : CX, :])

        def split(r, carry, f=f):
            at = pl.ds(pl.multiple_of(r * CHUNK, CHUNK), CHUNK)
            high, low = halves(gx[f, at, :])
            gx_cat[f, at, 0:CX] = high
            gx_cat[f, at, CX:] = low
            return carry

        lax.fori_loop(0, CX // CHUNK, split, 0)
        edge_x[f, 0:1, :] = jnp.transpose(gx[f, :, 0:128])[0:1]
        edge_x[f, 1:2, :] = jnp.transpose(gx[f, :, CX - 128 : CX])[127:128]
        coefs[f * NZ : (f + 1) * NZ, :] = fill_coefs(
            beta_x[f],
            gx[f, 0:1, 0:1],
            gx[f, 0:1, CX - 1 : CX],
            gx[f, CX - 1 : CX, 0:1],
            gx[f, CX - 1 : CX, CX - 1 : CX],
        )


def packed(*dims):
    return jax.ShapeDtypeStruct(dims, BF16)


def prep(ginv_x, ginv_y, beta_x):
    return pl.pallas_call(
        prep_kernel,
        out_shape=(
            packed(NF, CX, 2 * CX),
            packed(NF, 3 * CY, CY),
            packed(NF, 16, CX),
            packed(NF, 16, CY),
            shaped(NF, 8, CX),
            shaped(NF, 8, CY),
            shaped(ROWS, 128),
        ),
        in_specs=[VM, VM, SM],
        out_specs=(VM,) * 7,
        compiler_params=SMALL,
        cost_estimate=pl.CostEstimate(flops=20_000_000, bytes_accessed=5 * MIB, transcendentals=0),
        name="split_matrices",
    )(ginv_x, ginv_y, beta_x)


def forcing_kernel(
    fields, x_inner, x_outer, y_inner, y_outer, gx_rows, gy_rows, coefs,
    forcing, message, weighted,
    band_y, band_x, q_0, q_1, halo_rows, halo_cols, turned,
):
    both = band((CY, CY), 0, 0)
    band_y[0:CY, :] = both
    band_y[CY:, :] = both
    for r in range(STRIPS):
        band_x[r] = band((CHUNK, WINDOW), r * CHUNK - BASES[r], 1)
    halo_rows[...] = jnp.zeros_like(halo_rows)
    turned[...] = jnp.zeros_like(turned)
    x_odd, y_odd = odd_blocks()
    above = [jnp.where(x_odd, x_inner[c], x_outer[c]) for c in range(3)]
    below = [jnp.where(x_odd, x_outer[c], x_inner[c]) for c in range(3)]
    for j, value in enumerate(halo_sums(above, below)):
        for k in range(ROWS):
            if j < 3:
                halo_rows[k, j : j + 1, :] = value[k : k + 1, :]
            else:
                halo_rows[k, j + 10 : j + 11, :] = value[k : k + 1, :]
    before = [jnp.where(y_odd, y_inner[c], y_outer[c]) for c in range(3)]
    behind = [jnp.where(y_odd, y_outer[c], y_inner[c]) for c in range(3)]
    for j, value in enumerate(halo_sums(before, behind)):
        for t in range(STRIPS):
            turned[t, pl.ds(j if j < 3 else j + 2, ROWS, stride=8), :] = value[:, t * 128 : (t + 1) * 128]
    for t in range(STRIPS):
        halo_cols[t * 128 : (t + 1) * 128, :] = jnp.transpose(turned[t])
    message[:, 2 * CY :] = coefs[...]

    def cut(z, f, q_cat):
        for r in range(STRIPS):
            at = slice(r * CHUNK, (r + 1) * CHUNK)
            high, low = halves(fields[f, z, at, :])
            q_cat[at, 0:CY] = high
            q_cat[at, CY:] = low

    def force(z, f, r, q_cat):
        at = slice(r * CHUNK, (r + 1) * CHUNK)
        k = f * NZ + z
        window = slice(BASES[r], BASES[r] + WINDOW)
        dx = dot(band_x[r], q_cat[window, 0:CY]) + dot(band_x[r], q_cat[window, CY:])
        dy = dot(q_cat[at, :], band_y[...])
        if r == 0:
            dx = jnp.concatenate([dx[0:8] + halo_rows[k, 0:8], dx[8:]], axis=0)
        if r == STRIPS - 1:
            dx = jnp.concatenate([dx[: CHUNK - 8], dx[CHUNK - 8 :] + halo_rows[k, 8:16]], axis=0)
        spot = lax.broadcasted_iota(jnp.int32, (CHUNK, 128), 1)
        side = halo_cols[at, :]
        left = jnp.where(spot < 3, pltpu.roll(side, lax.rem(128 - 8 * k, 128), 1), 0.0)
        right = jnp.where(spot >= 125, pltpu.roll(side, lax.rem(248 - 8 * k, 128), 1), 0.0)
        dy = dy + jnp.concatenate([left, right], axis=1)
        rise = fields[f, lax.rem(z + 1, NZ), at, :] - fields[f, lax.rem(z + NZ - 1, NZ), at, :]
        value = fields[f, z, at, :] - (
            (ADVECT / 60.0) * (fields[1, z, at, :] * dx + fields[2, z, at, :] * dy)
            + (0.5 * ADVECT) * (fields[3, z, at, :] * rise)
        )
        if f == 3:
            value = value + BUOY * fields[0, z, at, :]
        high, low = halves(value)
        forcing[k, at, :] = high
        forcing[k, CX + r * CHUNK : CX + (r + 1) * CHUNK, :] = low

    def contract(z, f):
        k = f * NZ + z
        by_high = dot(gx_rows[f], forcing[k, 0:CX, :])
        by_low = dot(gx_rows[f], forcing[k, CX:, :])
        message[pl.ds(k, 1), 0:CY] = by_high[0:1] + by_high[2:3] + by_low[0:1]
        message[pl.ds(k, 1), CY : 2 * CY] = by_high[1:2] + by_high[3:4] + by_low[1:2]
        by_high = dot_nt(gy_rows[f], forcing[k, 0:CX, :])
        by_low = dot_nt(gy_rows[f], forcing[k, CX:, :])
        weighted[0, pl.ds(k, 1), :] = by_high[0:1] + by_high[2:3] + by_low[0:1]
        weighted[1, pl.ds(k, 1), :] = by_high[1:2] + by_high[3:4] + by_low[1:2]

    q_bufs = (q_0, q_1)
    cut(0, 0, q_0)

    def step(z, carry):
        for f in range(NF):
            z_next, f_next = (z, f + 1) if f + 1 < NF else (lax.rem(z + 1, NZ), 0)
            cut(z_next, f_next, q_bufs[f_next % 2])
            for r in range(STRIPS):
                force(z, f, r, q_bufs[f % 2])
            if f > 0:
                contract(z, f - 1)
        contract(z, NF - 1)
        return carry

    lax.fori_loop(0, NZ, step, 0)


def force_all(fields, received, gx_rows, gy_rows, coefs):
    return pl.pallas_call(
        forcing_kernel,
        out_shape=(packed(ROWS, 2 * CX, CY), shaped(ROWS, 2 * CY + 128), shaped(2, ROWS, CX)),
        in_specs=[VM] * 8,
        out_specs=(VM,) * 3,
        scratch_shapes=[
            pltpu.VMEM((2 * CY, CY), BF16),
            pltpu.VMEM((STRIPS, CHUNK, WINDOW), BF16),
            pltpu.VMEM((CX, 2 * CY), BF16),
            pltpu.VMEM((CX, 2 * CY), BF16),
            pltpu.VMEM((ROWS, 16, CY), F32),
            pltpu.VMEM((CX, 128), F32),
            pltpu.VMEM((CX // 128, 128, 128), F32),
        ],
        compiler_params=pltpu.CompilerParams(vmem_limit_bytes=12 * MIB),
        cost_estimate=pl.CostEstimate(flops=4_000_000_000, bytes_accessed=16 * MIB, transcendentals=0),
        name="forcing",
    )(fields, *received, gx_rows, gy_rows, coefs)


def products_kernel(f, forcing, gx_cat, gy_cat, out, s_0, s_1):
    def solve_x(z, r, s_cat):
        at = slice(r * CHUNK, (r + 1) * CHUNK)
        k = f * NZ + z
        high, low = forcing.at[k, 0:CX, :], forcing.at[k, CX : 2 * CX, :]
        section = dot(gx_cat[f, at, 0:CX], high[...]) + dot(gx_cat[f, at, 0:CX], low[...])
        section = section + dot(gx_cat[f, at, CX:], high[...])
        s_high, s_low = halves(section)
        s_cat[at, 0:CY] = s_high
        s_cat[at, CY:] = s_low

    def solve_y(z, r, s_cat):
        at = slice(r * CHUNK, (r + 1) * CHUNK)
        out[z, at, :] = dot(s_cat[at, :], gy_cat[f, 0 : 2 * CY, :]) + dot(s_cat[at, 0:CY], gy_cat[f, 2 * CY :, :])

    bufs = (s_0, s_1)
    for z in range(NZ + 1):
        for r in range(STRIPS):
            if z < NZ:
                solve_x(z, r, bufs[z % 2])
            if z > 0:
                solve_y(z - 1, r, bufs[(z - 1) % 2])


def products(f, forcing, gx_cat, gy_cat):
    return pl.pallas_call(
        functools.partial(products_kernel, f),
        out_shape=shaped(NZ, CX, CY),
        in_specs=[VM] * 3,
        out_specs=VM,
        scratch_shapes=[pltpu.VMEM((CX, 2 * CY), BF16), pltpu.VMEM((CX, 2 * CY), BF16)],
        compiler_params=pltpu.CompilerParams(vmem_limit_bytes=6 * MIB),
        cost_estimate=pl.CostEstimate(flops=2_400_000_000, bytes_accessed=6 * MIB, transcendentals=0),
        name="block_products",
    )(forcing, gx_cat, gy_cat)


def weigh_kernel(weighted, gx_cat, out):
    high, low = halves(weighted[...].reshape(2 * ROWS, CX))
    owner = lax.rem(lax.broadcasted_iota(jnp.int32, (2 * ROWS, 1), 0), ROWS) // NZ
    total = jnp.zeros((2 * ROWS, CX), F32)
    for f in range(NF):
        value = dot_nt(high, gx_cat[f, :, 0:CX]) + dot_nt(low, gx_cat[f, :, 0:CX]) + dot_nt(high, gx_cat[f, :, CX:])
        total = jnp.where(owner == f, value, total)
    out[...] = total.reshape(2, ROWS, CX)


def weigh(weighted, gx_cat):
    return pl.pallas_call(
        weigh_kernel,
        out_shape=shaped(2, ROWS, CX),
        in_specs=[VM, VM],
        out_specs=VM,
        compiler_params=SMALL,
        cost_estimate=pl.CostEstimate(flops=500_000_000, bytes_accessed=5 * MIB, transcendentals=0),
        name="y_right_side",
    )(weighted, gx_cat)


def merge(side, mine, other, state, width):
    axis, reach = side
    is_right = jnp.broadcast_to(lax.rem(lax.axis_index(axis) // reach, 2), (ROWS, 1)) == 1

    def parts(ref):
        c = 2 * width
        return [
            ref[:, 0:width], ref[:, width:c],
            ref[:, c : c + 1], ref[:, c + 1 : c + 2], ref[:, c + 2 : c + 3], ref[:, c + 3 : c + 4],
        ]

    own, far = parts(mine), parts(other)
    l_first, l_last, l_p, l_s, l_q, l_t = [jnp.where(is_right, b, a) for a, b in zip(own, far)]
    r_first, r_last, r_p, r_s, r_q, r_t = [jnp.where(is_right, a, b) for a, b in zip(own, far)]
    inner = 1.0 / (1.0 - l_t * r_p)
    m_b = (l_last + l_t * r_first) * inner
    m_a = (r_first + r_p * l_last) * inner
    b_from_b, b_from_a = l_q * inner, l_t * r_s * inner
    a_from_b, a_from_a = r_p * l_q * inner, r_s * inner
    group = (
        l_first + l_s * m_a,
        r_last + r_q * m_b,
        l_p + l_s * a_from_b,
        l_s * a_from_a,
        r_q * b_from_b,
        r_t + r_q * b_from_a,
    )
    if state is None:
        prior, later, prior_b, prior_a, later_b, later_a = 0.0, 0.0, 1.0, 0.0, 0.0, 1.0
    else:
        prior, later, prior_b, prior_a, later_b, later_a = parts(state)
    fresh = []
    for base, by_b, by_a in ((prior, prior_b, prior_a), (later, later_b, later_a)):
        fresh.append(
            (
                base + jnp.where(is_right, by_b * m_b, by_a * m_a),
                jnp.where(is_right, by_b * b_from_b, by_b + by_a * a_from_b),
                jnp.where(is_right, by_a + by_b * b_from_a, by_a * a_from_a),
            )
        )
    return group, fresh


def lanes_of(values):
    spot = lax.broadcasted_iota(jnp.int32, (ROWS, 128), 1)
    total = jnp.zeros((ROWS, 128), F32)
    for place, value in enumerate(values):
        total = jnp.where(spot == place, value, total)
    return total


def merge_kernel(side, width, mine, other, *refs):
    state, (group_out, state_out) = (refs[0], refs[1:]) if len(refs) == 3 else (None, refs)
    group, fresh = merge(side, mine, other, state, width)
    group_out[:, 0:width] = group[0]
    group_out[:, width : 2 * width] = group[1]
    group_out[:, 2 * width :] = lanes_of(group[2:])
    state_out[:, 0:width] = fresh[0][0]
    state_out[:, width : 2 * width] = fresh[1][0]
    state_out[:, 2 * width :] = lanes_of((fresh[0][1], fresh[0][2], fresh[1][1], fresh[1][2]))


def merge_step(side, mine, other, state, width):
    carried = [] if state is None else [state]
    return pl.pallas_call(
        functools.partial(merge_kernel, side, width),
        out_shape=(shaped(ROWS, 2 * width + 128),) * 2,
        in_specs=[VM, VM] + [VM] * len(carried),
        out_specs=(VM, VM),
        compiler_params=SMALL,
        cost_estimate=pl.CostEstimate(flops=200_000, bytes_accessed=200_000, transcendentals=0),
        name="merge_groups",
    )(mine, other, *carried)


def exchange(message, axis, width, fillers):
    count = lax.axis_size(axis)
    state = None
    reach = 1
    results = []
    while True:
        other = lax.ppermute(message, axis, [(i, i ^ reach) for i in range(count)])
        filler = fillers.get(reach)
        if filler is not None:
            function, first, *rest = filler
            first, message = lax.optimization_barrier((first, message))
            result = function(first, *rest)
            result, message = lax.optimization_barrier((result, message))
            results.append(result)
        if 2 * reach >= count:
            return ((axis, reach), message, other, state), results
        message, state = merge_step((axis, reach), message, other, state, width)
        reach *= 2


def middle_kernel(side, mine, other, state, y_rhs, edge_x, edge_y, beta_x, beta_y, enter, message):
    group, fresh = merge(side, mine, other, state, CY)
    for f in range(NF):
        s = slice(f * NZ, (f + 1) * NZ)
        for e in range(2):
            enter[e, s, :] = beta_x[f] * fresh[e][0][s, :]
        for e in range(2):
            value = y_rhs[e, s, :]
            for g in range(2):
                scale = jnp.sum(enter[g, s, :] * edge_y[f, 2 + e : 3 + e, :], axis=1, keepdims=True)
                value = value + scale * edge_x[f, g : g + 1, :]
            message[s, e * CX : (e + 1) * CX] = value
        message[s, 2 * CX :] = fill_coefs(
            beta_y[f],
            edge_y[f, 0:1, 0:1],
            edge_y[f, 1:2, 0:1],
            edge_y[f, 0:1, CY - 1 : CY],
            edge_y[f, 1:2, CY - 1 : CY],
        )


def middle(last, y_rhs, edge_x, edge_y, beta_x, beta_y):
    return pl.pallas_call(
        functools.partial(middle_kernel, last[0]),
        out_shape=(shaped(2, ROWS, CY), shaped(ROWS, 2 * CX + 128)),
        in_specs=[VM] * 6 + [SM, SM],
        out_specs=(VM, VM),
        compiler_params=SMALL,
        cost_estimate=pl.CostEstimate(flops=500_000, bytes_accessed=500_000, transcendentals=0),
        name="between_interfaces",
    )(*last[1:], y_rhs, edge_x, edge_y, beta_x, beta_y)


def rows_kernel(rows, ginv_y, out):
    high, low = halves(rows[...].reshape(2 * ROWS, CY))
    owner = lax.rem(lax.broadcasted_iota(jnp.int32, (2 * ROWS, 1), 0), ROWS) // NZ
    total = jnp.zeros((2 * ROWS, CY), F32)
    for f in range(NF):
        g_high, g_low = halves(ginv_y[f])
        value = dot_nt(high, g_high) + dot_nt(low, g_high) + dot_nt(high, g_low)
        total = jnp.where(owner == f, value, total)
    out[...] = total.reshape(2, ROWS, CY)


def row_products(rows, ginv_y):
    return pl.pallas_call(
        rows_kernel,
        out_shape=shaped(2, ROWS, CY),
        in_specs=[VM, VM],
        out_specs=VM,
        compiler_params=SMALL,
        cost_estimate=pl.CostEstimate(flops=300_000_000, bytes_accessed=2 * MIB, transcendentals=0),
        name="row_products",
    )(rows, ginv_y)


def update_kernel(side, mine, other, state, base_0, base_1, base_2, base_3, rows, edge_x, edge_y, beta_y, out, tall, wide, leave, done, sems):
    group, fresh = merge(side, mine, other, state, CX)
    for f in range(NF):
        s = slice(f * NZ, (f + 1) * NZ)
        for e in range(2):
            leave[e, s, :] = beta_y[f] * fresh[e][0][s, :]
    tall[...] = jnp.zeros_like(tall)
    wide[...] = jnp.zeros_like(wide)
    for k in range(ROWS):
        f = k // NZ
        tall[k, 0:2, :] = edge_x[f, 0:2, :]
        wide[k, 2:4, :] = edge_y[f, 0:2, :]
        for e in range(2):
            tall[k, 2 + e : 3 + e, :] = leave[e, k : k + 1, :]
            wide[k, e : e + 1, :] = rows[e, k : k + 1, :]

    for f, base in enumerate((base_0, base_1, base_2, base_3)):

        def step(z, carry, f=f, base=base):
            k = f * NZ + z
            a_high, a_low = halves(tall[k])
            b_high, b_low = halves(wide[k])
            change = dot_tn(
                jnp.concatenate([a_high, a_low, a_high], axis=0), jnp.concatenate([b_high, b_high, b_low], axis=0)
            )
            done[f, z] = base[z] + change
            pltpu.make_async_copy(done.at[f, z], out.at[f, z], sems.at[k]).start()
            return carry

        lax.fori_loop(0, NZ, step, 0)
    for k in range(ROWS):
        pltpu.make_async_copy(done.at[k // NZ, k % NZ], out.at[k // NZ, k % NZ], sems.at[k]).wait()


def update(last, base, rows, edge_x, edge_y, beta_y):
    return pl.pallas_call(
        functools.partial(update_kernel, last[0]),
        out_shape=shaped(NF, NZ, CX, CY),
        in_specs=[VM] * 10 + [SM],
        out_specs=HB,
        scratch_shapes=[
            pltpu.VMEM((ROWS, 16, CX), F32),
            pltpu.VMEM((ROWS, 16, CY), F32),
            pltpu.VMEM((2, ROWS, CX), F32),
            pltpu.VMEM((NF, NZ, CX, CY), F32),
            pltpu.SemaphoreType.DMA((ROWS,)),
        ],
        compiler_params=pltpu.CompilerParams(vmem_limit_bytes=12 * MIB),
        cost_estimate=pl.CostEstimate(flops=200_000_000, bytes_accessed=17 * MIB, transcendentals=0),
        name="update_result",
    )(*last[1:], *base, rows, edge_x, edge_y, beta_y)


def swap_pairs(value, axis, inner):
    count = lax.axis_size(axis)
    pairs = []
    for i in range(0 if inner else 1, count - 1, 2):
        pairs += [(i, i + 1), (i + 1, i)]
    return lax.ppermute(value, axis, pairs)


def local(fields, ginv_x, ginv_y, coupling_x, coupling_y):
    fields, x_inner, x_outer, y_inner, y_outer = pack(fields)
    received = (
        swap_pairs(x_inner, "gx", True),
        swap_pairs(x_outer, "gx", False),
        swap_pairs(y_inner, "gy", True),
        swap_pairs(y_outer, "gy", False),
    )
    gx_cat, gy_cat, gx_rows, gy_rows, edge_x, edge_y, coefs = prep(ginv_x, ginv_y, coupling_x)
    forcing, message, weighted = force_all(fields, received, gx_rows, gy_rows, coefs)

    def product(f):
        return lambda first, gx, gy: products(f, first, gx, gy), forcing, gx_cat, gy_cat

    last_x, (y_rhs, base_0) = exchange(message, "gx", CY, {2: (weigh, weighted, gx_cat), 4: product(0)})
    enter, message_y = middle(last_x, y_rhs, edge_x, edge_y, coupling_x, coupling_y)
    last_y, bases = exchange(message_y, "gy", CX, {2: product(1), 4: product(2), 8: product(3)})
    rows = row_products(enter, ginv_y)
    return update(last_y, [base_0] + bases, rows, edge_x, edge_y, coupling_y)


def solution(mesh):
    in_specs = (P(None, None, "gx", "gy"), P(None, "gx", None), P(None, "gy", None), P(), P())
    out_specs = P(None, None, "gx", "gy")
    return jax.shard_map(local, mesh=mesh, in_specs=in_specs, out_specs=out_specs, check_vma=False)
```

```python
import functools

import jax
import jax.numpy as jnp
from jax import lax
from jax.experimental import pallas as pl
from jax.experimental.pallas import tpu as pltpu
from jax.sharding import PartitionSpec as P

F32 = jnp.float32
BF16 = jnp.bfloat16
BAND = (45.0, -9.0, 1.0)
ADVECT = 0.3
BUOY = 0.5
CX = 512
CY = 256
NF = 4
NZ = 4
ROWS = NF * NZ
MIB = 1024 * 1024

VM = pl.BlockSpec(memory_space=pltpu.VMEM)
SM = pl.BlockSpec(memory_space=pltpu.SMEM)
HB = pl.BlockSpec(memory_space=pltpu.HBM)
SMALL = pltpu.CompilerParams(vmem_limit_bytes=4 * MIB)


def shaped(*dims):
    return jax.ShapeDtypeStruct(dims, F32)


def packed(*dims):
    return jax.ShapeDtypeStruct(dims, BF16)


def halves(value):
    high = value.astype(BF16)
    return high, (value - high.astype(F32)).astype(BF16)


def dot(left, right):
    return lax.dot_general(left, right, (((1,), (0,)), ((), ())), preferred_element_type=F32)


def dot_nt(left, right):
    return lax.dot_general(left, right, (((1,), (1,)), ((), ())), preferred_element_type=F32)


def dot_tn(left, right):
    return lax.dot_general(left, right, (((0,), (0,)), ((), ())), preferred_element_type=F32)


def odd_blocks():
    return [lax.rem(lax.axis_index(axis), 2) == 1 for axis in ("gx", "gy")]


def pack_kernel(fields, planes, q_cat, x_inner, x_outer, y_inner, y_outer, lanes, turned, sems):
    groups = [(f, z) for f in range(NF) for z in (0, 2)]
    copies = [
        pltpu.make_async_copy(fields.at[f, z : z + 2], planes.at[f, z : z + 2], sems.at[g])
        for g, (f, z) in enumerate(groups)
    ]
    for copy in copies:
        copy.start()
    x_odd, y_odd = odd_blocks()
    step = 64
    for g, (f, start) in enumerate(groups):
        copies[g].wait()

        def chunk(r, carry, f=f, start=start, g=g):
            at = pl.ds(pl.multiple_of(r * step, step), step)
            spot = lax.broadcasted_iota(jnp.int32, (step, 128), 1)
            total = jnp.zeros((step, 128), F32) if g == 0 else lanes[at, :]
            for z in (start, start + 1):
                k = f * NZ + z
                value = planes[f, z, at, :]
                ends = jnp.where(spot >= 125, value[:, 128:256], 0.0)
                ends = jnp.where(spot < 3, value[:, 0:128], ends)
                total = total + pltpu.roll(ends, 8 * k + 3, 1)
                high, low = halves(value)
                q_cat[k, at, 0:CY] = high
                q_cat[k, at, CY:] = low
            lanes[at, :] = total
            return carry

        lax.fori_loop(0, CX // step, chunk, 0, unroll=True)
        for z in (start, start + 1):
            k = f * NZ + z
            for c in range(3):
                top = planes[f, z, c : c + 1, :]
                bottom = planes[f, z, CX - 3 + c : CX - 2 + c, :]
                x_inner[c, k : k + 1, :] = jnp.where(x_odd, top, bottom)
                x_outer[c, k : k + 1, :] = jnp.where(x_odd, bottom, top)
    for t in range(CX // 128):
        part = slice(t * 128, (t + 1) * 128)
        turned[t] = jnp.transpose(lanes[part, :])
        for c in range(3):
            right = turned[t, pl.ds(c, ROWS, stride=8), :]
            left = turned[t, pl.ds(3 + c, ROWS, stride=8), :]
            y_inner[c, :, part] = jnp.where(y_odd, left, right)
            y_outer[c, :, part] = jnp.where(y_odd, right, left)


def pack(fields):
    return pl.pallas_call(
        pack_kernel,
        out_shape=(
            shaped(NF, NZ, CX, CY),
            packed(ROWS, CX, 2 * CY),
            shaped(3, ROWS, CY),
            shaped(3, ROWS, CY),
            shaped(3, ROWS, CX),
            shaped(3, ROWS, CX),
        ),
        in_specs=[HB],
        out_specs=(VM,) * 6,
        scratch_shapes=[
            pltpu.VMEM((CX, 128), F32),
            pltpu.VMEM((CX // 128, 128, 128), F32),
            pltpu.SemaphoreType.DMA((2 * NF,)),
        ],
        compiler_params=pltpu.CompilerParams(vmem_limit_bytes=35 * MIB),
        cost_estimate=pl.CostEstimate(flops=10_000_000, bytes_accessed=9 * MIB, transcendentals=0),
        name="pack_edges",
    )(fields)


WINDOW = 256
CHUNK = 128
STRIPS = CX // CHUNK
BASES = (0, 64, 192, 256)


def band(shape, offset, along):
    gap = lax.broadcasted_iota(jnp.int32, shape, along) - lax.broadcasted_iota(jnp.int32, shape, 1 - along)
    gap = gap - offset
    total = jnp.zeros(shape, F32)
    for reach, weight in zip((1, 2, 3), BAND):
        total = jnp.where(gap == reach, weight, total)
        total = jnp.where(gap == -reach, -weight, total)
    return total.astype(BF16)


def halo_sums(before, after):
    sums = []
    for j in range(3):
        sums.append(sum(-BAND[o - 1] * before[3 + j - o] for o in range(j + 1, 4)))
    for j in range(3):
        sums.append(sum(BAND[o - 1] * after[j + o - 3] for o in range(3 - j, 4)))
    return sums


def fill_coefs(beta, first_first, first_last, last_first, last_last):
    spot = lax.broadcasted_iota(jnp.int32, (NZ, 128), 1)
    values = jnp.where(
        spot == 0,
        first_first,
        jnp.where(spot == 1, first_last, jnp.where(spot == 2, last_first, jnp.where(spot == 3, last_last, 0.0))),
    )
    return beta * values


def prep_kernel(gx, gy, beta_x, gx_cat, gy_cat, gx_rows, gy_rows, edge_x, edge_y, coefs):
    gx_rows[...] = jnp.zeros_like(gx_rows)
    edge_x[...] = jnp.zeros_like(edge_x)
    gy_rows[...] = jnp.zeros_like(gy_rows)
    tile = 16
    spot = lax.broadcasted_iota(jnp.int32, (tile, 1), 0)

    def ends(first, last):
        f_high, f_low = halves(first)
        l_high, l_low = halves(last)
        parts = [value.astype(F32) for value in (f_high, l_high, f_low, l_low)]
        total = jnp.zeros((tile, first.shape[1]), F32)
        for place, value in enumerate(parts):
            total = jnp.where(spot == place, value, total)
        return total.astype(BF16)

    for f in range(NF):
        turned_g = jnp.transpose(gy[f])
        high, low = halves(turned_g)
        gy_cat[f, 0:CY, :] = high
        gy_cat[f, CY : 2 * CY, :] = high
        gy_cat[f, 2 * CY :, :] = low
        edge_y[f, 0:1, :] = turned_g[0:1]
        edge_y[f, 1:2, :] = turned_g[CY - 1 : CY]
        edge_y[f, 2:3, :] = gy[f, 0:1, :]
        edge_y[f, 3:4, :] = gy[f, CY - 1 : CY, :]
        gy_rows[f] = ends(gy[f, 0:1, :], gy[f, CY - 1 : CY, :])
        gx_rows[f] = ends(gx[f, 0:1, :], gx[f, CX - 1 : CX, :])

        def split(r, carry, f=f):
            at = pl.ds(pl.multiple_of(r * CHUNK, CHUNK), CHUNK)
            high, low = halves(gx[f, at, :])
            gx_cat[f, at, 0:CX] = high
            gx_cat[f, at, CX:] = low
            return carry

        lax.fori_loop(0, CX // CHUNK, split, 0)
        edge_x[f, 0:1, :] = jnp.transpose(gx[f, :, 0:128])[0:1]
        edge_x[f, 1:2, :] = jnp.transpose(gx[f, :, CX - 128 : CX])[127:128]
        coefs[f * NZ : (f + 1) * NZ, :] = fill_coefs(
            beta_x[f],
            gx[f, 0:1, 0:1],
            gx[f, 0:1, CX - 1 : CX],
            gx[f, CX - 1 : CX, 0:1],
            gx[f, CX - 1 : CX, CX - 1 : CX],
        )


def prep(ginv_x, ginv_y, beta_x):
    return pl.pallas_call(
        prep_kernel,
        out_shape=(
            packed(NF, CX, 2 * CX),
            packed(NF, 3 * CY, CY),
            packed(NF, 16, CX),
            packed(NF, 16, CY),
            shaped(NF, 8, CX),
            shaped(NF, 8, CY),
            shaped(ROWS, 128),
        ),
        in_specs=[VM, VM, SM],
        out_specs=(VM,) * 7,
        compiler_params=SMALL,
        cost_estimate=pl.CostEstimate(flops=20_000_000, bytes_accessed=5 * MIB, transcendentals=0),
        name="split_matrices",
    )(ginv_x, ginv_y, beta_x)


def forcing_kernel(
    fields, q_cat, x_inner, x_outer, y_inner, y_outer, gx_rows, coefs,
    forcing, message,
    band_y, band_x, halo_rows, halo_cols, turned,
):
    both = band((CY, CY), 0, 0)
    band_y[0:CY, :] = both
    band_y[CY:, :] = both
    for r in range(STRIPS):
        band_x[r] = band((CHUNK, WINDOW), r * CHUNK - BASES[r], 1)
    halo_rows[...] = jnp.zeros_like(halo_rows)
    turned[...] = jnp.zeros_like(turned)
    x_odd, y_odd = odd_blocks()
    above = [jnp.where(x_odd, x_inner[c], x_outer[c]) for c in range(3)]
    below = [jnp.where(x_odd, x_outer[c], x_inner[c]) for c in range(3)]
    for j, value in enumerate(halo_sums(above, below)):
        for k in range(ROWS):
            if j < 3:
                halo_rows[k, j : j + 1, :] = value[k : k + 1, :]
            else:
                halo_rows[k, j + 10 : j + 11, :] = value[k : k + 1, :]
    before = [jnp.where(y_odd, y_inner[c], y_outer[c]) for c in range(3)]
    behind = [jnp.where(y_odd, y_outer[c], y_inner[c]) for c in range(3)]
    for j, value in enumerate(halo_sums(before, behind)):
        for t in range(STRIPS):
            turned[t, pl.ds(j if j < 3 else j + 2, ROWS, stride=8), :] = value[:, t * 128 : (t + 1) * 128]
    for t in range(STRIPS):
        halo_cols[t * 128 : (t + 1) * 128, :] = jnp.transpose(turned[t])
    message[:, 2 * CY :] = coefs[...]

    def force(z, f, r):
        at = slice(r * CHUNK, (r + 1) * CHUNK)
        k = f * NZ + z
        window = slice(BASES[r], BASES[r] + WINDOW)
        dx = dot(band_x[r], q_cat[k, window, 0:CY]) + dot(band_x[r], q_cat[k, window, CY:])
        dy = dot(q_cat[k, at, :], band_y[...])
        if r == 0:
            dx = jnp.concatenate([dx[0:8] + halo_rows[k, 0:8], dx[8:]], axis=0)
        if r == STRIPS - 1:
            dx = jnp.concatenate([dx[: CHUNK - 8], dx[CHUNK - 8 :] + halo_rows[k, 8:16]], axis=0)
        spot = lax.broadcasted_iota(jnp.int32, (CHUNK, 128), 1)
        side = halo_cols[at, :]
        left = jnp.where(spot < 3, pltpu.roll(side, lax.rem(128 - 8 * k, 128), 1), 0.0)
        right = jnp.where(spot >= 125, pltpu.roll(side, lax.rem(248 - 8 * k, 128), 1), 0.0)
        dy = dy + jnp.concatenate([left, right], axis=1)
        rise = fields[f, lax.rem(z + 1, NZ), at, :] - fields[f, lax.rem(z + NZ - 1, NZ), at, :]
        value = fields[f, z, at, :] - (
            (ADVECT / 60.0) * (fields[1, z, at, :] * dx + fields[2, z, at, :] * dy)
            + (0.5 * ADVECT) * (fields[3, z, at, :] * rise)
        )
        if f == 3:
            value = value + BUOY * fields[0, z, at, :]
        high, low = halves(value)
        forcing[k, at, :] = high
        forcing[k, CX + r * CHUNK : CX + (r + 1) * CHUNK, :] = low

    def contract(z, f):
        k = f * NZ + z
        by_high = dot(gx_rows[f], forcing[k, 0:CX, :])
        by_low = dot(gx_rows[f], forcing[k, CX:, :])
        message[pl.ds(k, 1), 0:CY] = by_high[0:1] + by_high[2:3] + by_low[0:1]
        message[pl.ds(k, 1), CY : 2 * CY] = by_high[1:2] + by_high[3:4] + by_low[1:2]

    def step(z, carry):
        for f in range(NF):
            for r in range(STRIPS):
                force(z, f, r)
            if f > 0:
                contract(z, f - 1)
        contract(z, NF - 1)
        return carry

    lax.fori_loop(0, NZ, step, 0)


def force_all(fields, q_cat, received, gx_rows, coefs):
    return pl.pallas_call(
        forcing_kernel,
        out_shape=(packed(ROWS, 2 * CX, CY), shaped(ROWS, 2 * CY + 128)),
        in_specs=[VM] * 8,
        out_specs=(VM,) * 2,
        scratch_shapes=[
            pltpu.VMEM((2 * CY, CY), BF16),
            pltpu.VMEM((STRIPS, CHUNK, WINDOW), BF16),
            pltpu.VMEM((ROWS, 16, CY), F32),
            pltpu.VMEM((CX, 128), F32),
            pltpu.VMEM((CX // 128, 128, 128), F32),
        ],
        compiler_params=pltpu.CompilerParams(vmem_limit_bytes=8 * MIB),
        cost_estimate=pl.CostEstimate(flops=4_000_000_000, bytes_accessed=16 * MIB, transcendentals=0),
        name="forcing",
    )(fields, q_cat, *received, gx_rows, coefs)


def products_kernel(f, forcing, gx_cat, gy_cat, out, s_0, s_1):
    def solve_x(z, r, s_cat):
        at = slice(r * CHUNK, (r + 1) * CHUNK)
        k = f * NZ + z
        high, low = forcing.at[k, 0:CX, :], forcing.at[k, CX : 2 * CX, :]
        section = dot(gx_cat[f, at, 0:CX], high[...]) + dot(gx_cat[f, at, 0:CX], low[...])
        section = section + dot(gx_cat[f, at, CX:], high[...])
        s_high, s_low = halves(section)
        s_cat[at, 0:CY] = s_high
        s_cat[at, CY:] = s_low

    def solve_y(z, r, s_cat):
        at = slice(r * CHUNK, (r + 1) * CHUNK)
        out[z, at, :] = dot(s_cat[at, :], gy_cat[f, 0 : 2 * CY, :]) + dot(s_cat[at, 0:CY], gy_cat[f, 2 * CY :, :])

    bufs = (s_0, s_1)
    for z in range(NZ + 1):
        for r in range(STRIPS):
            if z < NZ:
                solve_x(z, r, bufs[z % 2])
            if z > 0:
                solve_y(z - 1, r, bufs[(z - 1) % 2])


def products(f, forcing, gx_cat, gy_cat):
    return pl.pallas_call(
        functools.partial(products_kernel, f),
        out_shape=shaped(NZ, CX, CY),
        in_specs=[VM] * 3,
        out_specs=VM,
        scratch_shapes=[pltpu.VMEM((CX, 2 * CY), BF16), pltpu.VMEM((CX, 2 * CY), BF16)],
        compiler_params=pltpu.CompilerParams(vmem_limit_bytes=6 * MIB),
        cost_estimate=pl.CostEstimate(flops=2_400_000_000, bytes_accessed=6 * MIB, transcendentals=0),
        name="block_products",
    )(forcing, gx_cat, gy_cat)


def weight_kernel(forcing, gy_rows, weighted):
    for k in range(ROWS):
        rows = gy_rows[k // NZ]
        by_high = dot_nt(rows, forcing[k, 0:CX, :])
        by_low = dot_nt(rows, forcing[k, CX : 2 * CX, :])
        weighted[0, k : k + 1, :] = by_high[0:1] + by_high[2:3] + by_low[0:1]
        weighted[1, k : k + 1, :] = by_high[1:2] + by_high[3:4] + by_low[1:2]


def weight(forcing, gy_rows):
    return pl.pallas_call(
        weight_kernel,
        out_shape=shaped(2, ROWS, CX),
        in_specs=[VM, VM],
        out_specs=VM,
        compiler_params=SMALL,
        cost_estimate=pl.CostEstimate(flops=500_000_000, bytes_accessed=8 * MIB, transcendentals=0),
        name="weighted_sums",
    )(forcing, gy_rows)


def weigh_kernel(weighted, gx_cat, out):
    high, low = halves(weighted[...].reshape(2 * ROWS, CX))
    owner = lax.rem(lax.broadcasted_iota(jnp.int32, (2 * ROWS, 1), 0), ROWS) // NZ
    total = jnp.zeros((2 * ROWS, CX), F32)
    for f in range(NF):
        value = dot_nt(high, gx_cat[f, :, 0:CX]) + dot_nt(low, gx_cat[f, :, 0:CX]) + dot_nt(high, gx_cat[f, :, CX:])
        total = jnp.where(owner == f, value, total)
    out[...] = total.reshape(2, ROWS, CX)


def weigh(weighted, gx_cat):
    return pl.pallas_call(
        weigh_kernel,
        out_shape=shaped(2, ROWS, CX),
        in_specs=[VM, VM],
        out_specs=VM,
        compiler_params=SMALL,
        cost_estimate=pl.CostEstimate(flops=500_000_000, bytes_accessed=5 * MIB, transcendentals=0),
        name="y_right_side",
    )(weighted, gx_cat)


def merge(side, mine, other, state, width):
    axis, reach = side
    is_right = jnp.broadcast_to(lax.rem(lax.axis_index(axis) // reach, 2), (ROWS, 1)) == 1

    def parts(ref):
        c = 2 * width
        return [
            ref[:, 0:width], ref[:, width:c],
            ref[:, c : c + 1], ref[:, c + 1 : c + 2], ref[:, c + 2 : c + 3], ref[:, c + 3 : c + 4],
        ]

    own, far = parts(mine), parts(other)
    l_first, l_last, l_p, l_s, l_q, l_t = [jnp.where(is_right, b, a) for a, b in zip(own, far)]
    r_first, r_last, r_p, r_s, r_q, r_t = [jnp.where(is_right, a, b) for a, b in zip(own, far)]
    inner = 1.0 / (1.0 - l_t * r_p)
    m_b = (l_last + l_t * r_first) * inner
    m_a = (r_first + r_p * l_last) * inner
    b_from_b, b_from_a = l_q * inner, l_t * r_s * inner
    a_from_b, a_from_a = r_p * l_q * inner, r_s * inner
    group = (
        l_first + l_s * m_a,
        r_last + r_q * m_b,
        l_p + l_s * a_from_b,
        l_s * a_from_a,
        r_q * b_from_b,
        r_t + r_q * b_from_a,
    )
    if state is None:
        prior, later, prior_b, prior_a, later_b, later_a = 0.0, 0.0, 1.0, 0.0, 0.0, 1.0
    else:
        prior, later, prior_b, prior_a, later_b, later_a = parts(state)
    fresh = []
    for base, by_b, by_a in ((prior, prior_b, prior_a), (later, later_b, later_a)):
        fresh.append(
            (
                base + jnp.where(is_right, by_b * m_b, by_a * m_a),
                jnp.where(is_right, by_b * b_from_b, by_b + by_a * a_from_b),
                jnp.where(is_right, by_a + by_b * b_from_a, by_a * a_from_a),
            )
        )
    return group, fresh


def lanes_of(values):
    spot = lax.broadcasted_iota(jnp.int32, (ROWS, 128), 1)
    total = jnp.zeros((ROWS, 128), F32)
    for place, value in enumerate(values):
        total = jnp.where(spot == place, value, total)
    return total


def merge_kernel(side, width, mine, other, *refs):
    state, (group_out, state_out) = (refs[0], refs[1:]) if len(refs) == 3 else (None, refs)
    group, fresh = merge(side, mine, other, state, width)
    group_out[:, 0:width] = group[0]
    group_out[:, width : 2 * width] = group[1]
    group_out[:, 2 * width :] = lanes_of(group[2:])
    state_out[:, 0:width] = fresh[0][0]
    state_out[:, width : 2 * width] = fresh[1][0]
    state_out[:, 2 * width :] = lanes_of((fresh[0][1], fresh[0][2], fresh[1][1], fresh[1][2]))


def merge_step(side, mine, other, state, width):
    carried = [] if state is None else [state]
    return pl.pallas_call(
        functools.partial(merge_kernel, side, width),
        out_shape=(shaped(ROWS, 2 * width + 128),) * 2,
        in_specs=[VM, VM] + [VM] * len(carried),
        out_specs=(VM, VM),
        compiler_params=SMALL,
        cost_estimate=pl.CostEstimate(flops=200_000, bytes_accessed=200_000, transcendentals=0),
        name="merge_groups",
    )(mine, other, *carried)


def exchange(message, axis, width, fillers):
    count = lax.axis_size(axis)
    state = None
    reach = 1
    results = []
    while True:
        other = lax.ppermute(message, axis, [(i, i ^ reach) for i in range(count)])
        filler = fillers.get(reach)
        if filler is not None:
            function, first, *rest = filler
            first, message = lax.optimization_barrier((first, message))
            result = function(first, *rest)
            result, message = lax.optimization_barrier((result, message))
            results.append(result)
        if 2 * reach >= count:
            return ((axis, reach), message, other, state), results
        message, state = merge_step((axis, reach), message, other, state, width)
        reach *= 2


def middle_kernel(side, mine, other, state, y_rhs, edge_x, edge_y, beta_x, beta_y, enter, message):
    group, fresh = merge(side, mine, other, state, CY)
    for f in range(NF):
        s = slice(f * NZ, (f + 1) * NZ)
        for e in range(2):
            enter[e, s, :] = beta_x[f] * fresh[e][0][s, :]
        for e in range(2):
            value = y_rhs[e, s, :]
            for g in range(2):
                scale = jnp.sum(enter[g, s, :] * edge_y[f, 2 + e : 3 + e, :], axis=1, keepdims=True)
                value = value + scale * edge_x[f, g : g + 1, :]
            message[s, e * CX : (e + 1) * CX] = value
        message[s, 2 * CX :] = fill_coefs(
            beta_y[f],
            edge_y[f, 0:1, 0:1],
            edge_y[f, 1:2, 0:1],
            edge_y[f, 0:1, CY - 1 : CY],
            edge_y[f, 1:2, CY - 1 : CY],
        )


def middle(last, y_rhs, edge_x, edge_y, beta_x, beta_y):
    return pl.pallas_call(
        functools.partial(middle_kernel, last[0]),
        out_shape=(shaped(2, ROWS, CY), shaped(ROWS, 2 * CX + 128)),
        in_specs=[VM] * 6 + [SM, SM],
        out_specs=(VM, VM),
        compiler_params=SMALL,
        cost_estimate=pl.CostEstimate(flops=500_000, bytes_accessed=500_000, transcendentals=0),
        name="between_interfaces",
    )(*last[1:], y_rhs, edge_x, edge_y, beta_x, beta_y)


def rows_kernel(enter, ginv_y, edge_y, out, spread):
    high, low = halves(enter[...].reshape(2 * ROWS, CY))
    spot = lax.broadcasted_iota(jnp.int32, (16, 1), 0)
    for f in range(NF):
        g_high, g_low = halves(ginv_y[f])
        spread[...] = dot_nt(high, g_high) + dot_nt(low, g_high) + dot_nt(high, g_low)
        for z in range(NZ):
            k = f * NZ + z
            value = jnp.where(spot == z, edge_y[f, 0:1, :], 0.0) + jnp.where(spot == NZ + z, edge_y[f, 1:2, :], 0.0)
            value = value + jnp.where(spot == 8, spread[k : k + 1, :], 0.0)
            value = value + jnp.where(spot == 9, spread[ROWS + k : ROWS + k + 1, :], 0.0)
            v_high, v_low = halves(value)
            out[k, 0:16, :] = v_high
            out[k, 16:32, :] = v_high
            out[k, 32:48, :] = v_low
            out[k, 48:, :] = jnp.zeros((80, CY), BF16)


def row_products(enter, ginv_y, edge_y):
    return pl.pallas_call(
        rows_kernel,
        out_shape=packed(ROWS, 128, CY),
        in_specs=[VM, VM, VM],
        out_specs=VM,
        scratch_shapes=[pltpu.VMEM((2 * ROWS, CY), F32)],
        compiler_params=SMALL,
        cost_estimate=pl.CostEstimate(flops=300_000_000, bytes_accessed=2 * MIB, transcendentals=0),
        name="row_products",
    )(enter, ginv_y, edge_y)


def update_kernel(side, mine, other, state, base_0, base_1, base_2, base_3, wide, edge_x, beta_y, out, tall, slim, done, sems):
    group, fresh = merge(side, mine, other, state, CX)
    for f in range(NF):
        s = slice(f * NZ, (f + 1) * NZ)
        value = jnp.concatenate([beta_y[f] * fresh[e][0][s, :] for e in range(2)], axis=0)
        value = jnp.concatenate([value, edge_x[f, 0:8, :]], axis=0)
        high = value.astype(BF16).astype(F32)
        tall[0:16, :] = high
        tall[16:32, :] = (value - high).astype(BF16).astype(F32)
        tall[32:48, :] = high
        tall[48:, :] = jnp.zeros((80, CX), F32)
        for t in range(CX // 128):
            slim[f, t * 128 : (t + 1) * 128, :] = jnp.transpose(tall[:, t * 128 : (t + 1) * 128]).astype(BF16)
    for f, base in enumerate((base_0, base_1, base_2, base_3)):
        for z in range(NZ):
            k = f * NZ + z
            for r in range(STRIPS):
                at = slice(r * CHUNK, (r + 1) * CHUNK)
                done[f, z, at, :] = base[z, at, :] + dot(slim[f, at, :], wide[k])
            pltpu.make_async_copy(done.at[f, z], out.at[f, z], sems.at[k]).start()
    for k in range(ROWS):
        pltpu.make_async_copy(done.at[k // NZ, k % NZ], out.at[k // NZ, k % NZ], sems.at[k]).wait()


def update(last, base, wide, edge_x, beta_y):
    return pl.pallas_call(
        functools.partial(update_kernel, last[0]),
        out_shape=shaped(NF, NZ, CX, CY),
        in_specs=[VM] * 9 + [SM],
        out_specs=HB,
        scratch_shapes=[
            pltpu.VMEM((128, CX), F32),
            pltpu.VMEM((NF, CX, 128), BF16),
            pltpu.VMEM((NF, NZ, CX, CY), F32),
            pltpu.SemaphoreType.DMA((ROWS,)),
        ],
        compiler_params=pltpu.CompilerParams(vmem_limit_bytes=12 * MIB),
        cost_estimate=pl.CostEstimate(flops=200_000_000, bytes_accessed=17 * MIB, transcendentals=0),
        name="update_result",
    )(*last[1:], *base, wide, edge_x, beta_y)


def swap_pairs(value, axis, inner):
    count = lax.axis_size(axis)
    pairs = []
    for i in range(0 if inner else 1, count - 1, 2):
        pairs += [(i, i + 1), (i + 1, i)]
    return lax.ppermute(value, axis, pairs)


def local(fields, ginv_x, ginv_y, coupling_x, coupling_y):
    fields, q_cat, x_inner, x_outer, y_inner, y_outer = pack(fields)
    received = (
        swap_pairs(x_inner, "gx", True),
        swap_pairs(x_outer, "gx", False),
        swap_pairs(y_inner, "gy", True),
        swap_pairs(y_outer, "gy", False),
    )
    gx_cat, gy_cat, gx_rows, gy_rows, edge_x, edge_y, coefs = prep(ginv_x, ginv_y, coupling_x)
    forcing, message = force_all(fields, q_cat, received, gx_rows, coefs)

    def product(f):
        return lambda first, gx, gy: products(f, first, gx, gy), forcing, gx_cat, gy_cat

    sums = []

    def sum_up(rows):
        sums.append(weight(forcing, rows))
        return sums[0]

    def multiply(matrices):
        return weigh(sums[0], matrices)

    last_x, (_, y_rhs) = exchange(message, "gx", CY, {2: (sum_up, gy_rows), 4: (multiply, gx_cat)})
    enter, message_y = middle(last_x, y_rhs, edge_x, edge_y, coupling_x, coupling_y)

    def last_work(first):
        cells, matrices = first
        return products(3, cells, gx_cat, gy_cat), row_products(enter, matrices, edge_y)

    fillers = {1: product(0), 2: product(1), 4: product(2), 8: (last_work, (forcing, ginv_y))}
    last_y, (base_0, base_1, base_2, (base_3, wide)) = exchange(message_y, "gy", CX, fillers)
    return update(last_y, (base_0, base_1, base_2, base_3), wide, edge_x, coupling_y)


def solution(mesh):
    in_specs = (P(None, None, "gx", "gy"), P(None, "gx", None), P(None, "gy", None), P(), P())
    out_specs = P(None, None, "gx", "gy")
    return jax.shard_map(local, mesh=mesh, in_specs=in_specs, out_specs=out_specs, check_vma=False)
```

```python
import functools

import jax
import jax.numpy as jnp
from jax import lax
from jax.experimental import pallas as pl
from jax.experimental.pallas import tpu as pltpu
from jax.sharding import PartitionSpec as P

F32 = jnp.float32
BF16 = jnp.bfloat16
BAND = (45.0, -9.0, 1.0)
ADVECT = 0.3
BUOY = 0.5
CX = 512
CY = 256
NF = 4
NZ = 4
ROWS = NF * NZ
MIB = 1024 * 1024

VM = pl.BlockSpec(memory_space=pltpu.VMEM)
SM = pl.BlockSpec(memory_space=pltpu.SMEM)
HB = pl.BlockSpec(memory_space=pltpu.HBM)
SMALL = pltpu.CompilerParams(vmem_limit_bytes=4 * MIB)


def shaped(*dims):
    return jax.ShapeDtypeStruct(dims, F32)


def packed(*dims):
    return jax.ShapeDtypeStruct(dims, BF16)


def halves(value):
    high = value.astype(BF16)
    return high, (value - high.astype(F32)).astype(BF16)


def dot(left, right):
    return lax.dot_general(left, right, (((1,), (0,)), ((), ())), preferred_element_type=F32)


def dot_nt(left, right):
    return lax.dot_general(left, right, (((1,), (1,)), ((), ())), preferred_element_type=F32)


def dot_tn(left, right):
    return lax.dot_general(left, right, (((0,), (0,)), ((), ())), preferred_element_type=F32)


def odd_blocks():
    return [lax.rem(lax.axis_index(axis), 2) == 1 for axis in ("gx", "gy")]


def pack_kernel(fields, planes, q_cat, x_inner, x_outer, y_inner, y_outer, lanes, turned, sems):
    groups = [(f, z) for f in range(NF) for z in (0, 2)]
    copies = [
        pltpu.make_async_copy(fields.at[f, z : z + 2], planes.at[f, z : z + 2], sems.at[g])
        for g, (f, z) in enumerate(groups)
    ]
    for copy in copies:
        copy.start()
    x_odd, y_odd = odd_blocks()
    step = 64
    for g, (f, start) in enumerate(groups):
        copies[g].wait()

        def chunk(r, carry, f=f, start=start, g=g):
            at = pl.ds(pl.multiple_of(r * step, step), step)
            spot = lax.broadcasted_iota(jnp.int32, (step, 128), 1)
            total = jnp.zeros((step, 128), F32) if g == 0 else lanes[at, :]
            for z in (start, start + 1):
                k = f * NZ + z
                value = planes[f, z, at, :]
                ends = jnp.where(spot >= 125, value[:, 128:256], 0.0)
                ends = jnp.where(spot < 3, value[:, 0:128], ends)
                total = total + pltpu.roll(ends, 8 * k + 3, 1)
                high, low = halves(value)
                q_cat[k, at, 0:CY] = high
                q_cat[k, at, CY:] = low
            lanes[at, :] = total
            return carry

        lax.fori_loop(0, CX // step, chunk, 0, unroll=True)
        for z in (start, start + 1):
            k = f * NZ + z
            for c in range(3):
                top = planes[f, z, c : c + 1, :]
                bottom = planes[f, z, CX - 3 + c : CX - 2 + c, :]
                x_inner[c, k : k + 1, :] = jnp.where(x_odd, top, bottom)
                x_outer[c, k : k + 1, :] = jnp.where(x_odd, bottom, top)
    for t in range(CX // 128):
        part = slice(t * 128, (t + 1) * 128)
        turned[t] = jnp.transpose(lanes[part, :])
        for c in range(3):
            right = turned[t, pl.ds(c, ROWS, stride=8), :]
            left = turned[t, pl.ds(3 + c, ROWS, stride=8), :]
            y_inner[c, :, part] = jnp.where(y_odd, left, right)
            y_outer[c, :, part] = jnp.where(y_odd, right, left)


def pack(fields):
    return pl.pallas_call(
        pack_kernel,
        out_shape=(
            shaped(NF, NZ, CX, CY),
            packed(ROWS, CX, 2 * CY),
            shaped(3, ROWS, CY),
            shaped(3, ROWS, CY),
            shaped(3, ROWS, CX),
            shaped(3, ROWS, CX),
        ),
        in_specs=[HB],
        out_specs=(VM,) * 6,
        scratch_shapes=[
            pltpu.VMEM((CX, 128), F32),
            pltpu.VMEM((CX // 128, 128, 128), F32),
            pltpu.SemaphoreType.DMA((2 * NF,)),
        ],
        compiler_params=pltpu.CompilerParams(vmem_limit_bytes=35 * MIB),
        cost_estimate=pl.CostEstimate(flops=10_000_000, bytes_accessed=9 * MIB, transcendentals=0),
        name="pack_edges",
    )(fields)


WINDOW = 256
CHUNK = 128
STRIPS = CX // CHUNK
BASES = (0, 64, 192, 256)


def band(shape, offset, along):
    gap = lax.broadcasted_iota(jnp.int32, shape, along) - lax.broadcasted_iota(jnp.int32, shape, 1 - along)
    gap = gap - offset
    total = jnp.zeros(shape, F32)
    for reach, weight in zip((1, 2, 3), BAND):
        total = jnp.where(gap == reach, weight, total)
        total = jnp.where(gap == -reach, -weight, total)
    return total.astype(BF16)


def halo_sums(before, after):
    sums = []
    for j in range(3):
        sums.append(sum(-BAND[o - 1] * before[3 + j - o] for o in range(j + 1, 4)))
    for j in range(3):
        sums.append(sum(BAND[o - 1] * after[j + o - 3] for o in range(3 - j, 4)))
    return sums


def fill_coefs(beta, first_first, first_last, last_first, last_last):
    spot = lax.broadcasted_iota(jnp.int32, (NZ, 128), 1)
    values = jnp.where(
        spot == 0,
        first_first,
        jnp.where(spot == 1, first_last, jnp.where(spot == 2, last_first, jnp.where(spot == 3, last_last, 0.0))),
    )
    return beta * values


def prep_kernel(gx, gy, beta_x, gx_cat, gy_cat, gx_rows, gy_rows, edge_x, edge_y, coefs):
    gx_rows[...] = jnp.zeros_like(gx_rows)
    edge_x[...] = jnp.zeros_like(edge_x)
    gy_rows[...] = jnp.zeros_like(gy_rows)
    tile = 16
    spot = lax.broadcasted_iota(jnp.int32, (tile, 1), 0)

    def ends(first, last):
        f_high, f_low = halves(first)
        l_high, l_low = halves(last)
        parts = [value.astype(F32) for value in (f_high, l_high, f_low, l_low)]
        total = jnp.zeros((tile, first.shape[1]), F32)
        for place, value in enumerate(parts):
            total = jnp.where(spot == place, value, total)
        return total.astype(BF16)

    for f in range(NF):
        turned_g = jnp.transpose(gy[f])
        high, low = halves(turned_g)
        gy_cat[f, 0:CY, :] = high
        gy_cat[f, CY : 2 * CY, :] = high
        gy_cat[f, 2 * CY :, :] = low
        edge_y[f, 0:1, :] = turned_g[0:1]
        edge_y[f, 1:2, :] = turned_g[CY - 1 : CY]
        edge_y[f, 2:3, :] = gy[f, 0:1, :]
        edge_y[f, 3:4, :] = gy[f, CY - 1 : CY, :]
        gy_rows[f] = ends(gy[f, 0:1, :], gy[f, CY - 1 : CY, :])
        gx_rows[f] = ends(gx[f, 0:1, :], gx[f, CX - 1 : CX, :])

        def split(r, carry, f=f):
            at = pl.ds(pl.multiple_of(r * CHUNK, CHUNK), CHUNK)
            high, low = halves(gx[f, at, :])
            gx_cat[f, at, 0:CX] = high
            gx_cat[f, at, CX:] = low
            return carry

        lax.fori_loop(0, CX // CHUNK, split, 0)
        edge_x[f, 0:1, :] = jnp.transpose(gx[f, :, 0:128])[0:1]
        edge_x[f, 1:2, :] = jnp.transpose(gx[f, :, CX - 128 : CX])[127:128]
        coefs[f * NZ : (f + 1) * NZ, :] = fill_coefs(
            beta_x[f],
            gx[f, 0:1, 0:1],
            gx[f, 0:1, CX - 1 : CX],
            gx[f, CX - 1 : CX, 0:1],
            gx[f, CX - 1 : CX, CX - 1 : CX],
        )


def prep(ginv_x, ginv_y, beta_x):
    return pl.pallas_call(
        prep_kernel,
        out_shape=(
            packed(NF, CX, 2 * CX),
            packed(NF, 3 * CY, CY),
            packed(NF, 16, CX),
            packed(NF, 16, CY),
            shaped(NF, 8, CX),
            shaped(NF, 8, CY),
            shaped(ROWS, 128),
        ),
        in_specs=[VM, VM, SM],
        out_specs=(VM,) * 7,
        compiler_params=SMALL,
        cost_estimate=pl.CostEstimate(flops=20_000_000, bytes_accessed=5 * MIB, transcendentals=0),
        name="split_matrices",
    )(ginv_x, ginv_y, beta_x)


def forcing_kernel(
    fields, q_cat, x_inner, x_outer, y_inner, y_outer, gx_rows, coefs,
    forcing, message,
    band_y, band_x, halo_rows, halo_cols, turned,
):
    both = band((CY, CY), 0, 0)
    band_y[0:CY, :] = both
    band_y[CY:, :] = both
    for r in range(STRIPS):
        band_x[r] = band((CHUNK, WINDOW), r * CHUNK - BASES[r], 1)
    halo_rows[...] = jnp.zeros_like(halo_rows)
    turned[...] = jnp.zeros_like(turned)
    x_odd, y_odd = odd_blocks()
    above = [jnp.where(x_odd, x_inner[c], x_outer[c]) for c in range(3)]
    below = [jnp.where(x_odd, x_outer[c], x_inner[c]) for c in range(3)]
    for j, value in enumerate(halo_sums(above, below)):
        for k in range(ROWS):
            if j < 3:
                halo_rows[k, j : j + 1, :] = value[k : k + 1, :]
            else:
                halo_rows[k, j + 10 : j + 11, :] = value[k : k + 1, :]
    before = [jnp.where(y_odd, y_inner[c], y_outer[c]) for c in range(3)]
    behind = [jnp.where(y_odd, y_outer[c], y_inner[c]) for c in range(3)]
    for j, value in enumerate(halo_sums(before, behind)):
        for t in range(STRIPS):
            turned[t, pl.ds(j if j < 3 else j + 2, ROWS, stride=8), :] = value[:, t * 128 : (t + 1) * 128]
    for t in range(STRIPS):
        halo_cols[t * 128 : (t + 1) * 128, :] = jnp.transpose(turned[t])
    message[:, 2 * CY :] = coefs[...]

    def force(z, f, r):
        at = slice(r * CHUNK, (r + 1) * CHUNK)
        k = f * NZ + z
        window = slice(BASES[r], BASES[r] + WINDOW)
        dx = dot(band_x[r], q_cat[k, window, 0:CY]) + dot(band_x[r], q_cat[k, window, CY:])
        dy = dot(q_cat[k, at, :], band_y[...])
        if r == 0:
            dx = jnp.concatenate([dx[0:8] + halo_rows[k, 0:8], dx[8:]], axis=0)
        if r == STRIPS - 1:
            dx = jnp.concatenate([dx[: CHUNK - 8], dx[CHUNK - 8 :] + halo_rows[k, 8:16]], axis=0)
        spot = lax.broadcasted_iota(jnp.int32, (CHUNK, 128), 1)
        side = halo_cols[at, :]
        left = jnp.where(spot < 3, pltpu.roll(side, lax.rem(128 - 8 * k, 128), 1), 0.0)
        right = jnp.where(spot >= 125, pltpu.roll(side, lax.rem(248 - 8 * k, 128), 1), 0.0)
        dy = dy + jnp.concatenate([left, right], axis=1)
        rise = fields[f, lax.rem(z + 1, NZ), at, :] - fields[f, lax.rem(z + NZ - 1, NZ), at, :]
        value = fields[f, z, at, :] - (
            (ADVECT / 60.0) * (fields[1, z, at, :] * dx + fields[2, z, at, :] * dy)
            + (0.5 * ADVECT) * (fields[3, z, at, :] * rise)
        )
        if f == 3:
            value = value + BUOY * fields[0, z, at, :]
        high, low = halves(value)
        forcing[k, at, :] = high
        forcing[k, CX + r * CHUNK : CX + (r + 1) * CHUNK, :] = low

    def contract(z, f):
        k = f * NZ + z
        by_high = dot(gx_rows[f], forcing[k, 0:CX, :])
        by_low = dot(gx_rows[f], forcing[k, CX:, :])
        message[pl.ds(k, 1), 0:CY] = by_high[0:1] + by_high[2:3] + by_low[0:1]
        message[pl.ds(k, 1), CY : 2 * CY] = by_high[1:2] + by_high[3:4] + by_low[1:2]

    def step(z, carry):
        for f in range(NF):
            for r in range(STRIPS):
                force(z, f, r)
            if f > 0:
                contract(z, f - 1)
        contract(z, NF - 1)
        return carry

    lax.fori_loop(0, NZ, step, 0)


def force_all(fields, q_cat, received, gx_rows, coefs):
    return pl.pallas_call(
        forcing_kernel,
        out_shape=(packed(ROWS, 2 * CX, CY), shaped(ROWS, 2 * CY + 128)),
        in_specs=[VM] * 8,
        out_specs=(VM,) * 2,
        scratch_shapes=[
            pltpu.VMEM((2 * CY, CY), BF16),
            pltpu.VMEM((STRIPS, CHUNK, WINDOW), BF16),
            pltpu.VMEM((ROWS, 16, CY), F32),
            pltpu.VMEM((CX, 128), F32),
            pltpu.VMEM((CX // 128, 128, 128), F32),
        ],
        compiler_params=pltpu.CompilerParams(vmem_limit_bytes=8 * MIB),
        cost_estimate=pl.CostEstimate(flops=4_000_000_000, bytes_accessed=16 * MIB, transcendentals=0),
        name="forcing",
    )(fields, q_cat, *received, gx_rows, coefs)


def products_kernel(f, forcing, gx_cat, gy_cat, out, s_0, s_1):
    def solve_x(z, r, s_cat):
        at = slice(r * CHUNK, (r + 1) * CHUNK)
        k = f * NZ + z
        high, low = forcing.at[k, 0:CX, :], forcing.at[k, CX : 2 * CX, :]
        section = dot(gx_cat[f, at, 0:CX], high[...]) + dot(gx_cat[f, at, 0:CX], low[...])
        section = section + dot(gx_cat[f, at, CX:], high[...])
        s_high, s_low = halves(section)
        s_cat[at, 0:CY] = s_high
        s_cat[at, CY:] = s_low

    def solve_y(z, r, s_cat):
        at = slice(r * CHUNK, (r + 1) * CHUNK)
        out[z, at, :] = dot(s_cat[at, :], gy_cat[f, 0 : 2 * CY, :]) + dot(s_cat[at, 0:CY], gy_cat[f, 2 * CY :, :])

    bufs = (s_0, s_1)
    for z in range(NZ + 1):
        for r in range(STRIPS):
            if z < NZ:
                solve_x(z, r, bufs[z % 2])
            if z > 0:
                solve_y(z - 1, r, bufs[(z - 1) % 2])


def products(f, forcing, gx_cat, gy_cat):
    return pl.pallas_call(
        functools.partial(products_kernel, f),
        out_shape=shaped(NZ, CX, CY),
        in_specs=[VM] * 3,
        out_specs=VM,
        scratch_shapes=[pltpu.VMEM((CX, 2 * CY), BF16), pltpu.VMEM((CX, 2 * CY), BF16)],
        compiler_params=pltpu.CompilerParams(vmem_limit_bytes=6 * MIB),
        cost_estimate=pl.CostEstimate(flops=2_400_000_000, bytes_accessed=6 * MIB, transcendentals=0),
        name="block_products",
    )(forcing, gx_cat, gy_cat)


def weight_kernel(forcing, gy_rows, weighted):
    for k in range(ROWS):
        rows = gy_rows[k // NZ]
        by_high = dot_nt(rows, forcing[k, 0:CX, :])
        by_low = dot_nt(rows, forcing[k, CX : 2 * CX, :])
        weighted[0, k : k + 1, :] = by_high[0:1] + by_high[2:3] + by_low[0:1]
        weighted[1, k : k + 1, :] = by_high[1:2] + by_high[3:4] + by_low[1:2]


def weight(forcing, gy_rows):
    return pl.pallas_call(
        weight_kernel,
        out_shape=shaped(2, ROWS, CX),
        in_specs=[VM, VM],
        out_specs=VM,
        compiler_params=SMALL,
        cost_estimate=pl.CostEstimate(flops=500_000_000, bytes_accessed=8 * MIB, transcendentals=0),
        name="weighted_sums",
    )(forcing, gy_rows)


def weigh_kernel(weighted, gx_cat, out):
    high, low = halves(weighted[...].reshape(2 * ROWS, CX))
    owner = lax.rem(lax.broadcasted_iota(jnp.int32, (2 * ROWS, 1), 0), ROWS) // NZ
    total = jnp.zeros((2 * ROWS, CX), F32)
    for f in range(NF):
        value = dot_nt(high, gx_cat[f, :, 0:CX]) + dot_nt(low, gx_cat[f, :, 0:CX]) + dot_nt(high, gx_cat[f, :, CX:])
        total = jnp.where(owner == f, value, total)
    out[...] = total.reshape(2, ROWS, CX)


def weigh(weighted, gx_cat):
    return pl.pallas_call(
        weigh_kernel,
        out_shape=shaped(2, ROWS, CX),
        in_specs=[VM, VM],
        out_specs=VM,
        compiler_params=SMALL,
        cost_estimate=pl.CostEstimate(flops=500_000_000, bytes_accessed=5 * MIB, transcendentals=0),
        name="y_right_side",
    )(weighted, gx_cat)


def merge(side, mine, other, state, width):
    axis, reach = side
    is_right = jnp.broadcast_to(lax.rem(lax.axis_index(axis) // reach, 2), (ROWS, 1)) == 1

    def parts(ref):
        c = 2 * width
        return [
            ref[:, 0:width], ref[:, width:c],
            ref[:, c : c + 1], ref[:, c + 1 : c + 2], ref[:, c + 2 : c + 3], ref[:, c + 3 : c + 4],
        ]

    own, far = parts(mine), parts(other)
    l_first, l_last, l_p, l_s, l_q, l_t = [jnp.where(is_right, b, a) for a, b in zip(own, far)]
    r_first, r_last, r_p, r_s, r_q, r_t = [jnp.where(is_right, a, b) for a, b in zip(own, far)]
    inner = 1.0 / (1.0 - l_t * r_p)
    m_b = (l_last + l_t * r_first) * inner
    m_a = (r_first + r_p * l_last) * inner
    b_from_b, b_from_a = l_q * inner, l_t * r_s * inner
    a_from_b, a_from_a = r_p * l_q * inner, r_s * inner
    group = (
        l_first + l_s * m_a,
        r_last + r_q * m_b,
        l_p + l_s * a_from_b,
        l_s * a_from_a,
        r_q * b_from_b,
        r_t + r_q * b_from_a,
    )
    if state is None:
        prior, later, prior_b, prior_a, later_b, later_a = 0.0, 0.0, 1.0, 0.0, 0.0, 1.0
    else:
        prior, later, prior_b, prior_a, later_b, later_a = parts(state)
    fresh = []
    for base, by_b, by_a in ((prior, prior_b, prior_a), (later, later_b, later_a)):
        fresh.append(
            (
                base + jnp.where(is_right, by_b * m_b, by_a * m_a),
                jnp.where(is_right, by_b * b_from_b, by_b + by_a * a_from_b),
                jnp.where(is_right, by_a + by_b * b_from_a, by_a * a_from_a),
            )
        )
    return group, fresh


def last_merge(side, mine, other, state, width):
    axis, reach = side
    is_right = jnp.broadcast_to(lax.rem(lax.axis_index(axis) // reach, 2), (ROWS, 1)) == 1
    own, own_coef = mine[:, 0:width], mine[:, width : width + 1]
    far, far_coef = other[:, 0:width], other[:, width : width + 1]
    between = (far + far_coef * own) * (1.0 / (1.0 - own_coef * far_coef))
    c = 2 * width
    by_prior = jnp.where(is_right, state[:, c : c + 1], state[:, c + 1 : c + 2])
    by_later = jnp.where(is_right, state[:, c + 2 : c + 3], state[:, c + 3 : c + 4])
    return state[:, 0:width] + by_prior * between, state[:, width:c] + by_later * between


def lanes_of(values):
    spot = lax.broadcasted_iota(jnp.int32, (ROWS, 128), 1)
    total = jnp.zeros((ROWS, 128), F32)
    for place, value in enumerate(values):
        total = jnp.where(spot == place, value, total)
    return total


def merge_kernel(side, width, final, mine, other, *refs):
    state, (group_out, state_out) = (refs[0], refs[1:]) if len(refs) == 3 else (None, refs)
    group, fresh = merge(side, mine, other, state, width)
    if final:
        axis, reach = side
        is_right = jnp.broadcast_to(lax.rem(lax.axis_index(axis) // (2 * reach), 2), (ROWS, 1)) == 1
        group_out[:, 0:width] = jnp.where(is_right, group[0], group[1])
        group_out[:, width:] = lanes_of((jnp.where(is_right, group[2], group[5]),))
    else:
        group_out[:, 0:width] = group[0]
        group_out[:, width : 2 * width] = group[1]
        group_out[:, 2 * width :] = lanes_of(group[2:])
    state_out[:, 0:width] = fresh[0][0]
    state_out[:, width : 2 * width] = fresh[1][0]
    state_out[:, 2 * width :] = lanes_of((fresh[0][1], fresh[0][2], fresh[1][1], fresh[1][2]))


def merge_step(side, mine, other, state, width, final):
    carried = [] if state is None else [state]
    return pl.pallas_call(
        functools.partial(merge_kernel, side, width, final),
        out_shape=(shaped(ROWS, (1 if final else 2) * width + 128), shaped(ROWS, 2 * width + 128)),
        in_specs=[VM, VM] + [VM] * len(carried),
        out_specs=(VM, VM),
        compiler_params=SMALL,
        cost_estimate=pl.CostEstimate(flops=200_000, bytes_accessed=200_000, transcendentals=0),
        name="merge_groups",
    )(mine, other, *carried)


PARTNERS = {"gx": {1: 1, 2: 2, 4: 6}, "gy": {1: 1, 2: 3, 4: 4, 8: 12}}


def exchange(message, axis, width, fillers):
    count = lax.axis_size(axis)
    state = None
    reach = 1
    results = []
    while True:
        mask = PARTNERS[axis].get(reach, reach)
        other = lax.ppermute(message, axis, [(i, i ^ mask) for i in range(count)])
        filler = fillers.get(reach)
        if filler is not None:
            function, first, *rest = filler
            first, message = lax.optimization_barrier((first, message))
            result = function(first, *rest)
            result, message = lax.optimization_barrier((result, message))
            results.append(result)
        if 2 * reach >= count:
            return ((axis, reach), message, other, state), results
        message, state = merge_step((axis, reach), message, other, state, width, 4 * reach >= count)
        reach *= 2


def middle_kernel(side, mine, other, state, y_rhs, edge_x, edge_y, beta_x, beta_y, enter, message):
    fresh = last_merge(side, mine, other, state, CY)
    for f in range(NF):
        s = slice(f * NZ, (f + 1) * NZ)
        for e in range(2):
            enter[e, s, :] = beta_x[f] * fresh[e][s, :]
        for e in range(2):
            value = y_rhs[e, s, :]
            for g in range(2):
                scale = jnp.sum(enter[g, s, :] * edge_y[f, 2 + e : 3 + e, :], axis=1, keepdims=True)
                value = value + scale * edge_x[f, g : g + 1, :]
            message[s, e * CX : (e + 1) * CX] = value
        message[s, 2 * CX :] = fill_coefs(
            beta_y[f],
            edge_y[f, 0:1, 0:1],
            edge_y[f, 1:2, 0:1],
            edge_y[f, 0:1, CY - 1 : CY],
            edge_y[f, 1:2, CY - 1 : CY],
        )


def middle(last, y_rhs, edge_x, edge_y, beta_x, beta_y):
    return pl.pallas_call(
        functools.partial(middle_kernel, last[0]),
        out_shape=(shaped(2, ROWS, CY), shaped(ROWS, 2 * CX + 128)),
        in_specs=[VM] * 6 + [SM, SM],
        out_specs=(VM, VM),
        compiler_params=SMALL,
        cost_estimate=pl.CostEstimate(flops=500_000, bytes_accessed=500_000, transcendentals=0),
        name="between_interfaces",
    )(*last[1:], y_rhs, edge_x, edge_y, beta_x, beta_y)


def rows_kernel(enter, ginv_y, edge_y, out, spread):
    high, low = halves(enter[...].reshape(2 * ROWS, CY))
    spot = lax.broadcasted_iota(jnp.int32, (16, 1), 0)
    for f in range(NF):
        g_high, g_low = halves(ginv_y[f])
        spread[...] = dot_nt(high, g_high) + dot_nt(low, g_high) + dot_nt(high, g_low)
        for z in range(NZ):
            k = f * NZ + z
            value = jnp.where(spot == z, edge_y[f, 0:1, :], 0.0) + jnp.where(spot == NZ + z, edge_y[f, 1:2, :], 0.0)
            value = value + jnp.where(spot == 8, spread[k : k + 1, :], 0.0)
            value = value + jnp.where(spot == 9, spread[ROWS + k : ROWS + k + 1, :], 0.0)
            v_high, v_low = halves(value)
            out[k, 0:16, :] = v_high
            out[k, 16:32, :] = v_high
            out[k, 32:48, :] = v_low
            out[k, 48:, :] = jnp.zeros((80, CY), BF16)


def row_products(enter, ginv_y, edge_y):
    return pl.pallas_call(
        rows_kernel,
        out_shape=packed(ROWS, 128, CY),
        in_specs=[VM, VM, VM],
        out_specs=VM,
        scratch_shapes=[pltpu.VMEM((2 * ROWS, CY), F32)],
        compiler_params=SMALL,
        cost_estimate=pl.CostEstimate(flops=300_000_000, bytes_accessed=2 * MIB, transcendentals=0),
        name="row_products",
    )(enter, ginv_y, edge_y)


def update_kernel(side, mine, other, state, base_0, base_1, base_2, base_3, wide, edge_x, beta_y, out, tall, slim, done, sems):
    fresh = last_merge(side, mine, other, state, CX)
    for f, base in enumerate((base_0, base_1, base_2, base_3)):
        s = slice(f * NZ, (f + 1) * NZ)
        value = jnp.concatenate([beta_y[f] * fresh[e][s, :] for e in range(2)], axis=0)
        value = jnp.concatenate([value, edge_x[f, 0:8, :]], axis=0)
        high = value.astype(BF16).astype(F32)
        tall[0:16, :] = high
        tall[16:32, :] = (value - high).astype(BF16).astype(F32)
        tall[32:48, :] = high
        tall[48:, :] = jnp.zeros((80, CX), F32)
        for t in range(CX // 128):
            slim[f, t * 128 : (t + 1) * 128, :] = jnp.transpose(tall[:, t * 128 : (t + 1) * 128]).astype(BF16)
        for z in range(NZ):
            k = f * NZ + z
            for r in range(STRIPS):
                at = slice(r * CHUNK, (r + 1) * CHUNK)
                done[f, z, at, :] = base[z, at, :] + dot(slim[f, at, :], wide[k])
            pltpu.make_async_copy(done.at[f, z], out.at[f, z], sems.at[k]).start()
    for k in range(ROWS):
        pltpu.make_async_copy(done.at[k // NZ, k % NZ], out.at[k // NZ, k % NZ], sems.at[k]).wait()


def update(last, base, wide, edge_x, beta_y):
    return pl.pallas_call(
        functools.partial(update_kernel, last[0]),
        out_shape=shaped(NF, NZ, CX, CY),
        in_specs=[VM] * 9 + [SM],
        out_specs=HB,
        scratch_shapes=[
            pltpu.VMEM((128, CX), F32),
            pltpu.VMEM((NF, CX, 128), BF16),
            pltpu.VMEM((NF, NZ, CX, CY), F32),
            pltpu.SemaphoreType.DMA((ROWS,)),
        ],
        compiler_params=pltpu.CompilerParams(vmem_limit_bytes=12 * MIB),
        cost_estimate=pl.CostEstimate(flops=200_000_000, bytes_accessed=17 * MIB, transcendentals=0),
        name="update_result",
    )(*last[1:], *base, wide, edge_x, beta_y)


def swap_pairs(value, axis, inner):
    count = lax.axis_size(axis)
    pairs = []
    for i in range(0 if inner else 1, count - 1, 2):
        pairs += [(i, i + 1), (i + 1, i)]
    return lax.ppermute(value, axis, pairs)


def local(fields, ginv_x, ginv_y, coupling_x, coupling_y):
    fields, q_cat, x_inner, x_outer, y_inner, y_outer = pack(fields)
    received = (
        swap_pairs(x_inner, "gx", True),
        swap_pairs(x_outer, "gx", False),
        swap_pairs(y_inner, "gy", True),
        swap_pairs(y_outer, "gy", False),
    )
    gx_cat, gy_cat, gx_rows, gy_rows, edge_x, edge_y, coefs = prep(ginv_x, ginv_y, coupling_x)
    forcing, message = force_all(fields, q_cat, received, gx_rows, coefs)

    def product(f):
        return lambda first, gx, gy: products(f, first, gx, gy), forcing, gx_cat, gy_cat

    sums = []

    def sum_up(rows):
        sums.append(weight(forcing, rows))
        return sums[0]

    def multiply(matrices):
        return weigh(sums[0], matrices)

    last_x, (_, y_rhs) = exchange(message, "gx", CY, {2: (sum_up, gy_rows), 4: (multiply, gx_cat)})
    enter, message_y = middle(last_x, y_rhs, edge_x, edge_y, coupling_x, coupling_y)

    def last_work(first):
        cells, matrices = first
        return products(3, cells, gx_cat, gy_cat), row_products(enter, matrices, edge_y)

    fillers = {1: product(0), 2: product(1), 4: product(2), 8: (last_work, (forcing, ginv_y))}
    last_y, (base_0, base_1, base_2, (base_3, wide)) = exchange(message_y, "gy", CX, fillers)
    return update(last_y, (base_0, base_1, base_2, base_3), wide, edge_x, coupling_y)


def solution(mesh):
    in_specs = (P(None, None, "gx", "gy"), P(None, "gx", None), P(None, "gy", None), P(), P())
    out_specs = P(None, None, "gx", "gy")
    return jax.shard_map(local, mesh=mesh, in_specs=in_specs, out_specs=out_specs, check_vma=False)
```

```python
import functools

import jax
import jax.numpy as jnp
from jax import lax
from jax.experimental import pallas as pl
from jax.experimental.pallas import tpu as pltpu
from jax.sharding import PartitionSpec as P

F32 = jnp.float32
BF16 = jnp.bfloat16
BAND = (45.0, -9.0, 1.0)
ADVECT = 0.3
BUOY = 0.5
CX = 512
CY = 256
NF = 4
NZ = 4
ROWS = NF * NZ
MIB = 1024 * 1024

VM = pl.BlockSpec(memory_space=pltpu.VMEM)
SM = pl.BlockSpec(memory_space=pltpu.SMEM)
HB = pl.BlockSpec(memory_space=pltpu.HBM)
SMALL = pltpu.CompilerParams(vmem_limit_bytes=4 * MIB)


def shaped(*dims):
    return jax.ShapeDtypeStruct(dims, F32)


def packed(*dims):
    return jax.ShapeDtypeStruct(dims, BF16)


def halves(value):
    high = value.astype(BF16)
    return high, (value - high.astype(F32)).astype(BF16)


def dot(left, right):
    return lax.dot_general(left, right, (((1,), (0,)), ((), ())), preferred_element_type=F32)


def dot_nt(left, right):
    return lax.dot_general(left, right, (((1,), (1,)), ((), ())), preferred_element_type=F32)


def dot_tn(left, right):
    return lax.dot_general(left, right, (((0,), (0,)), ((), ())), preferred_element_type=F32)


def odd_blocks():
    return [lax.rem(lax.axis_index(axis), 2) == 1 for axis in ("gx", "gy")]


def pack_kernel(fields, planes, q_cat, x_inner, x_outer, y_inner, y_outer, lanes, turned, sems):
    groups = [(f, z) for f in range(NF) for z in (0, 2)]
    copies = [
        pltpu.make_async_copy(fields.at[f, z : z + 2], planes.at[f, z : z + 2], sems.at[g])
        for g, (f, z) in enumerate(groups)
    ]
    for copy in copies:
        copy.start()
    x_odd, y_odd = odd_blocks()
    step = 64
    for g, (f, start) in enumerate(groups):
        copies[g].wait()

        def chunk(r, carry, f=f, start=start, g=g):
            at = pl.ds(pl.multiple_of(r * step, step), step)
            spot = lax.broadcasted_iota(jnp.int32, (step, 128), 1)
            total = jnp.zeros((step, 128), F32) if g == 0 else lanes[at, :]
            for z in (start, start + 1):
                k = f * NZ + z
                value = planes[f, z, at, :]
                ends = jnp.where(spot >= 125, value[:, 128:256], 0.0)
                ends = jnp.where(spot < 3, value[:, 0:128], ends)
                total = total + pltpu.roll(ends, 8 * k + 3, 1)
                high, low = halves(value)
                q_cat[k, at, 0:CY] = high
                q_cat[k, at, CY:] = low
            lanes[at, :] = total
            return carry

        lax.fori_loop(0, CX // step, chunk, 0, unroll=True)
        for z in (start, start + 1):
            k = f * NZ + z
            for c in range(3):
                top = planes[f, z, c : c + 1, :]
                bottom = planes[f, z, CX - 3 + c : CX - 2 + c, :]
                x_inner[c, k : k + 1, :] = jnp.where(x_odd, top, bottom)
                x_outer[c, k : k + 1, :] = jnp.where(x_odd, bottom, top)
    for t in range(CX // 128):
        part = slice(t * 128, (t + 1) * 128)
        turned[t] = jnp.transpose(lanes[part, :])
        for c in range(3):
            right = turned[t, pl.ds(c, ROWS, stride=8), :]
            left = turned[t, pl.ds(3 + c, ROWS, stride=8), :]
            y_inner[c, :, part] = jnp.where(y_odd, left, right)
            y_outer[c, :, part] = jnp.where(y_odd, right, left)


def pack(fields):
    return pl.pallas_call(
        pack_kernel,
        out_shape=(
            shaped(NF, NZ, CX, CY),
            packed(ROWS, CX, 2 * CY),
            shaped(3, ROWS, CY),
            shaped(3, ROWS, CY),
            shaped(3, ROWS, CX),
            shaped(3, ROWS, CX),
        ),
        in_specs=[HB],
        out_specs=(VM,) * 6,
        scratch_shapes=[
            pltpu.VMEM((CX, 128), F32),
            pltpu.VMEM((CX // 128, 128, 128), F32),
            pltpu.SemaphoreType.DMA((2 * NF,)),
        ],
        compiler_params=pltpu.CompilerParams(vmem_limit_bytes=35 * MIB),
        cost_estimate=pl.CostEstimate(flops=10_000_000, bytes_accessed=9 * MIB, transcendentals=0),
        name="pack_edges",
    )(fields)


WINDOW = 256
CHUNK = 128
STRIPS = CX // CHUNK
BASES = (0, 64, 192, 256)


def band(shape, offset, along):
    gap = lax.broadcasted_iota(jnp.int32, shape, along) - lax.broadcasted_iota(jnp.int32, shape, 1 - along)
    gap = gap - offset
    total = jnp.zeros(shape, F32)
    for reach, weight in zip((1, 2, 3), BAND):
        total = jnp.where(gap == reach, weight, total)
        total = jnp.where(gap == -reach, -weight, total)
    return total.astype(BF16)


def halo_sums(before, after):
    sums = []
    for j in range(3):
        sums.append(sum(-BAND[o - 1] * before[3 + j - o] for o in range(j + 1, 4)))
    for j in range(3):
        sums.append(sum(BAND[o - 1] * after[j + o - 3] for o in range(3 - j, 4)))
    return sums


BETA = 4


def fill_coefs(beta, first_first, first_last, last_first, last_last):
    spot = lax.broadcasted_iota(jnp.int32, (NZ, 128), 1)
    values = jnp.where(
        spot == 0,
        first_first,
        jnp.where(
            spot == 1,
            first_last,
            jnp.where(spot == 2, last_first, jnp.where(spot == 3, last_last, jnp.where(spot == 4, 1.0, 0.0))),
        ),
    )
    return beta * values


def prep_kernel(gx, gy, beta_x, beta_y, gx_cat, gy_cat, gx_rows, gy_rows, edge_x, edge_y, x_ends, y_ends, coefs):
    gx_rows[...] = jnp.zeros_like(gx_rows)
    edge_x[...] = jnp.zeros_like(edge_x)
    gy_rows[...] = jnp.zeros_like(gy_rows)
    tile = 16
    spot = lax.broadcasted_iota(jnp.int32, (tile, 1), 0)

    def ends(first, last):
        f_high, f_low = halves(first)
        l_high, l_low = halves(last)
        parts = [value.astype(F32) for value in (f_high, l_high, f_low, l_low)]
        total = jnp.zeros((tile, first.shape[1]), F32)
        for place, value in enumerate(parts):
            total = jnp.where(spot == place, value, total)
        return total.astype(BF16)

    for f in range(NF):
        turned_g = jnp.transpose(gy[f])
        high, low = halves(turned_g)
        gy_cat[f, 0:CY, :] = high
        gy_cat[f, CY : 2 * CY, :] = high
        gy_cat[f, 2 * CY :, :] = low
        edge_y[f, 0:1, :] = turned_g[0:1]
        edge_y[f, 1:2, :] = turned_g[CY - 1 : CY]
        edge_y[f, 2:3, :] = gy[f, 0:1, :]
        edge_y[f, 3:4, :] = gy[f, CY - 1 : CY, :]
        gy_rows[f] = ends(gy[f, 0:1, :], gy[f, CY - 1 : CY, :])
        gx_rows[f] = ends(gx[f, 0:1, :], gx[f, CX - 1 : CX, :])

        def split(r, carry, f=f):
            at = pl.ds(pl.multiple_of(r * CHUNK, CHUNK), CHUNK)
            high, low = halves(gx[f, at, :])
            gx_cat[f, at, 0:CX] = high
            gx_cat[f, at, CX:] = low
            return carry

        lax.fori_loop(0, CX // CHUNK, split, 0)
        edge_x[f, 0:1, :] = jnp.transpose(gx[f, :, 0:128])[0:1]
        edge_x[f, 1:2, :] = jnp.transpose(gx[f, :, CX - 128 : CX])[127:128]
        s = slice(f * NZ, (f + 1) * NZ)
        for e in range(2):
            x_ends[e, s, :] = jnp.broadcast_to(edge_x[f, e : e + 1, :], (NZ, CX))
            y_ends[e, s, :] = jnp.broadcast_to(edge_y[f, 2 + e : 3 + e, :], (NZ, CY))
        for axis, (g, beta, n) in enumerate(((gx, beta_x, CX), (gy, beta_y, CY))):
            coefs[axis, s, :] = fill_coefs(
                beta[f], g[f, 0:1, 0:1], g[f, 0:1, n - 1 : n], g[f, n - 1 : n, 0:1], g[f, n - 1 : n, n - 1 : n]
            )


def prep(ginv_x, ginv_y, beta_x, beta_y):
    return pl.pallas_call(
        prep_kernel,
        out_shape=(
            packed(NF, CX, 2 * CX),
            packed(NF, 3 * CY, CY),
            packed(NF, 16, CX),
            packed(NF, 16, CY),
            shaped(NF, 8, CX),
            shaped(NF, 8, CY),
            shaped(2, ROWS, CX),
            shaped(2, ROWS, CY),
            shaped(2, ROWS, 128),
        ),
        in_specs=[VM, VM, SM, SM],
        out_specs=(VM,) * 9,
        compiler_params=SMALL,
        cost_estimate=pl.CostEstimate(flops=20_000_000, bytes_accessed=5 * MIB, transcendentals=0),
        name="split_matrices",
    )(ginv_x, ginv_y, beta_x, beta_y)


def forcing_kernel(
    fields, q_cat, x_inner, x_outer, y_inner, y_outer, gx_rows, coefs,
    forcing, message,
    band_y, band_x, halo_rows, halo_cols, turned,
):
    both = band((CY, CY), 0, 0)
    band_y[0:CY, :] = both
    band_y[CY:, :] = both
    for r in range(STRIPS):
        band_x[r] = band((CHUNK, WINDOW), r * CHUNK - BASES[r], 1)
    halo_rows[...] = jnp.zeros_like(halo_rows)
    turned[...] = jnp.zeros_like(turned)
    x_odd, y_odd = odd_blocks()
    above = [jnp.where(x_odd, x_inner[c], x_outer[c]) for c in range(3)]
    below = [jnp.where(x_odd, x_outer[c], x_inner[c]) for c in range(3)]
    for j, value in enumerate(halo_sums(above, below)):
        for k in range(ROWS):
            if j < 3:
                halo_rows[k, j : j + 1, :] = value[k : k + 1, :]
            else:
                halo_rows[k, j + 10 : j + 11, :] = value[k : k + 1, :]
    before = [jnp.where(y_odd, y_inner[c], y_outer[c]) for c in range(3)]
    behind = [jnp.where(y_odd, y_outer[c], y_inner[c]) for c in range(3)]
    for j, value in enumerate(halo_sums(before, behind)):
        for t in range(STRIPS):
            turned[t, pl.ds(j if j < 3 else j + 2, ROWS, stride=8), :] = value[:, t * 128 : (t + 1) * 128]
    for t in range(STRIPS):
        halo_cols[t * 128 : (t + 1) * 128, :] = jnp.transpose(turned[t])
    message[:, 2 * CY :] = coefs[0]

    def force(z, f, r):
        at = slice(r * CHUNK, (r + 1) * CHUNK)
        k = f * NZ + z
        window = slice(BASES[r], BASES[r] + WINDOW)
        dx = dot(band_x[r], q_cat[k, window, 0:CY]) + dot(band_x[r], q_cat[k, window, CY:])
        dy = dot(q_cat[k, at, :], band_y[...])
        if r == 0:
            dx = jnp.concatenate([dx[0:8] + halo_rows[k, 0:8], dx[8:]], axis=0)
        if r == STRIPS - 1:
            dx = jnp.concatenate([dx[: CHUNK - 8], dx[CHUNK - 8 :] + halo_rows[k, 8:16]], axis=0)
        spot = lax.broadcasted_iota(jnp.int32, (CHUNK, 128), 1)
        side = halo_cols[at, :]
        left = jnp.where(spot < 3, pltpu.roll(side, lax.rem(128 - 8 * k, 128), 1), 0.0)
        right = jnp.where(spot >= 125, pltpu.roll(side, lax.rem(248 - 8 * k, 128), 1), 0.0)
        dy = dy + jnp.concatenate([left, right], axis=1)
        rise = fields[f, lax.rem(z + 1, NZ), at, :] - fields[f, lax.rem(z + NZ - 1, NZ), at, :]
        value = fields[f, z, at, :] - (
            (ADVECT / 60.0) * (fields[1, z, at, :] * dx + fields[2, z, at, :] * dy)
            + (0.5 * ADVECT) * (fields[3, z, at, :] * rise)
        )
        if f == 3:
            value = value + BUOY * fields[0, z, at, :]
        high, low = halves(value)
        forcing[k, at, :] = high
        forcing[k, CX + r * CHUNK : CX + (r + 1) * CHUNK, :] = low

    def contract(z, f):
        k = f * NZ + z
        by_high = dot(gx_rows[f], forcing[k, 0:CX, :])
        by_low = dot(gx_rows[f], forcing[k, CX:, :])
        message[pl.ds(k, 1), 0:CY] = by_high[0:1] + by_high[2:3] + by_low[0:1]
        message[pl.ds(k, 1), CY : 2 * CY] = by_high[1:2] + by_high[3:4] + by_low[1:2]

    def step(z, carry):
        for f in range(NF):
            for r in range(STRIPS):
                force(z, f, r)
            if f > 0:
                contract(z, f - 1)
        contract(z, NF - 1)
        return carry

    lax.fori_loop(0, NZ, step, 0)


def force_all(fields, q_cat, received, gx_rows, coefs):
    return pl.pallas_call(
        forcing_kernel,
        out_shape=(packed(ROWS, 2 * CX, CY), shaped(ROWS, 2 * CY + 128)),
        in_specs=[VM] * 8,
        out_specs=(VM,) * 2,
        scratch_shapes=[
            pltpu.VMEM((2 * CY, CY), BF16),
            pltpu.VMEM((STRIPS, CHUNK, WINDOW), BF16),
            pltpu.VMEM((ROWS, 16, CY), F32),
            pltpu.VMEM((CX, 128), F32),
            pltpu.VMEM((CX // 128, 128, 128), F32),
        ],
        compiler_params=pltpu.CompilerParams(vmem_limit_bytes=8 * MIB),
        cost_estimate=pl.CostEstimate(flops=4_000_000_000, bytes_accessed=16 * MIB, transcendentals=0),
        name="forcing",
    )(fields, q_cat, *received, gx_rows, coefs)


def products_kernel(items, forcing, gx_cat, gy_cat, out, s_0, s_1):
    def solve_x(k, r, s_cat):
        at = slice(r * CHUNK, (r + 1) * CHUNK)
        f = k // NZ
        high, low = forcing.at[k, 0:CX, :], forcing.at[k, CX : 2 * CX, :]
        section = dot(gx_cat[f, at, 0:CX], high[...]) + dot(gx_cat[f, at, 0:CX], low[...])
        section = section + dot(gx_cat[f, at, CX:], high[...])
        s_high, s_low = halves(section)
        s_cat[at, 0:CY] = s_high
        s_cat[at, CY:] = s_low

    def solve_y(k, place, r, s_cat):
        at = slice(r * CHUNK, (r + 1) * CHUNK)
        f = k // NZ
        out[place, at, :] = dot(s_cat[at, :], gy_cat[f, 0 : 2 * CY, :]) + dot(s_cat[at, 0:CY], gy_cat[f, 2 * CY :, :])

    bufs = (s_0, s_1)
    for n in range(len(items) + 1):
        for r in range(STRIPS):
            if n < len(items):
                solve_x(items[n], r, bufs[n % 2])
            if n > 0:
                solve_y(items[n - 1], n - 1, r, bufs[(n - 1) % 2])


def products(items, forcing, gx_cat, gy_cat):
    return pl.pallas_call(
        functools.partial(products_kernel, items),
        out_shape=shaped(len(items), CX, CY),
        in_specs=[VM] * 3,
        out_specs=VM,
        scratch_shapes=[pltpu.VMEM((CX, 2 * CY), BF16), pltpu.VMEM((CX, 2 * CY), BF16)],
        compiler_params=pltpu.CompilerParams(vmem_limit_bytes=6 * MIB),
        cost_estimate=pl.CostEstimate(
            flops=600_000_000 * len(items), bytes_accessed=1_500_000 * len(items), transcendentals=0
        ),
        name="block_products",
    )(forcing, gx_cat, gy_cat)


def weight_kernel(forcing, gy_rows, weighted):
    for k in range(ROWS):
        rows = gy_rows[k // NZ]
        by_high = dot_nt(rows, forcing[k, 0:CX, :])
        by_low = dot_nt(rows, forcing[k, CX : 2 * CX, :])
        weighted[0, k : k + 1, :] = by_high[0:1] + by_high[2:3] + by_low[0:1]
        weighted[1, k : k + 1, :] = by_high[1:2] + by_high[3:4] + by_low[1:2]


def weight(forcing, gy_rows):
    return pl.pallas_call(
        weight_kernel,
        out_shape=shaped(2, ROWS, CX),
        in_specs=[VM, VM],
        out_specs=VM,
        compiler_params=SMALL,
        cost_estimate=pl.CostEstimate(flops=500_000_000, bytes_accessed=8 * MIB, transcendentals=0),
        name="weighted_sums",
    )(forcing, gy_rows)


def weigh_kernel(weighted, gx_cat, out):
    high, low = halves(weighted[...].reshape(2 * ROWS, CX))
    owner = lax.rem(lax.broadcasted_iota(jnp.int32, (2 * ROWS, 1), 0), ROWS) // NZ
    total = jnp.zeros((2 * ROWS, CX), F32)
    for f in range(NF):
        value = dot_nt(high, gx_cat[f, :, 0:CX]) + dot_nt(low, gx_cat[f, :, 0:CX]) + dot_nt(high, gx_cat[f, :, CX:])
        total = jnp.where(owner == f, value, total)
    out[...] = total.reshape(2, ROWS, CX)


def weigh(weighted, gx_cat):
    return pl.pallas_call(
        weigh_kernel,
        out_shape=shaped(2, ROWS, CX),
        in_specs=[VM, VM],
        out_specs=VM,
        compiler_params=SMALL,
        cost_estimate=pl.CostEstimate(flops=500_000_000, bytes_accessed=5 * MIB, transcendentals=0),
        name="y_right_side",
    )(weighted, gx_cat)


def merge(side, mine, other, state, width):
    axis, reach = side
    is_right = jnp.broadcast_to(lax.rem(lax.axis_index(axis) // reach, 2), (ROWS, 1)) == 1

    def parts(ref):
        c = 2 * width
        return [
            ref[:, 0:width], ref[:, width:c],
            ref[:, c : c + 1], ref[:, c + 1 : c + 2], ref[:, c + 2 : c + 3], ref[:, c + 3 : c + 4],
        ]

    own, far = parts(mine), parts(other)
    l_first, l_last, l_p, l_s, l_q, l_t = [jnp.where(is_right, b, a) for a, b in zip(own, far)]
    r_first, r_last, r_p, r_s, r_q, r_t = [jnp.where(is_right, a, b) for a, b in zip(own, far)]
    inner = 1.0 / (1.0 - l_t * r_p)
    m_b = (l_last + l_t * r_first) * inner
    m_a = (r_first + r_p * l_last) * inner
    b_from_b, b_from_a = l_q * inner, l_t * r_s * inner
    a_from_b, a_from_a = r_p * l_q * inner, r_s * inner
    group = (
        l_first + l_s * m_a,
        r_last + r_q * m_b,
        l_p + l_s * a_from_b,
        l_s * a_from_a,
        r_q * b_from_b,
        r_t + r_q * b_from_a,
    )
    if state is None:
        prior, later, prior_b, prior_a, later_b, later_a = 0.0, 0.0, 1.0, 0.0, 0.0, 1.0
    else:
        prior, later, prior_b, prior_a, later_b, later_a = parts(state)
    fresh = []
    for base, by_b, by_a in ((prior, prior_b, prior_a), (later, later_b, later_a)):
        fresh.append(
            (
                base + jnp.where(is_right, by_b * m_b, by_a * m_a),
                jnp.where(is_right, by_b * b_from_b, by_b + by_a * a_from_b),
                jnp.where(is_right, by_a + by_b * b_from_a, by_a * a_from_a),
            )
        )
    return group, fresh


def last_merge(side, mine, other, state, width):
    axis, reach = side
    is_right = jnp.broadcast_to(lax.rem(lax.axis_index(axis) // reach, 2), (ROWS, 1)) == 1
    own, own_coef = mine[:, 0:width], mine[:, width : width + 1]
    far, far_coef = other[:, 0:width], other[:, width : width + 1]
    between = (far + far_coef * own) * (1.0 / (1.0 - own_coef * far_coef))
    c = 2 * width
    by_prior = jnp.where(is_right, state[:, c : c + 1], state[:, c + 1 : c + 2])
    by_later = jnp.where(is_right, state[:, c + 2 : c + 3], state[:, c + 3 : c + 4])
    return state[:, 0:width] + by_prior * between, state[:, width:c] + by_later * between


def lanes_of(values):
    spot = lax.broadcasted_iota(jnp.int32, (ROWS, 128), 1)
    total = jnp.zeros((ROWS, 128), F32)
    for place, value in enumerate(values):
        total = jnp.where(spot == place, value, total)
    return total


def merge_kernel(side, width, final, mine, other, *refs):
    state, (group_out, state_out) = (refs[0], refs[1:]) if len(refs) == 3 else (None, refs)
    group, fresh = merge(side, mine, other, state, width)
    if final:
        axis, reach = side
        is_right = jnp.broadcast_to(lax.rem(lax.axis_index(axis) // (2 * reach), 2), (ROWS, 1)) == 1
        group_out[:, 0:width] = jnp.where(is_right, group[0], group[1])
        group_out[:, width:] = lanes_of((jnp.where(is_right, group[2], group[5]),))
    else:
        group_out[:, 0:width] = group[0]
        group_out[:, width : 2 * width] = group[1]
        group_out[:, 2 * width :] = lanes_of(group[2:])
    state_out[:, 0:width] = fresh[0][0]
    state_out[:, width : 2 * width] = fresh[1][0]
    state_out[:, 2 * width :] = lanes_of((fresh[0][1], fresh[0][2], fresh[1][1], fresh[1][2]))


def merge_step(side, mine, other, state, width, final):
    carried = [] if state is None else [state]
    return pl.pallas_call(
        functools.partial(merge_kernel, side, width, final),
        out_shape=(shaped(ROWS, (1 if final else 2) * width + 128), shaped(ROWS, 2 * width + 128)),
        in_specs=[VM, VM] + [VM] * len(carried),
        out_specs=(VM, VM),
        compiler_params=SMALL,
        cost_estimate=pl.CostEstimate(flops=200_000, bytes_accessed=200_000, transcendentals=0),
        name="merge_groups",
    )(mine, other, *carried)


PARTNERS = {"gx": {1: 1, 2: 2, 4: 6}, "gy": {1: 1, 2: 3, 4: 4, 8: 12}}


def exchange(message, axis, width, fillers):
    count = lax.axis_size(axis)
    state = None
    reach = 1
    results = []
    while True:
        mask = PARTNERS[axis].get(reach, reach)
        other = lax.ppermute(message, axis, [(i, i ^ mask) for i in range(count)])
        filler = fillers.get(reach)
        if filler is not None:
            function, first, *rest = filler
            first, message = lax.optimization_barrier((first, message))
            result = function(first, *rest)
            result, message = lax.optimization_barrier((result, message))
            results.append(result)
        if 2 * reach >= count:
            return ((axis, reach), message, other, state), results
        message, state = merge_step((axis, reach), message, other, state, width, 4 * reach >= count)
        reach *= 2


def middle_kernel(side, mine, other, state, y_rhs, x_ends, y_ends, coefs, enter, message):
    fresh = last_merge(side, mine, other, state, CY)
    beta = coefs[0, :, BETA : BETA + 1]
    values = [beta * fresh[e] for e in range(2)]
    for e in range(2):
        enter[e] = values[e]
        total = y_rhs[e]
        for g in range(2):
            total = total + jnp.sum(values[g] * y_ends[e], axis=1, keepdims=True) * x_ends[g]
        message[:, e * CX : (e + 1) * CX] = total
    message[:, 2 * CX :] = coefs[1]


def middle(last, y_rhs, x_ends, y_ends, coefs):
    return pl.pallas_call(
        functools.partial(middle_kernel, last[0]),
        out_shape=(shaped(2, ROWS, CY), shaped(ROWS, 2 * CX + 128)),
        in_specs=[VM] * 7,
        out_specs=(VM, VM),
        compiler_params=SMALL,
        cost_estimate=pl.CostEstimate(flops=500_000, bytes_accessed=500_000, transcendentals=0),
        name="between_interfaces",
    )(*last[1:], y_rhs, x_ends, y_ends, coefs)


def rows_kernel(enter, ginv_y, edge_y, out, spread):
    high, low = halves(enter[...].reshape(2 * ROWS, CY))
    spot = lax.broadcasted_iota(jnp.int32, (16, 1), 0)
    for f in range(NF):
        g_high, g_low = halves(ginv_y[f])
        spread[...] = dot_nt(high, g_high) + dot_nt(low, g_high) + dot_nt(high, g_low)
        for z in range(NZ):
            k = f * NZ + z
            value = jnp.where(spot == z, edge_y[f, 0:1, :], 0.0) + jnp.where(spot == NZ + z, edge_y[f, 1:2, :], 0.0)
            value = value + jnp.where(spot == 8, spread[k : k + 1, :], 0.0)
            value = value + jnp.where(spot == 9, spread[ROWS + k : ROWS + k + 1, :], 0.0)
            v_high, v_low = halves(value)
            out[k, 0:16, :] = v_high
            out[k, 16:32, :] = v_high
            out[k, 32:48, :] = v_low
            out[k, 48:, :] = jnp.zeros((80, CY), BF16)


def row_products(enter, ginv_y, edge_y):
    return pl.pallas_call(
        rows_kernel,
        out_shape=packed(ROWS, 128, CY),
        in_specs=[VM, VM, VM],
        out_specs=VM,
        scratch_shapes=[pltpu.VMEM((2 * ROWS, CY), F32)],
        compiler_params=SMALL,
        cost_estimate=pl.CostEstimate(flops=300_000_000, bytes_accessed=2 * MIB, transcendentals=0),
        name="row_products",
    )(enter, ginv_y, edge_y)


def update_kernel(side, items, mine, other, state, *refs):
    bases, (wide, edge_x, coefs, out, tall, slim, done, sems) = refs[: len(items)], refs[len(items) :]
    where = {k: (base, place) for base, group in zip(bases, items) for place, k in enumerate(group)}
    fresh = last_merge(side, mine, other, state, CX)
    beta = coefs[1, :, BETA : BETA + 1]
    leave = [beta * fresh[e] for e in range(2)]
    for f in range(NF):
        s = slice(f * NZ, (f + 1) * NZ)
        value = jnp.concatenate([leave[e][s, :] for e in range(2)], axis=0)
        value = jnp.concatenate([value, edge_x[f, 0:8, :]], axis=0)
        high = value.astype(BF16).astype(F32)
        tall[0:16, :] = high
        tall[16:32, :] = (value - high).astype(BF16).astype(F32)
        tall[32:48, :] = high
        tall[48:, :] = jnp.zeros((80, CX), F32)
        for t in range(CX // 128):
            slim[f, t * 128 : (t + 1) * 128, :] = jnp.transpose(tall[:, t * 128 : (t + 1) * 128]).astype(BF16)
        for z in range(NZ):
            k = f * NZ + z
            base, place = where[k]
            for r in range(STRIPS):
                at = slice(r * CHUNK, (r + 1) * CHUNK)
                done[f, z, at, :] = base[place, at, :] + dot(slim[f, at, :], wide[k])
            pltpu.make_async_copy(done.at[f, z], out.at[f, z], sems.at[k]).start()
    for k in range(ROWS):
        pltpu.make_async_copy(done.at[k // NZ, k % NZ], out.at[k // NZ, k % NZ], sems.at[k]).wait()


def update(last, items, bases, wide, edge_x, coefs):
    return pl.pallas_call(
        functools.partial(update_kernel, last[0], items),
        out_shape=shaped(NF, NZ, CX, CY),
        in_specs=[VM] * (6 + len(bases)),
        out_specs=HB,
        scratch_shapes=[
            pltpu.VMEM((128, CX), F32),
            pltpu.VMEM((NF, CX, 128), BF16),
            pltpu.VMEM((NF, NZ, CX, CY), F32),
            pltpu.SemaphoreType.DMA((ROWS,)),
        ],
        compiler_params=pltpu.CompilerParams(vmem_limit_bytes=12 * MIB),
        cost_estimate=pl.CostEstimate(flops=200_000_000, bytes_accessed=17 * MIB, transcendentals=0),
        name="update_result",
    )(*last[1:], *bases, wide, edge_x, coefs)


def swap_pairs(value, axis, inner):
    count = lax.axis_size(axis)
    pairs = []
    for i in range(0 if inner else 1, count - 1, 2):
        pairs += [(i, i + 1), (i + 1, i)]
    return lax.ppermute(value, axis, pairs)


def local(fields, ginv_x, ginv_y, coupling_x, coupling_y):
    fields, q_cat, x_inner, x_outer, y_inner, y_outer = pack(fields)
    received = (
        swap_pairs(x_inner, "gx", True),
        swap_pairs(x_outer, "gx", False),
        swap_pairs(y_inner, "gy", True),
        swap_pairs(y_outer, "gy", False),
    )
    gx_cat, gy_cat, gx_rows, gy_rows, edge_x, edge_y, x_ends, y_ends, coefs = prep(
        ginv_x, ginv_y, coupling_x, coupling_y
    )
    forcing, message = force_all(fields, q_cat, received, gx_rows, coefs)

    def product(items):
        return lambda first, gx, gy: products(items, first, gx, gy), forcing, gx_cat, gy_cat

    sums = []

    def sum_up(rows):
        sums.append(weight(forcing, rows))
        return sums[0]

    def multiply(matrices):
        return weigh(sums[0], matrices)

    items = [tuple(range(*ends)) for ends in ((0, 2), (2, 6), (6, 10), (10, 13), (13, 16))]
    fillers = {1: product(items[0]), 2: (sum_up, gy_rows), 4: (multiply, gx_cat)}
    last_x, (base_0, _, y_rhs) = exchange(message, "gx", CY, fillers)
    enter, message_y = middle(last_x, y_rhs, x_ends, y_ends, coefs)

    def last_work(first):
        cells, matrices = first
        return products(items[4], cells, gx_cat, gy_cat), row_products(enter, matrices, edge_y)

    fillers = {1: product(items[1]), 2: product(items[2]), 4: product(items[3]), 8: (last_work, (forcing, ginv_y))}
    last_y, (base_1, base_2, base_3, (base_4, wide)) = exchange(message_y, "gy", CX, fillers)
    return update(last_y, items, (base_0, base_1, base_2, base_3, base_4), wide, edge_x, coefs)


def solution(mesh):
    in_specs = (P(None, None, "gx", "gy"), P(None, "gx", None), P(None, "gy", None), P(), P())
    out_specs = P(None, None, "gx", "gy")
    return jax.shard_map(local, mesh=mesh, in_specs=in_specs, out_specs=out_specs, check_vma=False)
```

```python
import functools

import jax
import jax.numpy as jnp
from jax import lax
from jax.experimental import pallas as pl
from jax.experimental.pallas import tpu as pltpu
from jax.sharding import PartitionSpec as P

F32 = jnp.float32
BF16 = jnp.bfloat16
BAND = (45.0, -9.0, 1.0)
ADVECT = 0.3
BUOY = 0.5
CX = 512
CY = 256
NF = 4
NZ = 4
ROWS = NF * NZ
MIB = 1024 * 1024

VM = pl.BlockSpec(memory_space=pltpu.VMEM)
SM = pl.BlockSpec(memory_space=pltpu.SMEM)
HB = pl.BlockSpec(memory_space=pltpu.HBM)
SMALL = pltpu.CompilerParams(vmem_limit_bytes=4 * MIB)


def shaped(*dims):
    return jax.ShapeDtypeStruct(dims, F32)


def packed(*dims):
    return jax.ShapeDtypeStruct(dims, BF16)


def halves(value):
    high = value.astype(BF16)
    return high, (value - high.astype(F32)).astype(BF16)


def dot(left, right):
    return lax.dot_general(left, right, (((1,), (0,)), ((), ())), preferred_element_type=F32)


def dot_nt(left, right):
    return lax.dot_general(left, right, (((1,), (1,)), ((), ())), preferred_element_type=F32)


def dot_tn(left, right):
    return lax.dot_general(left, right, (((0,), (0,)), ((), ())), preferred_element_type=F32)


def odd_blocks():
    return [lax.rem(lax.axis_index(axis), 2) == 1 for axis in ("gx", "gy")]


def pack_kernel(fields, planes, q_cat, x_inner, x_outer, y_inner, y_outer, lanes, turned, sems):
    groups = [(f, z) for f in range(NF) for z in (0, 2)]
    copies = [
        pltpu.make_async_copy(fields.at[f, z : z + 2], planes.at[f, z : z + 2], sems.at[g])
        for g, (f, z) in enumerate(groups)
    ]
    for copy in copies:
        copy.start()
    x_odd, y_odd = odd_blocks()
    step = 64
    for g, (f, start) in enumerate(groups):
        copies[g].wait()

        def chunk(r, carry, f=f, start=start, g=g):
            at = pl.ds(pl.multiple_of(r * step, step), step)
            spot = lax.broadcasted_iota(jnp.int32, (step, 128), 1)
            total = jnp.zeros((step, 128), F32) if g == 0 else lanes[at, :]
            for z in (start, start + 1):
                k = f * NZ + z
                value = planes[f, z, at, :]
                ends = jnp.where(spot >= 125, value[:, 128:256], 0.0)
                ends = jnp.where(spot < 3, value[:, 0:128], ends)
                total = total + pltpu.roll(ends, 8 * k + 3, 1)
                high, low = halves(value)
                q_cat[k, at, 0:CY] = high
                q_cat[k, at, CY:] = low
            lanes[at, :] = total
            return carry

        lax.fori_loop(0, CX // step, chunk, 0, unroll=True)
        for z in (start, start + 1):
            k = f * NZ + z
            for c in range(3):
                top = planes[f, z, c : c + 1, :]
                bottom = planes[f, z, CX - 3 + c : CX - 2 + c, :]
                x_inner[c, k : k + 1, :] = jnp.where(x_odd, top, bottom)
                x_outer[c, k : k + 1, :] = jnp.where(x_odd, bottom, top)
    for t in range(CX // 128):
        part = slice(t * 128, (t + 1) * 128)
        turned[t] = jnp.transpose(lanes[part, :])
        for c in range(3):
            right = turned[t, pl.ds(c, ROWS, stride=8), :]
            left = turned[t, pl.ds(3 + c, ROWS, stride=8), :]
            y_inner[c, :, part] = jnp.where(y_odd, left, right)
            y_outer[c, :, part] = jnp.where(y_odd, right, left)


def pack(fields):
    return pl.pallas_call(
        pack_kernel,
        out_shape=(
            shaped(NF, NZ, CX, CY),
            packed(ROWS, CX, 2 * CY),
            shaped(3, ROWS, CY),
            shaped(3, ROWS, CY),
            shaped(3, ROWS, CX),
            shaped(3, ROWS, CX),
        ),
        in_specs=[HB],
        out_specs=(VM,) * 6,
        scratch_shapes=[
            pltpu.VMEM((CX, 128), F32),
            pltpu.VMEM((CX // 128, 128, 128), F32),
            pltpu.SemaphoreType.DMA((2 * NF,)),
        ],
        compiler_params=pltpu.CompilerParams(vmem_limit_bytes=35 * MIB),
        cost_estimate=pl.CostEstimate(flops=10_000_000, bytes_accessed=9 * MIB, transcendentals=0),
        name="pack_edges",
    )(fields)


WINDOW = 256
CHUNK = 128
STRIPS = CX // CHUNK
BASES = (0, 64, 192, 256)


def band(shape, offset, along):
    gap = lax.broadcasted_iota(jnp.int32, shape, along) - lax.broadcasted_iota(jnp.int32, shape, 1 - along)
    gap = gap - offset
    total = jnp.zeros(shape, F32)
    for reach, weight in zip((1, 2, 3), BAND):
        total = jnp.where(gap == reach, weight, total)
        total = jnp.where(gap == -reach, -weight, total)
    return total.astype(BF16)


def halo_sums(before, after):
    sums = []
    for j in range(3):
        sums.append(sum(-BAND[o - 1] * before[3 + j - o] for o in range(j + 1, 4)))
    for j in range(3):
        sums.append(sum(BAND[o - 1] * after[j + o - 3] for o in range(3 - j, 4)))
    return sums


BETA = 4


def fill_coefs(beta, first_first, first_last, last_first, last_last):
    spot = lax.broadcasted_iota(jnp.int32, (NZ, 128), 1)
    values = jnp.where(
        spot == 0,
        first_first,
        jnp.where(
            spot == 1,
            first_last,
            jnp.where(spot == 2, last_first, jnp.where(spot == 3, last_last, jnp.where(spot == 4, 1.0, 0.0))),
        ),
    )
    return beta * values


def prep_kernel(gx, gy, beta_x, beta_y, gx_cat, gy_cat, gx_rows, gy_rows, edge_x, edge_y, x_ends, y_ends, coefs):
    gx_rows[...] = jnp.zeros_like(gx_rows)
    edge_x[...] = jnp.zeros_like(edge_x)
    gy_rows[...] = jnp.zeros_like(gy_rows)
    tile = 16
    spot = lax.broadcasted_iota(jnp.int32, (tile, 1), 0)

    def ends(first, last):
        f_high, f_low = halves(first)
        l_high, l_low = halves(last)
        parts = [value.astype(F32) for value in (f_high, l_high, f_low, l_low)]
        total = jnp.zeros((tile, first.shape[1]), F32)
        for place, value in enumerate(parts):
            total = jnp.where(spot == place, value, total)
        return total.astype(BF16)

    for f in range(NF):
        turned_g = jnp.transpose(gy[f])
        high, low = halves(turned_g)
        gy_cat[f, 0:CY, :] = high
        gy_cat[f, CY : 2 * CY, :] = high
        gy_cat[f, 2 * CY :, :] = low
        edge_y[f, 0:1, :] = turned_g[0:1]
        edge_y[f, 1:2, :] = turned_g[CY - 1 : CY]
        edge_y[f, 2:3, :] = gy[f, 0:1, :]
        edge_y[f, 3:4, :] = gy[f, CY - 1 : CY, :]
        gy_rows[f] = ends(gy[f, 0:1, :], gy[f, CY - 1 : CY, :])
        gx_rows[f] = ends(gx[f, 0:1, :], gx[f, CX - 1 : CX, :])

        def split(r, carry, f=f):
            at = pl.ds(pl.multiple_of(r * CHUNK, CHUNK), CHUNK)
            high, low = halves(gx[f, at, :])
            gx_cat[f, at, 0:CX] = high
            gx_cat[f, at, CX:] = low
            return carry

        lax.fori_loop(0, CX // CHUNK, split, 0)
        edge_x[f, 0:1, :] = jnp.transpose(gx[f, :, 0:128])[0:1]
        edge_x[f, 1:2, :] = jnp.transpose(gx[f, :, CX - 128 : CX])[127:128]
        s = slice(f * NZ, (f + 1) * NZ)
        for e in range(2):
            x_ends[e, s, :] = jnp.broadcast_to(edge_x[f, e : e + 1, :], (NZ, CX))
            y_ends[e, s, :] = jnp.broadcast_to(edge_y[f, 2 + e : 3 + e, :], (NZ, CY))
        for axis, (g, beta, n) in enumerate(((gx, beta_x, CX), (gy, beta_y, CY))):
            coefs[axis, s, :] = fill_coefs(
                beta[f], g[f, 0:1, 0:1], g[f, 0:1, n - 1 : n], g[f, n - 1 : n, 0:1], g[f, n - 1 : n, n - 1 : n]
            )


def prep(ginv_x, ginv_y, beta_x, beta_y):
    return pl.pallas_call(
        prep_kernel,
        out_shape=(
            packed(NF, CX, 2 * CX),
            packed(NF, 3 * CY, CY),
            packed(NF, 16, CX),
            packed(NF, 16, CY),
            shaped(NF, 8, CX),
            shaped(NF, 8, CY),
            shaped(2, ROWS, CX),
            shaped(2, ROWS, CY),
            shaped(2, ROWS, 128),
        ),
        in_specs=[VM, VM, SM, SM],
        out_specs=(VM,) * 9,
        compiler_params=SMALL,
        cost_estimate=pl.CostEstimate(flops=20_000_000, bytes_accessed=5 * MIB, transcendentals=0),
        name="split_matrices",
    )(ginv_x, ginv_y, beta_x, beta_y)


def forcing_kernel(
    fields, q_cat, x_inner, x_outer, y_inner, y_outer, gx_rows, coefs,
    forcing, message,
    band_y, band_x, halo_rows, halo_cols, turned,
):
    both = band((CY, CY), 0, 0)
    band_y[0:CY, :] = both
    band_y[CY:, :] = both
    for r in range(STRIPS):
        band_x[r] = band((CHUNK, WINDOW), r * CHUNK - BASES[r], 1)
    halo_rows[...] = jnp.zeros_like(halo_rows)
    turned[...] = jnp.zeros_like(turned)
    x_odd, y_odd = odd_blocks()
    above = [jnp.where(x_odd, x_inner[c], x_outer[c]) for c in range(3)]
    below = [jnp.where(x_odd, x_outer[c], x_inner[c]) for c in range(3)]
    for j, value in enumerate(halo_sums(above, below)):
        for k in range(ROWS):
            if j < 3:
                halo_rows[k, j : j + 1, :] = value[k : k + 1, :]
            else:
                halo_rows[k, j + 10 : j + 11, :] = value[k : k + 1, :]
    before = [jnp.where(y_odd, y_inner[c], y_outer[c]) for c in range(3)]
    behind = [jnp.where(y_odd, y_outer[c], y_inner[c]) for c in range(3)]
    for j, value in enumerate(halo_sums(before, behind)):
        for t in range(STRIPS):
            turned[t, pl.ds(j if j < 3 else j + 2, ROWS, stride=8), :] = value[:, t * 128 : (t + 1) * 128]
    for t in range(STRIPS):
        halo_cols[t * 128 : (t + 1) * 128, :] = jnp.transpose(turned[t])
    message[:, 2 * CY :] = coefs[0]

    def force(z, f, r):
        at = slice(r * CHUNK, (r + 1) * CHUNK)
        k = f * NZ + z
        window = slice(BASES[r], BASES[r] + WINDOW)
        dx = dot(band_x[r], q_cat[k, window, 0:CY]) + dot(band_x[r], q_cat[k, window, CY:])
        dy = dot(q_cat[k, at, :], band_y[...])
        if r == 0:
            dx = jnp.concatenate([dx[0:8] + halo_rows[k, 0:8], dx[8:]], axis=0)
        if r == STRIPS - 1:
            dx = jnp.concatenate([dx[: CHUNK - 8], dx[CHUNK - 8 :] + halo_rows[k, 8:16]], axis=0)
        spot = lax.broadcasted_iota(jnp.int32, (CHUNK, 128), 1)
        side = halo_cols[at, :]
        left = jnp.where(spot < 3, pltpu.roll(side, lax.rem(128 - 8 * k, 128), 1), 0.0)
        right = jnp.where(spot >= 125, pltpu.roll(side, lax.rem(248 - 8 * k, 128), 1), 0.0)
        dy = dy + jnp.concatenate([left, right], axis=1)
        rise = fields[f, lax.rem(z + 1, NZ), at, :] - fields[f, lax.rem(z + NZ - 1, NZ), at, :]
        value = fields[f, z, at, :] - (
            (ADVECT / 60.0) * (fields[1, z, at, :] * dx + fields[2, z, at, :] * dy)
            + (0.5 * ADVECT) * (fields[3, z, at, :] * rise)
        )
        if f == 3:
            value = value + BUOY * fields[0, z, at, :]
        high, low = halves(value)
        forcing[k, at, :] = high
        forcing[k, CX + r * CHUNK : CX + (r + 1) * CHUNK, :] = low

    def contract(z, f):
        k = f * NZ + z
        by_high = dot(gx_rows[f], forcing[k, 0:CX, :])
        by_low = dot(gx_rows[f], forcing[k, CX:, :])
        message[pl.ds(k, 1), 0:CY] = by_high[0:1] + by_high[2:3] + by_low[0:1]
        message[pl.ds(k, 1), CY : 2 * CY] = by_high[1:2] + by_high[3:4] + by_low[1:2]

    def step(z, carry):
        for f in range(NF):
            for r in range(STRIPS):
                force(z, f, r)
            if f > 0:
                contract(z, f - 1)
        contract(z, NF - 1)
        return carry

    lax.fori_loop(0, NZ, step, 0)


def force_all(fields, q_cat, received, gx_rows, coefs):
    return pl.pallas_call(
        forcing_kernel,
        out_shape=(packed(ROWS, 2 * CX, CY), shaped(ROWS, 2 * CY + 128)),
        in_specs=[VM] * 8,
        out_specs=(VM,) * 2,
        scratch_shapes=[
            pltpu.VMEM((2 * CY, CY), BF16),
            pltpu.VMEM((STRIPS, CHUNK, WINDOW), BF16),
            pltpu.VMEM((ROWS, 16, CY), F32),
            pltpu.VMEM((CX, 128), F32),
            pltpu.VMEM((CX // 128, 128, 128), F32),
        ],
        compiler_params=pltpu.CompilerParams(vmem_limit_bytes=8 * MIB),
        cost_estimate=pl.CostEstimate(flops=4_000_000_000, bytes_accessed=16 * MIB, transcendentals=0),
        name="forcing",
    )(fields, q_cat, *received, gx_rows, coefs)


def products_kernel(items, forcing, gx_cat, gy_cat, out, s_0, s_1):
    def solve_x(k, r, s_cat):
        at = slice(r * CHUNK, (r + 1) * CHUNK)
        f = k // NZ
        high, low = forcing.at[k, 0:CX, :], forcing.at[k, CX : 2 * CX, :]
        section = dot(gx_cat[f, at, 0:CX], high[...]) + dot(gx_cat[f, at, 0:CX], low[...])
        section = section + dot(gx_cat[f, at, CX:], high[...])
        s_high, s_low = halves(section)
        s_cat[at, 0:CY] = s_high
        s_cat[at, CY:] = s_low

    def solve_y(k, place, r, s_cat):
        at = slice(r * CHUNK, (r + 1) * CHUNK)
        f = k // NZ
        out[place, at, :] = dot(s_cat[at, :], gy_cat[f, 0 : 2 * CY, :]) + dot(s_cat[at, 0:CY], gy_cat[f, 2 * CY :, :])

    bufs = (s_0, s_1)
    for n in range(len(items) + 1):
        for r in range(STRIPS):
            if n < len(items):
                solve_x(items[n], r, bufs[n % 2])
            if n > 0:
                solve_y(items[n - 1], n - 1, r, bufs[(n - 1) % 2])


def products(items, forcing, gx_cat, gy_cat):
    return pl.pallas_call(
        functools.partial(products_kernel, items),
        out_shape=shaped(len(items), CX, CY),
        in_specs=[VM] * 3,
        out_specs=VM,
        scratch_shapes=[pltpu.VMEM((CX, 2 * CY), BF16), pltpu.VMEM((CX, 2 * CY), BF16)],
        compiler_params=pltpu.CompilerParams(vmem_limit_bytes=6 * MIB),
        cost_estimate=pl.CostEstimate(
            flops=600_000_000 * len(items), bytes_accessed=1_500_000 * len(items), transcendentals=0
        ),
        name="block_products",
    )(forcing, gx_cat, gy_cat)


def weight_kernel(forcing, gy_rows, weighted):
    for k in range(ROWS):
        rows = gy_rows[k // NZ]
        by_high = dot_nt(rows, forcing[k, 0:CX, :])
        by_low = dot_nt(rows, forcing[k, CX : 2 * CX, :])
        weighted[0, k : k + 1, :] = by_high[0:1] + by_high[2:3] + by_low[0:1]
        weighted[1, k : k + 1, :] = by_high[1:2] + by_high[3:4] + by_low[1:2]


def weight(forcing, gy_rows):
    return pl.pallas_call(
        weight_kernel,
        out_shape=shaped(2, ROWS, CX),
        in_specs=[VM, VM],
        out_specs=VM,
        compiler_params=SMALL,
        cost_estimate=pl.CostEstimate(flops=500_000_000, bytes_accessed=8 * MIB, transcendentals=0),
        name="weighted_sums",
    )(forcing, gy_rows)


def weigh_kernel(weighted, gx_cat, out):
    high, low = halves(weighted[...].reshape(2 * ROWS, CX))
    owner = lax.rem(lax.broadcasted_iota(jnp.int32, (2 * ROWS, 1), 0), ROWS) // NZ
    total = jnp.zeros((2 * ROWS, CX), F32)
    for f in range(NF):
        value = dot_nt(high, gx_cat[f, :, 0:CX]) + dot_nt(low, gx_cat[f, :, 0:CX]) + dot_nt(high, gx_cat[f, :, CX:])
        total = jnp.where(owner == f, value, total)
    out[...] = total.reshape(2, ROWS, CX)


def weigh(weighted, gx_cat):
    return pl.pallas_call(
        weigh_kernel,
        out_shape=shaped(2, ROWS, CX),
        in_specs=[VM, VM],
        out_specs=VM,
        compiler_params=SMALL,
        cost_estimate=pl.CostEstimate(flops=500_000_000, bytes_accessed=5 * MIB, transcendentals=0),
        name="y_right_side",
    )(weighted, gx_cat)


def merge(side, mine, other, state, width):
    axis, reach = side
    is_right = jnp.broadcast_to(lax.rem(lax.axis_index(axis) // reach, 2), (ROWS, 1)) == 1

    def parts(ref):
        c = 2 * width
        return [
            ref[:, 0:width], ref[:, width:c],
            ref[:, c : c + 1], ref[:, c + 1 : c + 2], ref[:, c + 2 : c + 3], ref[:, c + 3 : c + 4],
        ]

    own, far = parts(mine), parts(other)
    l_first, l_last, l_p, l_s, l_q, l_t = [jnp.where(is_right, b, a) for a, b in zip(own, far)]
    r_first, r_last, r_p, r_s, r_q, r_t = [jnp.where(is_right, a, b) for a, b in zip(own, far)]
    inner = 1.0 / (1.0 - l_t * r_p)
    m_b = (l_last + l_t * r_first) * inner
    m_a = (r_first + r_p * l_last) * inner
    b_from_b, b_from_a = l_q * inner, l_t * r_s * inner
    a_from_b, a_from_a = r_p * l_q * inner, r_s * inner
    group = (
        l_first + l_s * m_a,
        r_last + r_q * m_b,
        l_p + l_s * a_from_b,
        l_s * a_from_a,
        r_q * b_from_b,
        r_t + r_q * b_from_a,
    )
    if state is None:
        prior, later, prior_b, prior_a, later_b, later_a = 0.0, 0.0, 1.0, 0.0, 0.0, 1.0
    else:
        prior, later, prior_b, prior_a, later_b, later_a = parts(state)
    fresh = []
    for base, by_b, by_a in ((prior, prior_b, prior_a), (later, later_b, later_a)):
        fresh.append(
            (
                base + jnp.where(is_right, by_b * m_b, by_a * m_a),
                jnp.where(is_right, by_b * b_from_b, by_b + by_a * a_from_b),
                jnp.where(is_right, by_a + by_b * b_from_a, by_a * a_from_a),
            )
        )
    return group, fresh


def last_merge(side, mine, other, state, width):
    axis, reach = side
    is_right = jnp.broadcast_to(lax.rem(lax.axis_index(axis) // reach, 2), (ROWS, 1)) == 1
    own, own_coef = mine[:, 0:width], mine[:, width : width + 1]
    far, far_coef = other[:, 0:width], other[:, width : width + 1]
    between = (far + far_coef * own) * (1.0 / (1.0 - own_coef * far_coef))
    c = 2 * width
    by_prior = jnp.where(is_right, state[:, c : c + 1], state[:, c + 1 : c + 2])
    by_later = jnp.where(is_right, state[:, c + 2 : c + 3], state[:, c + 3 : c + 4])
    return state[:, 0:width] + by_prior * between, state[:, width:c] + by_later * between


def lanes_of(values):
    spot = lax.broadcasted_iota(jnp.int32, (ROWS, 128), 1)
    total = jnp.zeros((ROWS, 128), F32)
    for place, value in enumerate(values):
        total = jnp.where(spot == place, value, total)
    return total


def merge_kernel(side, width, final, mine, other, *refs):
    state, (group_out, state_out) = (refs[0], refs[1:]) if len(refs) == 3 else (None, refs)
    group, fresh = merge(side, mine, other, state, width)
    if final:
        axis, reach = side
        is_right = jnp.broadcast_to(lax.rem(lax.axis_index(axis) // (2 * reach), 2), (ROWS, 1)) == 1
        group_out[:, 0:width] = jnp.where(is_right, group[0], group[1])
        group_out[:, width:] = lanes_of((jnp.where(is_right, group[2], group[5]),))
    else:
        group_out[:, 0:width] = group[0]
        group_out[:, width : 2 * width] = group[1]
        group_out[:, 2 * width :] = lanes_of(group[2:])
    state_out[:, 0:width] = fresh[0][0]
    state_out[:, width : 2 * width] = fresh[1][0]
    state_out[:, 2 * width :] = lanes_of((fresh[0][1], fresh[0][2], fresh[1][1], fresh[1][2]))


def merge_step(side, mine, other, state, width, final):
    carried = [] if state is None else [state]
    return pl.pallas_call(
        functools.partial(merge_kernel, side, width, final),
        out_shape=(shaped(ROWS, (1 if final else 2) * width + 128), shaped(ROWS, 2 * width + 128)),
        in_specs=[VM, VM] + [VM] * len(carried),
        out_specs=(VM, VM),
        compiler_params=SMALL,
        cost_estimate=pl.CostEstimate(flops=200_000, bytes_accessed=200_000, transcendentals=0),
        name="merge_groups",
    )(mine, other, *carried)


PARTNERS = {"gx": {1: 1, 2: 2, 4: 6}, "gy": {1: 1, 2: 3, 4: 4, 8: 12}}


def exchange(message, axis, width, fillers):
    count = lax.axis_size(axis)
    state = None
    reach = 1
    results = []
    while True:
        mask = PARTNERS[axis].get(reach, reach)
        other = lax.ppermute(message, axis, [(i, i ^ mask) for i in range(count)])
        filler = fillers.get(reach)
        if filler is not None:
            function, first, *rest = filler
            first, message = lax.optimization_barrier((first, message))
            result = function(first, *rest)
            result, message = lax.optimization_barrier((result, message))
            results.append(result)
        if 2 * reach >= count:
            return ((axis, reach), message, other, state), results
        message, state = merge_step((axis, reach), message, other, state, width, 4 * reach >= count)
        reach *= 2


def middle_kernel(side, mine, other, state, y_rhs, x_ends, y_ends, coefs, enter, message):
    fresh = last_merge(side, mine, other, state, CY)
    beta = coefs[0, :, BETA : BETA + 1]
    values = [beta * fresh[e] for e in range(2)]
    for e in range(2):
        enter[e] = values[e]
        total = y_rhs[e]
        for g in range(2):
            total = total + jnp.sum(values[g] * y_ends[e], axis=1, keepdims=True) * x_ends[g]
        message[:, e * CX : (e + 1) * CX] = total
    message[:, 2 * CX :] = coefs[1]


def middle(last, y_rhs, x_ends, y_ends, coefs):
    return pl.pallas_call(
        functools.partial(middle_kernel, last[0]),
        out_shape=(shaped(2, ROWS, CY), shaped(ROWS, 2 * CX + 128)),
        in_specs=[VM] * 7,
        out_specs=(VM, VM),
        compiler_params=SMALL,
        cost_estimate=pl.CostEstimate(flops=500_000, bytes_accessed=500_000, transcendentals=0),
        name="between_interfaces",
    )(*last[1:], y_rhs, x_ends, y_ends, coefs)


def rows_kernel(enter, ginv_y, edge_y, out, spread):
    high, low = halves(enter[...].reshape(2 * ROWS, CY))
    spot = lax.broadcasted_iota(jnp.int32, (16, 1), 0)
    for f in range(NF):
        g_high, g_low = halves(ginv_y[f])
        spread[...] = dot_nt(high, g_high) + dot_nt(low, g_high) + dot_nt(high, g_low)
        for z in range(NZ):
            k = f * NZ + z
            value = jnp.where(spot == z, edge_y[f, 0:1, :], 0.0) + jnp.where(spot == NZ + z, edge_y[f, 1:2, :], 0.0)
            value = value + jnp.where(spot == 8, spread[k : k + 1, :], 0.0)
            value = value + jnp.where(spot == 9, spread[ROWS + k : ROWS + k + 1, :], 0.0)
            v_high, v_low = halves(value)
            out[k, 0:16, :] = v_high
            out[k, 16:32, :] = v_high
            out[k, 32:48, :] = v_low
            out[k, 48:, :] = jnp.zeros((80, CY), BF16)


def row_products(enter, ginv_y, edge_y):
    return pl.pallas_call(
        rows_kernel,
        out_shape=packed(ROWS, 128, CY),
        in_specs=[VM, VM, VM],
        out_specs=VM,
        scratch_shapes=[pltpu.VMEM((2 * ROWS, CY), F32)],
        compiler_params=SMALL,
        cost_estimate=pl.CostEstimate(flops=300_000_000, bytes_accessed=2 * MIB, transcendentals=0),
        name="row_products",
    )(enter, ginv_y, edge_y)


def update_kernel(side, items, mine, other, state, *refs):
    bases, (wide, edge_x, coefs, out, tall, slim, done, sems) = refs[: len(items)], refs[len(items) :]
    where = {k: (base, place) for base, group in zip(bases, items) for place, k in enumerate(group)}
    fresh = last_merge(side, mine, other, state, CX)
    beta = coefs[1, :, BETA : BETA + 1]
    leave = [beta * fresh[e] for e in range(2)]
    for f in range(NF):
        s = slice(f * NZ, (f + 1) * NZ)
        value = jnp.concatenate([leave[e][s, :] for e in range(2)], axis=0)
        value = jnp.concatenate([value, edge_x[f, 0:8, :]], axis=0)
        high = value.astype(BF16).astype(F32)
        tall[0:16, :] = high
        tall[16:32, :] = (value - high).astype(BF16).astype(F32)
        tall[32:48, :] = high
        tall[48:, :] = jnp.zeros((80, CX), F32)
        for t in range(CX // 128):
            slim[f, t * 128 : (t + 1) * 128, :] = jnp.transpose(tall[:, t * 128 : (t + 1) * 128]).astype(BF16)
        for z in range(NZ):
            k = f * NZ + z
            base, place = where[k]
            for r in range(STRIPS):
                at = slice(r * CHUNK, (r + 1) * CHUNK)
                done[f, z, at, :] = base[place, at, :] + dot(slim[f, at, :], wide[k])
            pltpu.make_async_copy(done.at[f, z], out.at[f, z], sems.at[k]).start()
    for k in range(ROWS):
        pltpu.make_async_copy(done.at[k // NZ, k % NZ], out.at[k // NZ, k % NZ], sems.at[k]).wait()


def update(last, items, bases, wide, edge_x, coefs):
    return pl.pallas_call(
        functools.partial(update_kernel, last[0], items),
        out_shape=shaped(NF, NZ, CX, CY),
        in_specs=[VM] * (6 + len(bases)),
        out_specs=HB,
        scratch_shapes=[
            pltpu.VMEM((128, CX), F32),
            pltpu.VMEM((NF, CX, 128), BF16),
            pltpu.VMEM((NF, NZ, CX, CY), F32),
            pltpu.SemaphoreType.DMA((ROWS,)),
        ],
        compiler_params=pltpu.CompilerParams(vmem_limit_bytes=12 * MIB),
        cost_estimate=pl.CostEstimate(flops=200_000_000, bytes_accessed=17 * MIB, transcendentals=0),
        name="update_result",
    )(*last[1:], *bases, wide, edge_x, coefs)


def swap_pairs(value, axis, inner):
    count = lax.axis_size(axis)
    pairs = []
    for i in range(0 if inner else 1, count - 1, 2):
        pairs += [(i, i + 1), (i + 1, i)]
    return lax.ppermute(value, axis, pairs)


def local(fields, ginv_x, ginv_y, coupling_x, coupling_y):
    fields, q_cat, x_inner, x_outer, y_inner, y_outer = pack(fields)
    received = (
        swap_pairs(x_inner, "gx", True),
        swap_pairs(x_outer, "gx", False),
        swap_pairs(y_inner, "gy", True),
        swap_pairs(y_outer, "gy", False),
    )
    gx_cat, gy_cat, gx_rows, gy_rows, edge_x, edge_y, x_ends, y_ends, coefs = prep(
        ginv_x, ginv_y, coupling_x, coupling_y
    )
    forcing, message = force_all(fields, q_cat, received, gx_rows, coefs)

    def product(items):
        return lambda first, gx, gy: products(items, first, gx, gy), forcing, gx_cat, gy_cat

    sums = []

    def sum_up(rows):
        sums.append(weight(forcing, rows))
        return sums[0]

    items = [tuple(range(*ends)) for ends in ((0, 2), (2, 3), (3, 7), (7, 10), (10, 13), (13, 16))]

    def multiply(first):
        cells, matrices = first
        return products(items[1], cells, matrices, gy_cat), weigh(sums[0], matrices)

    fillers = {1: product(items[0]), 2: (sum_up, gy_rows), 4: (multiply, (forcing, gx_cat))}
    last_x, (base_0, _, (base_1, y_rhs)) = exchange(message, "gx", CY, fillers)
    enter, message_y = middle(last_x, y_rhs, x_ends, y_ends, coefs)

    def last_work(first):
        cells, matrices = first
        return products(items[5], cells, gx_cat, gy_cat), row_products(enter, matrices, edge_y)

    fillers = {1: product(items[2]), 2: product(items[3]), 4: product(items[4]), 8: (last_work, (forcing, ginv_y))}
    last_y, (base_2, base_3, base_4, (base_5, wide)) = exchange(message_y, "gy", CX, fillers)
    return update(last_y, items, (base_0, base_1, base_2, base_3, base_4, base_5), wide, edge_x, coefs)


def solution(mesh):
    in_specs = (P(None, None, "gx", "gy"), P(None, "gx", None), P(None, "gy", None), P(), P())
    out_specs = P(None, None, "gx", "gy")
    return jax.shard_map(local, mesh=mesh, in_specs=in_specs, out_specs=out_specs, check_vma=False)
```

```python
import functools

import jax
import jax.numpy as jnp
from jax import lax
from jax.experimental import pallas as pl
from jax.experimental.pallas import tpu as pltpu
from jax.sharding import PartitionSpec as P

F32 = jnp.float32
BF16 = jnp.bfloat16
BAND = (45.0, -9.0, 1.0)
ADVECT = 0.3
BUOY = 0.5
CX = 512
CY = 256
NF = 4
NZ = 4
ROWS = NF * NZ
MIB = 1024 * 1024

VM = pl.BlockSpec(memory_space=pltpu.VMEM)
SM = pl.BlockSpec(memory_space=pltpu.SMEM)
HB = pl.BlockSpec(memory_space=pltpu.HBM)
SMALL = pltpu.CompilerParams(vmem_limit_bytes=4 * MIB)


def shaped(*dims):
    return jax.ShapeDtypeStruct(dims, F32)


def packed(*dims):
    return jax.ShapeDtypeStruct(dims, BF16)


def halves(value):
    high = value.astype(BF16)
    return high, (value - high.astype(F32)).astype(BF16)


def dot(left, right):
    return lax.dot_general(left, right, (((1,), (0,)), ((), ())), preferred_element_type=F32)


def dot_nt(left, right):
    return lax.dot_general(left, right, (((1,), (1,)), ((), ())), preferred_element_type=F32)


def dot_tn(left, right):
    return lax.dot_general(left, right, (((0,), (0,)), ((), ())), preferred_element_type=F32)


def odd_blocks():
    return [lax.rem(lax.axis_index(axis), 2) == 1 for axis in ("gx", "gy")]


def pack_kernel(fields, planes, q_cat, x_inner, x_outer, y_inner, y_outer, lanes, turned, sems):
    groups = [(f, z) for f in range(NF) for z in (0, 2)]
    copies = [
        pltpu.make_async_copy(fields.at[f, z : z + 2], planes.at[f, z : z + 2], sems.at[g])
        for g, (f, z) in enumerate(groups)
    ]
    for copy in copies:
        copy.start()
    x_odd, y_odd = odd_blocks()
    step = 64
    for g, (f, start) in enumerate(groups):
        copies[g].wait()

        def chunk(r, carry, f=f, start=start, g=g):
            at = pl.ds(pl.multiple_of(r * step, step), step)
            spot = lax.broadcasted_iota(jnp.int32, (step, 128), 1)
            total = jnp.zeros((step, 128), F32) if g == 0 else lanes[at, :]
            for z in (start, start + 1):
                k = f * NZ + z
                value = planes[f, z, at, :]
                ends = jnp.where(spot >= 125, value[:, 128:256], 0.0)
                ends = jnp.where(spot < 3, value[:, 0:128], ends)
                total = total + pltpu.roll(ends, 8 * k + 3, 1)
                high, low = halves(value)
                q_cat[k, at, 0:CY] = high
                q_cat[k, at, CY:] = low
            lanes[at, :] = total
            return carry

        lax.fori_loop(0, CX // step, chunk, 0, unroll=True)
        for z in (start, start + 1):
            k = f * NZ + z
            for c in range(3):
                top = planes[f, z, c : c + 1, :]
                bottom = planes[f, z, CX - 3 + c : CX - 2 + c, :]
                x_inner[c, k : k + 1, :] = jnp.where(x_odd, top, bottom)
                x_outer[c, k : k + 1, :] = jnp.where(x_odd, bottom, top)
    for t in range(CX // 128):
        part = slice(t * 128, (t + 1) * 128)
        turned[t, 0:128, :] = jnp.transpose(lanes[part, :])
        for c in range(3):
            right = turned[t, pl.ds(c, ROWS, stride=8), :]
            left = turned[t, pl.ds(3 + c, ROWS, stride=8), :]
            y_inner[c, :, part] = jnp.where(y_odd, left, right)
            y_outer[c, :, part] = jnp.where(y_odd, right, left)


def pack(fields):
    return pl.pallas_call(
        pack_kernel,
        out_shape=(
            shaped(NF, NZ, CX, CY),
            packed(ROWS, CX, 2 * CY),
            shaped(3, ROWS, CY),
            shaped(3, ROWS, CY),
            shaped(3, ROWS, CX),
            shaped(3, ROWS, CX),
        ),
        in_specs=[HB],
        out_specs=(VM,) * 6,
        scratch_shapes=[
            pltpu.VMEM((CX, 128), F32),
            pltpu.VMEM((CX // 128, 136, 128), F32),
            pltpu.SemaphoreType.DMA((2 * NF,)),
        ],
        compiler_params=pltpu.CompilerParams(vmem_limit_bytes=35 * MIB),
        cost_estimate=pl.CostEstimate(flops=10_000_000, bytes_accessed=9 * MIB, transcendentals=0),
        name="pack_edges",
    )(fields)


WINDOW = 256
CHUNK = 128
STRIPS = CX // CHUNK
BASES = (0, 64, 192, 256)


def band(shape, offset, along):
    gap = lax.broadcasted_iota(jnp.int32, shape, along) - lax.broadcasted_iota(jnp.int32, shape, 1 - along)
    gap = gap - offset
    total = jnp.zeros(shape, F32)
    for reach, weight in zip((1, 2, 3), BAND):
        total = jnp.where(gap == reach, weight, total)
        total = jnp.where(gap == -reach, -weight, total)
    return total.astype(BF16)


def halo_sums(before, after):
    sums = []
    for j in range(3):
        sums.append(sum(-BAND[o - 1] * before[3 + j - o] for o in range(j + 1, 4)))
    for j in range(3):
        sums.append(sum(BAND[o - 1] * after[j + o - 3] for o in range(3 - j, 4)))
    return sums


BETA = 4


def fill_coefs(beta, first_first, first_last, last_first, last_last):
    spot = lax.broadcasted_iota(jnp.int32, (NZ, 128), 1)
    values = jnp.where(
        spot == 0,
        first_first,
        jnp.where(
            spot == 1,
            first_last,
            jnp.where(spot == 2, last_first, jnp.where(spot == 3, last_last, jnp.where(spot == 4, 1.0, 0.0))),
        ),
    )
    return beta * values


def prep_kernel(gx, gy, beta_x, beta_y, gx_cat, gy_cat, gx_rows, gy_rows, edge_x, edge_y, x_ends, y_ends, coefs):
    gx_rows[...] = jnp.zeros_like(gx_rows)
    edge_x[...] = jnp.zeros_like(edge_x)
    gy_rows[...] = jnp.zeros_like(gy_rows)
    tile = 16
    spot = lax.broadcasted_iota(jnp.int32, (tile, 1), 0)

    def ends(first, last):
        f_high, f_low = halves(first)
        l_high, l_low = halves(last)
        parts = [value.astype(F32) for value in (f_high, l_high, f_low, l_low)]
        total = jnp.zeros((tile, first.shape[1]), F32)
        for place, value in enumerate(parts):
            total = jnp.where(spot == place, value, total)
        return total.astype(BF16)

    for f in range(NF):
        turned_g = jnp.transpose(gy[f])
        high, low = halves(turned_g)
        gy_cat[f, 0:CY, :] = high
        gy_cat[f, CY : 2 * CY, :] = high
        gy_cat[f, 2 * CY :, :] = low
        edge_y[f, 0:1, :] = turned_g[0:1]
        edge_y[f, 1:2, :] = turned_g[CY - 1 : CY]
        edge_y[f, 2:3, :] = gy[f, 0:1, :]
        edge_y[f, 3:4, :] = gy[f, CY - 1 : CY, :]
        gy_rows[f] = ends(gy[f, 0:1, :], gy[f, CY - 1 : CY, :])
        gx_rows[f] = ends(gx[f, 0:1, :], gx[f, CX - 1 : CX, :])

        def split(r, carry, f=f):
            at = pl.ds(pl.multiple_of(r * CHUNK, CHUNK), CHUNK)
            high, low = halves(gx[f, at, :])
            gx_cat[f, at, 0:CX] = high
            gx_cat[f, at, CX:] = low
            return carry

        lax.fori_loop(0, CX // CHUNK, split, 0)
        edge_x[f, 0:1, :] = jnp.transpose(gx[f, :, 0:128])[0:1]
        edge_x[f, 1:2, :] = jnp.transpose(gx[f, :, CX - 128 : CX])[127:128]
        s = slice(f * NZ, (f + 1) * NZ)
        for e in range(2):
            x_ends[e, s, :] = jnp.broadcast_to(edge_x[f, e : e + 1, :], (NZ, CX))
            y_ends[e, s, :] = jnp.broadcast_to(edge_y[f, 2 + e : 3 + e, :], (NZ, CY))
        for axis, (g, beta, n) in enumerate(((gx, beta_x, CX), (gy, beta_y, CY))):
            coefs[axis, s, :] = fill_coefs(
                beta[f], g[f, 0:1, 0:1], g[f, 0:1, n - 1 : n], g[f, n - 1 : n, 0:1], g[f, n - 1 : n, n - 1 : n]
            )


def prep(ginv_x, ginv_y, beta_x, beta_y):
    return pl.pallas_call(
        prep_kernel,
        out_shape=(
            packed(NF, CX, 2 * CX),
            packed(NF, 3 * CY, CY),
            packed(NF, 16, CX),
            packed(NF, 16, CY),
            shaped(NF, 8, CX),
            shaped(NF, 8, CY),
            shaped(2, ROWS, CX),
            shaped(2, ROWS, CY),
            shaped(2, ROWS, 128),
        ),
        in_specs=[VM, VM, SM, SM],
        out_specs=(VM,) * 9,
        compiler_params=SMALL,
        cost_estimate=pl.CostEstimate(flops=20_000_000, bytes_accessed=5 * MIB, transcendentals=0),
        name="split_matrices",
    )(ginv_x, ginv_y, beta_x, beta_y)


def forcing_kernel(
    fields, q_cat, x_inner, x_outer, y_inner, y_outer, gx_rows, coefs,
    forcing, message,
    band_y, band_x, halo_rows, halo_cols, turned, ends,
):
    both = band((CY, CY), 0, 0)
    band_y[0:CY, :] = both
    band_y[CY:, :] = both
    for r in range(STRIPS):
        band_x[r] = band((CHUNK, WINDOW), r * CHUNK - BASES[r], 1)
    halo_rows[...] = jnp.zeros_like(halo_rows)
    turned[...] = jnp.zeros_like(turned)
    x_odd, y_odd = odd_blocks()
    above = [jnp.where(x_odd, x_inner[c], x_outer[c]) for c in range(3)]
    below = [jnp.where(x_odd, x_outer[c], x_inner[c]) for c in range(3)]
    for j, value in enumerate(halo_sums(above, below)):
        for k in range(ROWS):
            if j < 3:
                halo_rows[k, j : j + 1, :] = value[k : k + 1, :]
            else:
                halo_rows[k, j + 10 : j + 11, :] = value[k : k + 1, :]
    before = [jnp.where(y_odd, y_inner[c], y_outer[c]) for c in range(3)]
    behind = [jnp.where(y_odd, y_outer[c], y_inner[c]) for c in range(3)]
    for j, value in enumerate(halo_sums(before, behind)):
        for t in range(STRIPS):
            turned[t, pl.ds(j if j < 3 else j + 2, ROWS, stride=8), :] = value[:, t * 128 : (t + 1) * 128]
    for t in range(STRIPS):
        halo_cols[t * 128 : (t + 1) * 128, :] = jnp.transpose(turned[t, 0:128, :])
    message[:, 2 * CY :] = coefs[0]

    def force(z, f, r):
        at = slice(r * CHUNK, (r + 1) * CHUNK)
        k = f * NZ + z
        window = slice(BASES[r], BASES[r] + WINDOW)
        dx = dot(band_x[r], q_cat[k, window, 0:CY]) + dot(band_x[r], q_cat[k, window, CY:])
        dy = dot(q_cat[k, at, :], band_y[...])
        if r == 0:
            dx = jnp.concatenate([dx[0:8] + halo_rows[k, 0:8], dx[8:]], axis=0)
        if r == STRIPS - 1:
            dx = jnp.concatenate([dx[: CHUNK - 8], dx[CHUNK - 8 :] + halo_rows[k, 8:16]], axis=0)
        spot = lax.broadcasted_iota(jnp.int32, (CHUNK, 128), 1)
        side = halo_cols[at, :]
        left = jnp.where(spot < 3, pltpu.roll(side, lax.rem(128 - 8 * k, 128), 1), 0.0)
        right = jnp.where(spot >= 125, pltpu.roll(side, lax.rem(248 - 8 * k, 128), 1), 0.0)
        dy = dy + jnp.concatenate([left, right], axis=1)
        rise = fields[f, lax.rem(z + 1, NZ), at, :] - fields[f, lax.rem(z + NZ - 1, NZ), at, :]
        value = fields[f, z, at, :] - (
            (ADVECT / 60.0) * (fields[1, z, at, :] * dx + fields[2, z, at, :] * dy)
            + (0.5 * ADVECT) * (fields[3, z, at, :] * rise)
        )
        if f == 3:
            value = value + BUOY * fields[0, z, at, :]
        high, low = halves(value)
        forcing[k, at, :] = high
        forcing[k, CX + r * CHUNK : CX + (r + 1) * CHUNK, :] = low

    def contract(z, f):
        k = f * NZ + z
        by_high = dot(gx_rows[f], forcing[k, 0:CX, :])
        by_low = dot(gx_rows[f], forcing[k, CX:, :])
        ends[pl.ds(k, 1), 0:CY] = by_high[0:1] + by_high[2:3] + by_low[0:1]
        ends[pl.ds(k, 1), CY:] = by_high[1:2] + by_high[3:4] + by_low[1:2]

    def step(z, carry):
        for f in range(NF):
            for r in range(STRIPS):
                force(z, f, r)
            if f > 0:
                contract(z, f - 1)
        contract(z, NF - 1)
        return carry

    lax.fori_loop(0, NZ, step, 0)
    message[:, 0 : 2 * CY] = ends[0:ROWS, :]


def force_all(fields, q_cat, received, gx_rows, coefs):
    return pl.pallas_call(
        forcing_kernel,
        out_shape=(packed(ROWS, 2 * CX, CY), shaped(ROWS, 2 * CY + 128)),
        in_specs=[VM] * 8,
        out_specs=(VM,) * 2,
        scratch_shapes=[
            pltpu.VMEM((2 * CY, CY), BF16),
            pltpu.VMEM((STRIPS, CHUNK, WINDOW), BF16),
            pltpu.VMEM((ROWS, 16, CY), F32),
            pltpu.VMEM((CX, 128), F32),
            pltpu.VMEM((CX // 128, 136, 128), F32),
            pltpu.VMEM((2 * ROWS, 2 * CY), F32),
        ],
        compiler_params=pltpu.CompilerParams(vmem_limit_bytes=8 * MIB),
        cost_estimate=pl.CostEstimate(flops=4_000_000_000, bytes_accessed=16 * MIB, transcendentals=0),
        name="forcing",
    )(fields, q_cat, *received, gx_rows, coefs)


def products_kernel(items, forcing, gx_cat, gy_cat, out, s_0, s_1):
    def solve_x(k, r, s_cat):
        at = slice(r * CHUNK, (r + 1) * CHUNK)
        f = k // NZ
        high, low = forcing.at[k, 0:CX, :], forcing.at[k, CX : 2 * CX, :]
        section = dot(gx_cat[f, at, 0:CX], high[...]) + dot(gx_cat[f, at, 0:CX], low[...])
        section = section + dot(gx_cat[f, at, CX:], high[...])
        s_high, s_low = halves(section)
        s_cat[at, 0:CY] = s_high
        s_cat[at, CY:] = s_low

    def solve_y(k, place, r, s_cat):
        at = slice(r * CHUNK, (r + 1) * CHUNK)
        f = k // NZ
        out[place, at, :] = dot(s_cat[at, :], gy_cat[f, 0 : 2 * CY, :]) + dot(s_cat[at, 0:CY], gy_cat[f, 2 * CY :, :])

    bufs = (s_0, s_1)
    for n in range(len(items) + 1):
        for r in range(STRIPS):
            if n < len(items):
                solve_x(items[n], r, bufs[n % 2])
            if n > 0:
                solve_y(items[n - 1], n - 1, r, bufs[(n - 1) % 2])


def products(items, forcing, gx_cat, gy_cat):
    return pl.pallas_call(
        functools.partial(products_kernel, items),
        out_shape=shaped(len(items), CX, CY),
        in_specs=[VM] * 3,
        out_specs=VM,
        scratch_shapes=[pltpu.VMEM((CX, 2 * CY), BF16), pltpu.VMEM((CX, 2 * CY), BF16)],
        compiler_params=pltpu.CompilerParams(vmem_limit_bytes=6 * MIB),
        cost_estimate=pl.CostEstimate(
            flops=600_000_000 * len(items), bytes_accessed=1_500_000 * len(items), transcendentals=0
        ),
        name="block_products",
    )(forcing, gx_cat, gy_cat)


def weight_kernel(forcing, gy_rows, weighted):
    for k in range(ROWS):
        both = dot_nt(gy_rows[k // NZ], forcing[k])
        high, low = both[:, 0:CX], both[:, CX:]
        weighted[0, k : k + 1, :] = high[0:1] + high[2:3] + low[0:1]
        weighted[1, k : k + 1, :] = high[1:2] + high[3:4] + low[1:2]


def weight(forcing, gy_rows):
    return pl.pallas_call(
        weight_kernel,
        out_shape=shaped(2, ROWS, CX),
        in_specs=[VM, VM],
        out_specs=VM,
        compiler_params=SMALL,
        cost_estimate=pl.CostEstimate(flops=500_000_000, bytes_accessed=8 * MIB, transcendentals=0),
        name="weighted_sums",
    )(forcing, gy_rows)


def weigh_kernel(weighted, gx_cat, out):
    high, low = halves(weighted[...].reshape(2 * ROWS, CX))
    owner = lax.rem(lax.broadcasted_iota(jnp.int32, (2 * ROWS, 1), 0), ROWS) // NZ
    total = jnp.zeros((2 * ROWS, CX), F32)
    for f in range(NF):
        value = dot_nt(high, gx_cat[f, :, 0:CX]) + dot_nt(low, gx_cat[f, :, 0:CX]) + dot_nt(high, gx_cat[f, :, CX:])
        total = jnp.where(owner == f, value, total)
    out[...] = total.reshape(2, ROWS, CX)


def weigh(weighted, gx_cat):
    return pl.pallas_call(
        weigh_kernel,
        out_shape=shaped(2, ROWS, CX),
        in_specs=[VM, VM],
        out_specs=VM,
        compiler_params=SMALL,
        cost_estimate=pl.CostEstimate(flops=500_000_000, bytes_accessed=5 * MIB, transcendentals=0),
        name="y_right_side",
    )(weighted, gx_cat)


def merge(side, mine, other, state, width):
    axis, reach = side
    is_right = jnp.broadcast_to(lax.rem(lax.axis_index(axis) // reach, 2), (ROWS, 1)) == 1

    def parts(ref):
        c = 2 * width
        return [
            ref[:, 0:width], ref[:, width:c],
            ref[:, c : c + 1], ref[:, c + 1 : c + 2], ref[:, c + 2 : c + 3], ref[:, c + 3 : c + 4],
        ]

    own, far = parts(mine), parts(other)
    l_first, l_last, l_p, l_s, l_q, l_t = [jnp.where(is_right, b, a) for a, b in zip(own, far)]
    r_first, r_last, r_p, r_s, r_q, r_t = [jnp.where(is_right, a, b) for a, b in zip(own, far)]
    inner = 1.0 / (1.0 - l_t * r_p)
    m_b = (l_last + l_t * r_first) * inner
    m_a = (r_first + r_p * l_last) * inner
    b_from_b, b_from_a = l_q * inner, l_t * r_s * inner
    a_from_b, a_from_a = r_p * l_q * inner, r_s * inner
    group = (
        l_first + l_s * m_a,
        r_last + r_q * m_b,
        l_p + l_s * a_from_b,
        l_s * a_from_a,
        r_q * b_from_b,
        r_t + r_q * b_from_a,
    )
    if state is None:
        prior, later, prior_b, prior_a, later_b, later_a = 0.0, 0.0, 1.0, 0.0, 0.0, 1.0
    else:
        prior, later, prior_b, prior_a, later_b, later_a = parts(state)
    fresh = []
    for base, by_b, by_a in ((prior, prior_b, prior_a), (later, later_b, later_a)):
        fresh.append(
            (
                base + jnp.where(is_right, by_b * m_b, by_a * m_a),
                jnp.where(is_right, by_b * b_from_b, by_b + by_a * a_from_b),
                jnp.where(is_right, by_a + by_b * b_from_a, by_a * a_from_a),
            )
        )
    return group, fresh


def last_merge(side, mine, other, state, width):
    axis, reach = side
    is_right = jnp.broadcast_to(lax.rem(lax.axis_index(axis) // reach, 2), (ROWS, 1)) == 1
    own, own_coef = mine[:, 0:width], mine[:, width : width + 1]
    far, far_coef = other[:, 0:width], other[:, width : width + 1]
    between = (far + far_coef * own) * (1.0 / (1.0 - own_coef * far_coef))
    c = 2 * width
    by_prior = jnp.where(is_right, state[:, c : c + 1], state[:, c + 1 : c + 2])
    by_later = jnp.where(is_right, state[:, c + 2 : c + 3], state[:, c + 3 : c + 4])
    return state[:, 0:width] + by_prior * between, state[:, width:c] + by_later * between


def lanes_of(values):
    spot = lax.broadcasted_iota(jnp.int32, (ROWS, 128), 1)
    total = jnp.zeros((ROWS, 128), F32)
    for place, value in enumerate(values):
        total = jnp.where(spot == place, value, total)
    return total


def merge_kernel(side, width, final, mine, other, *refs):
    state, (group_out, state_out) = (refs[0], refs[1:]) if len(refs) == 3 else (None, refs)
    group, fresh = merge(side, mine, other, state, width)
    if final:
        axis, reach = side
        is_right = jnp.broadcast_to(lax.rem(lax.axis_index(axis) // (2 * reach), 2), (ROWS, 1)) == 1
        group_out[:, 0:width] = jnp.where(is_right, group[0], group[1])
        group_out[:, width:] = lanes_of((jnp.where(is_right, group[2], group[5]),))
    else:
        group_out[:, 0:width] = group[0]
        group_out[:, width : 2 * width] = group[1]
        group_out[:, 2 * width :] = lanes_of(group[2:])
    state_out[:, 0:width] = fresh[0][0]
    state_out[:, width : 2 * width] = fresh[1][0]
    state_out[:, 2 * width :] = lanes_of((fresh[0][1], fresh[0][2], fresh[1][1], fresh[1][2]))


def merge_step(side, mine, other, state, width, final):
    carried = [] if state is None else [state]
    return pl.pallas_call(
        functools.partial(merge_kernel, side, width, final),
        out_shape=(shaped(ROWS, (1 if final else 2) * width + 128), shaped(ROWS, 2 * width + 128)),
        in_specs=[VM, VM] + [VM] * len(carried),
        out_specs=(VM, VM),
        compiler_params=SMALL,
        cost_estimate=pl.CostEstimate(flops=200_000, bytes_accessed=200_000, transcendentals=0),
        name="merge_groups",
    )(mine, other, *carried)


PARTNERS = {"gx": {1: 1, 2: 2, 4: 6}, "gy": {1: 1, 2: 3, 4: 4, 8: 12}}


def exchange(message, axis, width, fillers):
    count = lax.axis_size(axis)
    state = None
    reach = 1
    results = []
    while True:
        mask = PARTNERS[axis].get(reach, reach)
        other = lax.ppermute(message, axis, [(i, i ^ mask) for i in range(count)])
        filler = fillers.get(reach)
        if filler is not None:
            function, first, *rest = filler
            first, message = lax.optimization_barrier((first, message))
            result = function(first, *rest)
            result, message = lax.optimization_barrier((result, message))
            results.append(result)
        if 2 * reach >= count:
            return ((axis, reach), message, other, state), results
        message, state = merge_step((axis, reach), message, other, state, width, 4 * reach >= count)
        reach *= 2


def middle_kernel(side, mine, other, state, y_rhs, x_ends, y_ends, coefs, enter, message):
    fresh = last_merge(side, mine, other, state, CY)
    beta = coefs[0, :, BETA : BETA + 1]
    values = [beta * fresh[e] for e in range(2)]
    for e in range(2):
        enter[e] = values[e]
        total = y_rhs[e]
        for g in range(2):
            total = total + jnp.sum(values[g] * y_ends[e], axis=1, keepdims=True) * x_ends[g]
        message[:, e * CX : (e + 1) * CX] = total
    message[:, 2 * CX :] = coefs[1]


def middle(last, y_rhs, x_ends, y_ends, coefs):
    return pl.pallas_call(
        functools.partial(middle_kernel, last[0]),
        out_shape=(shaped(2, ROWS, CY), shaped(ROWS, 2 * CX + 128)),
        in_specs=[VM] * 7,
        out_specs=(VM, VM),
        compiler_params=SMALL,
        cost_estimate=pl.CostEstimate(flops=500_000, bytes_accessed=500_000, transcendentals=0),
        name="between_interfaces",
    )(*last[1:], y_rhs, x_ends, y_ends, coefs)


def rows_kernel(enter, ginv_y, edge_y, out, spread):
    high, low = halves(enter[...].reshape(2 * ROWS, CY))
    spot = lax.broadcasted_iota(jnp.int32, (16, 1), 0)
    for f in range(NF):
        g_high, g_low = halves(ginv_y[f])
        spread[...] = dot_nt(high, g_high) + dot_nt(low, g_high) + dot_nt(high, g_low)
        for z in range(NZ):
            k = f * NZ + z
            value = jnp.where(spot == z, edge_y[f, 0:1, :], 0.0) + jnp.where(spot == NZ + z, edge_y[f, 1:2, :], 0.0)
            value = value + jnp.where(spot == 8, spread[k : k + 1, :], 0.0)
            value = value + jnp.where(spot == 9, spread[ROWS + k : ROWS + k + 1, :], 0.0)
            v_high, v_low = halves(value)
            out[k, 0:16, :] = v_high
            out[k, 16:32, :] = v_high
            out[k, 32:48, :] = v_low
            out[k, 48:, :] = jnp.zeros((80, CY), BF16)


def row_products(enter, ginv_y, edge_y):
    return pl.pallas_call(
        rows_kernel,
        out_shape=packed(ROWS, 128, CY),
        in_specs=[VM, VM, VM],
        out_specs=VM,
        scratch_shapes=[pltpu.VMEM((2 * ROWS, CY), F32)],
        compiler_params=SMALL,
        cost_estimate=pl.CostEstimate(flops=300_000_000, bytes_accessed=2 * MIB, transcendentals=0),
        name="row_products",
    )(enter, ginv_y, edge_y)


def update_kernel(side, items, mine, other, state, *refs):
    bases, (wide, edge_x, coefs, out, tall, slim, done, sems) = refs[: len(items)], refs[len(items) :]
    where = {k: (base, place) for base, group in zip(bases, items) for place, k in enumerate(group)}
    fresh = last_merge(side, mine, other, state, CX)
    beta = coefs[1, :, BETA : BETA + 1]
    leave = [beta * fresh[e] for e in range(2)]
    for f in range(NF):
        s = slice(f * NZ, (f + 1) * NZ)
        value = jnp.concatenate([leave[e][s, :] for e in range(2)], axis=0)
        value = jnp.concatenate([value, edge_x[f, 0:8, :]], axis=0)
        high = value.astype(BF16).astype(F32)
        tall[0:16, :] = high
        tall[16:32, :] = (value - high).astype(BF16).astype(F32)
        tall[32:48, :] = high
        tall[48:, :] = jnp.zeros((80, CX), F32)
        for t in range(CX // 128):
            slim[f, t * 128 : (t + 1) * 128, :] = jnp.transpose(tall[:, t * 128 : (t + 1) * 128]).astype(BF16)
        for z in range(NZ):
            k = f * NZ + z
            base, place = where[k]
            for r in range(STRIPS):
                at = slice(r * CHUNK, (r + 1) * CHUNK)
                done[f, z, at, :] = base[place, at, :] + dot(slim[f, at, :], wide[k])
            pltpu.make_async_copy(done.at[f, z], out.at[f, z], sems.at[k]).start()
    for k in range(ROWS):
        pltpu.make_async_copy(done.at[k // NZ, k % NZ], out.at[k // NZ, k % NZ], sems.at[k]).wait()


def update(last, items, bases, wide, edge_x, coefs):
    return pl.pallas_call(
        functools.partial(update_kernel, last[0], items),
        out_shape=shaped(NF, NZ, CX, CY),
        in_specs=[VM] * (6 + len(bases)),
        out_specs=HB,
        scratch_shapes=[
            pltpu.VMEM((128, CX), F32),
            pltpu.VMEM((NF, CX, 128), BF16),
            pltpu.VMEM((NF, NZ, CX, CY), F32),
            pltpu.SemaphoreType.DMA((ROWS,)),
        ],
        compiler_params=pltpu.CompilerParams(vmem_limit_bytes=12 * MIB),
        cost_estimate=pl.CostEstimate(flops=200_000_000, bytes_accessed=17 * MIB, transcendentals=0),
        name="update_result",
    )(*last[1:], *bases, wide, edge_x, coefs)


def swap_pairs(value, axis, inner):
    count = lax.axis_size(axis)
    pairs = []
    for i in range(0 if inner else 1, count - 1, 2):
        pairs += [(i, i + 1), (i + 1, i)]
    return lax.ppermute(value, axis, pairs)


def local(fields, ginv_x, ginv_y, coupling_x, coupling_y):
    fields, q_cat, x_inner, x_outer, y_inner, y_outer = pack(fields)
    received = (
        swap_pairs(x_inner, "gx", True),
        swap_pairs(x_outer, "gx", False),
        swap_pairs(y_inner, "gy", True),
        swap_pairs(y_outer, "gy", False),
    )
    gx_cat, gy_cat, gx_rows, gy_rows, edge_x, edge_y, x_ends, y_ends, coefs = prep(
        ginv_x, ginv_y, coupling_x, coupling_y
    )
    forcing, message = force_all(fields, q_cat, received, gx_rows, coefs)

    def product(items):
        return lambda first, gx, gy: products(items, first, gx, gy), forcing, gx_cat, gy_cat

    sums = []

    def sum_up(rows):
        sums.append(weight(forcing, rows))
        return sums[0]

    items = [tuple(range(*ends)) for ends in ((0, 2), (2, 3), (3, 7), (7, 10), (10, 13), (13, 16))]

    def multiply(first):
        cells, matrices = first
        return products(items[1], cells, matrices, gy_cat), weigh(sums[0], matrices)

    fillers = {1: product(items[0]), 2: (sum_up, gy_rows), 4: (multiply, (forcing, gx_cat))}
    last_x, (base_0, _, (base_1, y_rhs)) = exchange(message, "gx", CY, fillers)
    enter, message_y = middle(last_x, y_rhs, x_ends, y_ends, coefs)

    def last_work(first):
        cells, matrices = first
        return products(items[5], cells, gx_cat, gy_cat), row_products(enter, matrices, edge_y)

    fillers = {1: product(items[2]), 2: product(items[3]), 4: product(items[4]), 8: (last_work, (forcing, ginv_y))}
    last_y, (base_2, base_3, base_4, (base_5, wide)) = exchange(message_y, "gy", CX, fillers)
    return update(last_y, items, (base_0, base_1, base_2, base_3, base_4, base_5), wide, edge_x, coefs)


def solution(mesh):
    in_specs = (P(None, None, "gx", "gy"), P(None, "gx", None), P(None, "gy", None), P(), P())
    out_specs = P(None, None, "gx", "gy")
    return jax.shard_map(local, mesh=mesh, in_specs=in_specs, out_specs=out_specs, check_vma=False)
```

```python
import functools

import jax
import jax.numpy as jnp
from jax import lax
from jax.experimental import pallas as pl
from jax.experimental.pallas import tpu as pltpu
from jax.sharding import PartitionSpec as P

F32 = jnp.float32
BF16 = jnp.bfloat16
BAND = (45.0, -9.0, 1.0)
ADVECT = 0.3
BUOY = 0.5
CX = 512
CY = 256
NF = 4
NZ = 4
ROWS = NF * NZ
MIB = 1024 * 1024

VM = pl.BlockSpec(memory_space=pltpu.VMEM)
SM = pl.BlockSpec(memory_space=pltpu.SMEM)
HB = pl.BlockSpec(memory_space=pltpu.HBM)
SMALL = pltpu.CompilerParams(vmem_limit_bytes=4 * MIB)


def shaped(*dims):
    return jax.ShapeDtypeStruct(dims, F32)


def packed(*dims):
    return jax.ShapeDtypeStruct(dims, BF16)


def halves(value):
    high = value.astype(BF16)
    return high, (value - high.astype(F32)).astype(BF16)


def dot(left, right):
    return lax.dot_general(left, right, (((1,), (0,)), ((), ())), preferred_element_type=F32)


def dot_nt(left, right):
    return lax.dot_general(left, right, (((1,), (1,)), ((), ())), preferred_element_type=F32)


def dot_tn(left, right):
    return lax.dot_general(left, right, (((0,), (0,)), ((), ())), preferred_element_type=F32)


def odd_blocks():
    return [lax.rem(lax.axis_index(axis), 2) == 1 for axis in ("gx", "gy")]


def pack_kernel(fields, planes, q_cat, x_inner, x_outer, y_inner, y_outer, lanes, turned, sems):
    groups = [(f, z) for f in range(NF) for z in range(NZ)]
    copies = [
        pltpu.make_async_copy(fields.at[f, z], planes.at[f, z], sems.at[g])
        for g, (f, z) in enumerate(groups)
    ]
    for copy in copies:
        copy.start()
    x_odd, y_odd = odd_blocks()
    step = 64
    for g, (f, start) in enumerate(groups):
        copies[g].wait()

        def chunk(r, carry, f=f, start=start, g=g):
            at = pl.ds(pl.multiple_of(r * step, step), step)
            spot = lax.broadcasted_iota(jnp.int32, (step, 128), 1)
            total = jnp.zeros((step, 128), F32) if g == 0 else lanes[at, :]
            for z in (start,):
                k = f * NZ + z
                value = planes[f, z, at, :]
                ends = jnp.where(spot >= 125, value[:, 128:256], 0.0)
                ends = jnp.where(spot < 3, value[:, 0:128], ends)
                total = total + pltpu.roll(ends, 8 * k + 3, 1)
                high, low = halves(value)
                q_cat[k, at, 0:CY] = high
                q_cat[k, at, CY:] = low
            lanes[at, :] = total
            return carry

        lax.fori_loop(0, CX // step, chunk, 0, unroll=True)
        for z in (start,):
            k = f * NZ + z
            for c in range(3):
                top = planes[f, z, c : c + 1, :]
                bottom = planes[f, z, CX - 3 + c : CX - 2 + c, :]
                x_inner[c, k : k + 1, :] = jnp.where(x_odd, top, bottom)
                x_outer[c, k : k + 1, :] = jnp.where(x_odd, bottom, top)
    for t in range(CX // 128):
        part = slice(t * 128, (t + 1) * 128)
        turned[t, 0:128, :] = jnp.transpose(lanes[part, :])
        for c in range(3):
            right = turned[t, pl.ds(c, ROWS, stride=8), :]
            left = turned[t, pl.ds(3 + c, ROWS, stride=8), :]
            y_inner[c, :, part] = jnp.where(y_odd, left, right)
            y_outer[c, :, part] = jnp.where(y_odd, right, left)


def pack(fields):
    return pl.pallas_call(
        pack_kernel,
        out_shape=(
            shaped(NF, NZ, CX, CY),
            packed(ROWS, CX, 2 * CY),
            shaped(3, ROWS, CY),
            shaped(3, ROWS, CY),
            shaped(3, ROWS, CX),
            shaped(3, ROWS, CX),
        ),
        in_specs=[HB],
        out_specs=(VM,) * 6,
        scratch_shapes=[
            pltpu.VMEM((CX, 128), F32),
            pltpu.VMEM((CX // 128, 136, 128), F32),
            pltpu.SemaphoreType.DMA((ROWS,)),
        ],
        compiler_params=pltpu.CompilerParams(vmem_limit_bytes=35 * MIB),
        cost_estimate=pl.CostEstimate(flops=10_000_000, bytes_accessed=9 * MIB, transcendentals=0),
        name="pack_edges",
    )(fields)


WINDOW = 256
CHUNK = 128
STRIPS = CX // CHUNK
BANDS = ((0, 176, 0), (176, 160, 128), (336, 176, 256))


def band(shape, offset, along):
    gap = lax.broadcasted_iota(jnp.int32, shape, along) - lax.broadcasted_iota(jnp.int32, shape, 1 - along)
    gap = gap - offset
    total = jnp.zeros(shape, F32)
    for reach, weight in zip((1, 2, 3), BAND):
        total = jnp.where(gap == reach, weight, total)
        total = jnp.where(gap == -reach, -weight, total)
    return total.astype(BF16)


def halo_sums(before, after):
    sums = []
    for j in range(3):
        sums.append(sum(-BAND[o - 1] * before[3 + j - o] for o in range(j + 1, 4)))
    for j in range(3):
        sums.append(sum(BAND[o - 1] * after[j + o - 3] for o in range(3 - j, 4)))
    return sums


BETA = 4


def fill_coefs(beta, first_first, first_last, last_first, last_last):
    spot = lax.broadcasted_iota(jnp.int32, (NZ, 128), 1)
    values = jnp.where(
        spot == 0,
        first_first,
        jnp.where(
            spot == 1,
            first_last,
            jnp.where(spot == 2, last_first, jnp.where(spot == 3, last_last, jnp.where(spot == 4, 1.0, 0.0))),
        ),
    )
    return beta * values


def prep_kernel(gx, gy, beta_x, beta_y, gx_cat, gy_cat, gx_rows, gy_rows, edge_x, edge_y, x_ends, y_ends, coefs):
    gx_rows[...] = jnp.zeros_like(gx_rows)
    edge_x[...] = jnp.zeros_like(edge_x)
    gy_rows[...] = jnp.zeros_like(gy_rows)
    tile = 16
    spot = lax.broadcasted_iota(jnp.int32, (tile, 1), 0)

    def ends(first, last):
        f_high, f_low = halves(first)
        l_high, l_low = halves(last)
        parts = [value.astype(F32) for value in (f_high, l_high, f_low, l_low)]
        total = jnp.zeros((tile, first.shape[1]), F32)
        for place, value in enumerate(parts):
            total = jnp.where(spot == place, value, total)
        return total.astype(BF16)

    for f in range(NF):
        turned_g = jnp.transpose(gy[f])
        high, low = halves(turned_g)
        gy_cat[f, 0:CY, :] = high
        gy_cat[f, CY : 2 * CY, :] = high
        gy_cat[f, 2 * CY :, :] = low
        edge_y[f, 0:1, :] = turned_g[0:1]
        edge_y[f, 1:2, :] = turned_g[CY - 1 : CY]
        edge_y[f, 2:3, :] = gy[f, 0:1, :]
        edge_y[f, 3:4, :] = gy[f, CY - 1 : CY, :]
        gy_rows[f] = ends(gy[f, 0:1, :], gy[f, CY - 1 : CY, :])
        gx_rows[f] = ends(gx[f, 0:1, :], gx[f, CX - 1 : CX, :])

        def split(r, carry, f=f):
            at = pl.ds(pl.multiple_of(r * CHUNK, CHUNK), CHUNK)
            high, low = halves(gx[f, at, :])
            gx_cat[f, at, 0:CX] = high
            gx_cat[f, at, CX:] = low
            return carry

        lax.fori_loop(0, CX // CHUNK, split, 0)
        edge_x[f, 0:1, :] = jnp.transpose(gx[f, :, 0:128])[0:1]
        edge_x[f, 1:2, :] = jnp.transpose(gx[f, :, CX - 128 : CX])[127:128]
        s = slice(f * NZ, (f + 1) * NZ)
        for e in range(2):
            x_ends[e, s, :] = jnp.broadcast_to(edge_x[f, e : e + 1, :], (NZ, CX))
            y_ends[e, s, :] = jnp.broadcast_to(edge_y[f, 2 + e : 3 + e, :], (NZ, CY))
        for axis, (g, beta, n) in enumerate(((gx, beta_x, CX), (gy, beta_y, CY))):
            coefs[axis, s, :] = fill_coefs(
                beta[f], g[f, 0:1, 0:1], g[f, 0:1, n - 1 : n], g[f, n - 1 : n, 0:1], g[f, n - 1 : n, n - 1 : n]
            )


def prep(ginv_x, ginv_y, beta_x, beta_y):
    return pl.pallas_call(
        prep_kernel,
        out_shape=(
            packed(NF, CX, 2 * CX),
            packed(NF, 3 * CY, CY),
            packed(NF, 16, CX),
            packed(NF, 16, CY),
            shaped(NF, 8, CX),
            shaped(NF, 8, CY),
            shaped(2, ROWS, CX),
            shaped(2, ROWS, CY),
            shaped(2, ROWS, 128),
        ),
        in_specs=[VM, VM, SM, SM],
        out_specs=(VM,) * 9,
        compiler_params=SMALL,
        cost_estimate=pl.CostEstimate(flops=20_000_000, bytes_accessed=5 * MIB, transcendentals=0),
        name="split_matrices",
    )(ginv_x, ginv_y, beta_x, beta_y)


def forcing_kernel(
    fields, q_cat, x_inner, x_outer, y_inner, y_outer, gx_rows, coefs,
    forcing, message,
    band_y, band_x, halo_rows, halo_cols, turned, ends,
):
    both = band((CY, CY), 0, 0)
    band_y[0:CY, :] = both
    band_y[CY:, :] = both
    for start, count, base in BANDS:
        band_x[start : start + count, :] = band((count, WINDOW), start - base, 1)
    halo_rows[...] = jnp.zeros_like(halo_rows)
    turned[...] = jnp.zeros_like(turned)
    x_odd, y_odd = odd_blocks()
    above = [jnp.where(x_odd, x_inner[c], x_outer[c]) for c in range(3)]
    below = [jnp.where(x_odd, x_outer[c], x_inner[c]) for c in range(3)]
    for j, value in enumerate(halo_sums(above, below)):
        for k in range(ROWS):
            if j < 3:
                halo_rows[k, j : j + 1, :] = value[k : k + 1, :]
            else:
                halo_rows[k, j + 10 : j + 11, :] = value[k : k + 1, :]
    before = [jnp.where(y_odd, y_inner[c], y_outer[c]) for c in range(3)]
    behind = [jnp.where(y_odd, y_outer[c], y_inner[c]) for c in range(3)]
    for j, value in enumerate(halo_sums(before, behind)):
        for t in range(STRIPS):
            turned[t, pl.ds(j if j < 3 else j + 2, ROWS, stride=8), :] = value[:, t * 128 : (t + 1) * 128]
    for t in range(STRIPS):
        halo_cols[t * 128 : (t + 1) * 128, :] = jnp.transpose(turned[t, 0:128, :])
    message[:, 2 * CY :] = coefs[0]

    def force(z, f, r):
        start, count, base = BANDS[r]
        at = slice(start, start + count)
        k = f * NZ + z
        window = slice(base, base + WINDOW)
        dx = dot(band_x[at, :], q_cat[k, window, 0:CY]) + dot(band_x[at, :], q_cat[k, window, CY:])
        dy = dot(q_cat[k, at, :], band_y[...])
        if r == 0:
            dx = jnp.concatenate([dx[0:8] + halo_rows[k, 0:8], dx[8:]], axis=0)
        if r == len(BANDS) - 1:
            dx = jnp.concatenate([dx[: count - 8], dx[count - 8 :] + halo_rows[k, 8:16]], axis=0)
        spot = lax.broadcasted_iota(jnp.int32, (count, 128), 1)
        side = halo_cols[at, :]
        left = jnp.where(spot < 3, pltpu.roll(side, lax.rem(128 - 8 * k, 128), 1), 0.0)
        right = jnp.where(spot >= 125, pltpu.roll(side, lax.rem(248 - 8 * k, 128), 1), 0.0)
        dy = dy + jnp.concatenate([left, right], axis=1)
        rise = fields[f, lax.rem(z + 1, NZ), at, :] - fields[f, lax.rem(z + NZ - 1, NZ), at, :]
        value = fields[f, z, at, :] - (
            (ADVECT / 60.0) * (fields[1, z, at, :] * dx + fields[2, z, at, :] * dy)
            + (0.5 * ADVECT) * (fields[3, z, at, :] * rise)
        )
        if f == 3:
            value = value + BUOY * fields[0, z, at, :]
        high, low = halves(value)
        forcing[k, at, :] = high
        forcing[k, CX + start : CX + start + count, :] = low

    def contract(z, f):
        k = f * NZ + z
        by_high = dot(gx_rows[f], forcing[k, 0:CX, :])
        by_low = dot(gx_rows[f], forcing[k, CX:, :])
        ends[pl.ds(k, 1), 0:CY] = by_high[0:1] + by_high[2:3] + by_low[0:1]
        ends[pl.ds(k, 1), CY:] = by_high[1:2] + by_high[3:4] + by_low[1:2]

    def step(z, carry):
        for f in range(NF):
            for r in range(len(BANDS)):
                force(z, f, r)
            if f > 0:
                contract(z, f - 1)
        contract(z, NF - 1)
        return carry

    lax.fori_loop(0, NZ, step, 0)
    message[:, 0 : 2 * CY] = ends[0:ROWS, :]


def force_all(fields, q_cat, received, gx_rows, coefs):
    return pl.pallas_call(
        forcing_kernel,
        out_shape=(packed(ROWS, 2 * CX, CY), shaped(ROWS, 2 * CY + 128)),
        in_specs=[VM] * 8,
        out_specs=(VM,) * 2,
        scratch_shapes=[
            pltpu.VMEM((2 * CY, CY), BF16),
            pltpu.VMEM((CX, WINDOW), BF16),
            pltpu.VMEM((ROWS, 16, CY), F32),
            pltpu.VMEM((CX, 128), F32),
            pltpu.VMEM((CX // 128, 136, 128), F32),
            pltpu.VMEM((2 * ROWS, 2 * CY), F32),
        ],
        compiler_params=pltpu.CompilerParams(vmem_limit_bytes=8 * MIB),
        cost_estimate=pl.CostEstimate(flops=4_000_000_000, bytes_accessed=16 * MIB, transcendentals=0),
        name="forcing",
    )(fields, q_cat, *received, gx_rows, coefs)


def products_kernel(items, forcing, gx_cat, gy_cat, out, s_0, s_1):
    def solve_x(k, r, s_cat):
        at = slice(r * CHUNK, (r + 1) * CHUNK)
        f = k // NZ
        high, low = forcing.at[k, 0:CX, :], forcing.at[k, CX : 2 * CX, :]
        section = dot(gx_cat[f, at, 0:CX], high[...]) + dot(gx_cat[f, at, 0:CX], low[...])
        section = section + dot(gx_cat[f, at, CX:], high[...])
        s_high, s_low = halves(section)
        s_cat[at, 0:CY] = s_high
        s_cat[at, CY:] = s_low

    def solve_y(k, place, r, s_cat):
        at = slice(r * CHUNK, (r + 1) * CHUNK)
        f = k // NZ
        out[place, at, :] = dot(s_cat[at, :], gy_cat[f, 0 : 2 * CY, :]) + dot(s_cat[at, 0:CY], gy_cat[f, 2 * CY :, :])

    bufs = (s_0, s_1)
    for n in range(len(items) + 1):
        for r in range(STRIPS):
            if n < len(items):
                solve_x(items[n], r, bufs[n % 2])
            if n > 0:
                solve_y(items[n - 1], n - 1, r, bufs[(n - 1) % 2])


def products(items, forcing, gx_cat, gy_cat):
    return pl.pallas_call(
        functools.partial(products_kernel, items),
        out_shape=shaped(len(items), CX, CY),
        in_specs=[VM] * 3,
        out_specs=VM,
        scratch_shapes=[pltpu.VMEM((CX, 2 * CY), BF16), pltpu.VMEM((CX, 2 * CY), BF16)],
        compiler_params=pltpu.CompilerParams(vmem_limit_bytes=6 * MIB),
        cost_estimate=pl.CostEstimate(
            flops=600_000_000 * len(items), bytes_accessed=1_500_000 * len(items), transcendentals=0
        ),
        name="block_products",
    )(forcing, gx_cat, gy_cat)


def weight_kernel(forcing, gy_rows, weighted):
    for k in range(ROWS):
        both = dot_nt(gy_rows[k // NZ], forcing[k])
        high, low = both[:, 0:CX], both[:, CX:]
        weighted[0, k : k + 1, :] = high[0:1] + high[2:3] + low[0:1]
        weighted[1, k : k + 1, :] = high[1:2] + high[3:4] + low[1:2]


def weight(forcing, gy_rows):
    return pl.pallas_call(
        weight_kernel,
        out_shape=shaped(2, ROWS, CX),
        in_specs=[VM, VM],
        out_specs=VM,
        compiler_params=SMALL,
        cost_estimate=pl.CostEstimate(flops=500_000_000, bytes_accessed=8 * MIB, transcendentals=0),
        name="weighted_sums",
    )(forcing, gy_rows)


def weigh_kernel(weighted, gx_cat, out):
    high, low = halves(weighted[...].reshape(2 * ROWS, CX))
    owner = lax.rem(lax.broadcasted_iota(jnp.int32, (2 * ROWS, 1), 0), ROWS) // NZ
    total = jnp.zeros((2 * ROWS, CX), F32)
    for f in range(NF):
        value = dot_nt(high, gx_cat[f, :, 0:CX]) + dot_nt(low, gx_cat[f, :, 0:CX]) + dot_nt(high, gx_cat[f, :, CX:])
        total = jnp.where(owner == f, value, total)
    out[...] = total.reshape(2, ROWS, CX)


def weigh(weighted, gx_cat):
    return pl.pallas_call(
        weigh_kernel,
        out_shape=shaped(2, ROWS, CX),
        in_specs=[VM, VM],
        out_specs=VM,
        compiler_params=SMALL,
        cost_estimate=pl.CostEstimate(flops=500_000_000, bytes_accessed=5 * MIB, transcendentals=0),
        name="y_right_side",
    )(weighted, gx_cat)


def merge(side, mine, other, state, width):
    axis, reach = side
    is_right = jnp.broadcast_to(lax.rem(lax.axis_index(axis) // reach, 2), (ROWS, 1)) == 1

    def parts(ref):
        c = 2 * width
        return [
            ref[:, 0:width], ref[:, width:c],
            ref[:, c : c + 1], ref[:, c + 1 : c + 2], ref[:, c + 2 : c + 3], ref[:, c + 3 : c + 4],
        ]

    own, far = parts(mine), parts(other)
    l_first, l_last, l_p, l_s, l_q, l_t = [jnp.where(is_right, b, a) for a, b in zip(own, far)]
    r_first, r_last, r_p, r_s, r_q, r_t = [jnp.where(is_right, a, b) for a, b in zip(own, far)]
    inner = 1.0 / (1.0 - l_t * r_p)
    m_b = (l_last + l_t * r_first) * inner
    m_a = (r_first + r_p * l_last) * inner
    b_from_b, b_from_a = l_q * inner, l_t * r_s * inner
    a_from_b, a_from_a = r_p * l_q * inner, r_s * inner
    group = (
        l_first + l_s * m_a,
        r_last + r_q * m_b,
        l_p + l_s * a_from_b,
        l_s * a_from_a,
        r_q * b_from_b,
        r_t + r_q * b_from_a,
    )
    if state is None:
        prior, later, prior_b, prior_a, later_b, later_a = 0.0, 0.0, 1.0, 0.0, 0.0, 1.0
    else:
        prior, later, prior_b, prior_a, later_b, later_a = parts(state)
    fresh = []
    for base, by_b, by_a in ((prior, prior_b, prior_a), (later, later_b, later_a)):
        fresh.append(
            (
                base + jnp.where(is_right, by_b * m_b, by_a * m_a),
                jnp.where(is_right, by_b * b_from_b, by_b + by_a * a_from_b),
                jnp.where(is_right, by_a + by_b * b_from_a, by_a * a_from_a),
            )
        )
    return group, fresh


def last_merge(side, mine, other, state, width):
    axis, reach = side
    is_right = jnp.broadcast_to(lax.rem(lax.axis_index(axis) // reach, 2), (ROWS, 1)) == 1
    own, own_coef = mine[:, 0:width], mine[:, width : width + 1]
    far, far_coef = other[:, 0:width], other[:, width : width + 1]
    between = (far + far_coef * own) * (1.0 / (1.0 - own_coef * far_coef))
    c = 2 * width
    by_prior = jnp.where(is_right, state[:, c : c + 1], state[:, c + 1 : c + 2])
    by_later = jnp.where(is_right, state[:, c + 2 : c + 3], state[:, c + 3 : c + 4])
    return state[:, 0:width] + by_prior * between, state[:, width:c] + by_later * between


def lanes_of(values):
    spot = lax.broadcasted_iota(jnp.int32, (ROWS, 128), 1)
    total = jnp.zeros((ROWS, 128), F32)
    for place, value in enumerate(values):
        total = jnp.where(spot == place, value, total)
    return total


def merge_kernel(side, width, final, mine, other, *refs):
    state, (group_out, state_out) = (refs[0], refs[1:]) if len(refs) == 3 else (None, refs)
    group, fresh = merge(side, mine, other, state, width)
    if final:
        axis, reach = side
        is_right = jnp.broadcast_to(lax.rem(lax.axis_index(axis) // (2 * reach), 2), (ROWS, 1)) == 1
        group_out[:, 0:width] = jnp.where(is_right, group[0], group[1])
        group_out[:, width:] = lanes_of((jnp.where(is_right, group[2], group[5]),))
    else:
        group_out[:, 0:width] = group[0]
        group_out[:, width : 2 * width] = group[1]
        group_out[:, 2 * width :] = lanes_of(group[2:])
    state_out[:, 0:width] = fresh[0][0]
    state_out[:, width : 2 * width] = fresh[1][0]
    state_out[:, 2 * width :] = lanes_of((fresh[0][1], fresh[0][2], fresh[1][1], fresh[1][2]))


def merge_step(side, mine, other, state, width, final):
    carried = [] if state is None else [state]
    return pl.pallas_call(
        functools.partial(merge_kernel, side, width, final),
        out_shape=(shaped(ROWS, (1 if final else 2) * width + 128), shaped(ROWS, 2 * width + 128)),
        in_specs=[VM, VM] + [VM] * len(carried),
        out_specs=(VM, VM),
        compiler_params=SMALL,
        cost_estimate=pl.CostEstimate(flops=200_000, bytes_accessed=200_000, transcendentals=0),
        name="merge_groups",
    )(mine, other, *carried)


PARTNERS = {"gx": {1: 1, 2: 2, 4: 6}, "gy": {1: 1, 2: 3, 4: 4, 8: 12}}


def exchange(message, axis, width, fillers):
    count = lax.axis_size(axis)
    state = None
    reach = 1
    results = []
    while True:
        mask = PARTNERS[axis].get(reach, reach)
        other = lax.ppermute(message, axis, [(i, i ^ mask) for i in range(count)])
        filler = fillers.get(reach)
        if filler is not None:
            function, first, *rest = filler
            first, message = lax.optimization_barrier((first, message))
            result = function(first, *rest)
            result, message = lax.optimization_barrier((result, message))
            results.append(result)
        if 2 * reach >= count:
            return ((axis, reach), message, other, state), results
        message, state = merge_step((axis, reach), message, other, state, width, 4 * reach >= count)
        reach *= 2


def middle_kernel(side, mine, other, state, y_rhs, x_ends, y_ends, coefs, enter, message):
    fresh = last_merge(side, mine, other, state, CY)
    beta = coefs[0, :, BETA : BETA + 1]
    values = [beta * fresh[e] for e in range(2)]
    for e in range(2):
        enter[e] = values[e]
        total = y_rhs[e]
        for g in range(2):
            total = total + jnp.sum(values[g] * y_ends[e], axis=1, keepdims=True) * x_ends[g]
        message[:, e * CX : (e + 1) * CX] = total
    message[:, 2 * CX :] = coefs[1]


def middle(last, y_rhs, x_ends, y_ends, coefs):
    return pl.pallas_call(
        functools.partial(middle_kernel, last[0]),
        out_shape=(shaped(2, ROWS, CY), shaped(ROWS, 2 * CX + 128)),
        in_specs=[VM] * 7,
        out_specs=(VM, VM),
        compiler_params=SMALL,
        cost_estimate=pl.CostEstimate(flops=500_000, bytes_accessed=500_000, transcendentals=0),
        name="between_interfaces",
    )(*last[1:], y_rhs, x_ends, y_ends, coefs)


def rows_kernel(enter, ginv_y, edge_y, out, spread):
    high, low = halves(enter[...].reshape(2 * ROWS, CY))
    spot = lax.broadcasted_iota(jnp.int32, (16, 1), 0)
    for f in range(NF):
        g_high, g_low = halves(ginv_y[f])
        spread[...] = dot_nt(high, g_high) + dot_nt(low, g_high) + dot_nt(high, g_low)
        for z in range(NZ):
            k = f * NZ + z
            value = jnp.where(spot == z, edge_y[f, 0:1, :], 0.0) + jnp.where(spot == NZ + z, edge_y[f, 1:2, :], 0.0)
            value = value + jnp.where(spot == 8, spread[k : k + 1, :], 0.0)
            value = value + jnp.where(spot == 9, spread[ROWS + k : ROWS + k + 1, :], 0.0)
            v_high, v_low = halves(value)
            out[k, 0:16, :] = v_high
            out[k, 16:32, :] = v_high
            out[k, 32:48, :] = v_low
            out[k, 48:, :] = jnp.zeros((80, CY), BF16)


def row_products(enter, ginv_y, edge_y):
    return pl.pallas_call(
        rows_kernel,
        out_shape=packed(ROWS, 128, CY),
        in_specs=[VM, VM, VM],
        out_specs=VM,
        scratch_shapes=[pltpu.VMEM((2 * ROWS, CY), F32)],
        compiler_params=SMALL,
        cost_estimate=pl.CostEstimate(flops=300_000_000, bytes_accessed=2 * MIB, transcendentals=0),
        name="row_products",
    )(enter, ginv_y, edge_y)


def update_kernel(side, items, mine, other, state, *refs):
    bases, (wide, edge_x, coefs, out, tall, slim, done, sems) = refs[: len(items)], refs[len(items) :]
    where = {k: (base, place) for base, group in zip(bases, items) for place, k in enumerate(group)}
    fresh = last_merge(side, mine, other, state, CX)
    beta = coefs[1, :, BETA : BETA + 1]
    leave = [beta * fresh[e] for e in range(2)]
    for f in range(NF):
        s = slice(f * NZ, (f + 1) * NZ)
        value = jnp.concatenate([leave[e][s, :] for e in range(2)], axis=0)
        value = jnp.concatenate([value, edge_x[f, 0:8, :]], axis=0)
        high = value.astype(BF16).astype(F32)
        tall[0:16, :] = high
        tall[16:32, :] = (value - high).astype(BF16).astype(F32)
        tall[32:48, :] = high
        tall[48:, :] = jnp.zeros((80, CX), F32)
        for t in range(CX // 128):
            slim[f, t * 128 : (t + 1) * 128, :] = jnp.transpose(tall[:, t * 128 : (t + 1) * 128]).astype(BF16)
        for z in range(NZ):
            k = f * NZ + z
            base, place = where[k]
            for r in range(STRIPS):
                at = slice(r * CHUNK, (r + 1) * CHUNK)
                done[f, z, at, :] = base[place, at, :] + dot(slim[f, at, :], wide[k])
            pltpu.make_async_copy(done.at[f, z], out.at[f, z], sems.at[k]).start()
    for k in range(ROWS):
        pltpu.make_async_copy(done.at[k // NZ, k % NZ], out.at[k // NZ, k % NZ], sems.at[k]).wait()


def update(last, items, bases, wide, edge_x, coefs):
    return pl.pallas_call(
        functools.partial(update_kernel, last[0], items),
        out_shape=shaped(NF, NZ, CX, CY),
        in_specs=[VM] * (6 + len(bases)),
        out_specs=HB,
        scratch_shapes=[
            pltpu.VMEM((128, CX), F32),
            pltpu.VMEM((NF, CX, 128), BF16),
            pltpu.VMEM((NF, NZ, CX, CY), F32),
            pltpu.SemaphoreType.DMA((ROWS,)),
        ],
        compiler_params=pltpu.CompilerParams(vmem_limit_bytes=12 * MIB),
        cost_estimate=pl.CostEstimate(flops=200_000_000, bytes_accessed=17 * MIB, transcendentals=0),
        name="update_result",
    )(*last[1:], *bases, wide, edge_x, coefs)


def swap_pairs(value, axis, inner):
    count = lax.axis_size(axis)
    pairs = []
    for i in range(0 if inner else 1, count - 1, 2):
        pairs += [(i, i + 1), (i + 1, i)]
    return lax.ppermute(value, axis, pairs)


def local(fields, ginv_x, ginv_y, coupling_x, coupling_y):
    fields, q_cat, x_inner, x_outer, y_inner, y_outer = pack(fields)
    received = (
        swap_pairs(x_inner, "gx", True),
        swap_pairs(x_outer, "gx", False),
        swap_pairs(y_inner, "gy", True),
        swap_pairs(y_outer, "gy", False),
    )
    gx_cat, gy_cat, gx_rows, gy_rows, edge_x, edge_y, x_ends, y_ends, coefs = prep(
        ginv_x, ginv_y, coupling_x, coupling_y
    )
    forcing, message = force_all(fields, q_cat, received, gx_rows, coefs)

    def product(items):
        return lambda first, gx, gy: products(items, first, gx, gy), forcing, gx_cat, gy_cat

    sums = []

    def sum_up(rows):
        sums.append(weight(forcing, rows))
        return sums[0]

    items = [tuple(range(*ends)) for ends in ((0, 2), (2, 3), (3, 7), (7, 10), (10, 13), (13, 16))]

    def multiply(first):
        cells, matrices = first
        return products(items[1], cells, matrices, gy_cat), weigh(sums[0], matrices)

    fillers = {1: product(items[0]), 2: (sum_up, gy_rows), 4: (multiply, (forcing, gx_cat))}
    last_x, (base_0, _, (base_1, y_rhs)) = exchange(message, "gx", CY, fillers)
    enter, message_y = middle(last_x, y_rhs, x_ends, y_ends, coefs)

    def last_work(first):
        cells, matrices = first
        return products(items[5], cells, gx_cat, gy_cat), row_products(enter, matrices, edge_y)

    fillers = {1: product(items[2]), 2: product(items[3]), 4: product(items[4]), 8: (last_work, (forcing, ginv_y))}
    last_y, (base_2, base_3, base_4, (base_5, wide)) = exchange(message_y, "gy", CX, fillers)
    return update(last_y, items, (base_0, base_1, base_2, base_3, base_4, base_5), wide, edge_x, coefs)


def solution(mesh):
    in_specs = (P(None, None, "gx", "gy"), P(None, "gx", None), P(None, "gy", None), P(), P())
    out_specs = P(None, None, "gx", "gy")
    return jax.shard_map(local, mesh=mesh, in_specs=in_specs, out_specs=out_specs, check_vma=False)
```
